32 devices in a mesh: groups: 2 (over y), tile: 16 (over z, x, core).
Axes of the slice: x: 2, y: 2, z: 4, core: 2. Of those that a mesh axis runs over, the one named last changes fastest.
Arguments:
- object_slices: float32 [4096, 2, 2, 256], P(('groups', 'tile')), parts along dimension 0, may hold values from -4 to 4
- probe_field: float32 [256, 2, 2, 128], P(('groups', 'tile')), parts along dimension 0, may hold values from -2.5 to 2.5
- patterns: float32 [512, 128, 128], P(('groups', 'tile')), parts along dimension 0, may hold values from 0 to 2
- row_offsets: int32 [512], P(('groups', 'tile')), parts along dimension 0, may hold values from 0 to 127
- col_offsets: int32 [512], P(('groups', 'tile')), parts along dimension 0, may hold values from 0 to 128
- counts: int32 [32], P(('groups', 'tile')), parts along dimension 0, may hold values from 1 to 16, as said below
Outputs:
- object_grad: float32 [4096, 2, 2, 256], P(('groups', 'tile')), parts along dimension 0
- probe_grad: float32 [256, 2, 2, 128], P(('groups', 'tile')), parts along dimension 0
The draws below stay inside these ranges and needn't reach their ends.
There are 2 independent parts, one for each index of `groups`. The reference program is written for one: setup_inputs(seed, part) draws one part's arguments, and reference() takes and returns one part's arrays. A program takes and returns all parts, laid end to end along the dimension named above; each array names one. Nothing has to cross between parts.
Inputs may be any that keep to these rules, and one draw needn't show every extreme that they name: `counts`: each tile has 1 to 16 live slots, and one tile of every draw has 16.
All inputs are finite; a program needn't handle non-finite values.
Results may differ from the reference program's by a relative error of at most 0.0003.
Values sent between devices are 32-bit elements; how exact they have to be, the bound alone decides.
No kernel may reach another device: no remote copies, remote signals or barrier semaphores. Data moves between devices by JAX's collectives and lax.ppermute only.
A program may use at most 64 MiB of HBM per device.

```python
import math
import jax
import jax.numpy as jnp
from jax import lax

W = 128
MODES = 2
SLICES = 2
GROUP_DEV = 16
TR = 128
TC = 256
MOST = 16
TILES = 16
NROWS = 2048
NPROBE = 1
POSITIONS = 256


def draw_counts(key, part):
    key = jax.random.fold_in(key, 11)
    first_key, second_key = jax.random.split(key)
    baseline = jax.random.randint(first_key, (TILES,), 1, MOST // 2 + 1)
    heaviest = jax.random.randint(second_key, (), 0, TILES)
    return jnp.where(jnp.arange(TILES) == heaviest, MOST, baseline).astype(jnp.int32)


def plant(values, rng, smallest, top_value):
    longest = values.shape.index(max(values.shape))
    spots = []
    for shift in (0, 1):
        where = [jax.random.randint(jax.random.fold_in(rng, axis), (), 0, length) for axis, length in enumerate(values.shape)]
        where[longest] = (where[longest] + shift) % values.shape[longest]
        spots.append(tuple(where))
    return values.at[spots[0]].set(smallest).at[spots[1]].set(top_value)


def block_scale(own_key, shape, pieces, least, largest):
    loudness, own = 1.0, jax.random.fold_in(own_key, 6)
    for axis_at, parts in pieces:
        draws = jnp.exp(jax.random.uniform(jax.random.fold_in(own, axis_at), (parts,), jnp.float32, least / len(pieces), largest / len(pieces)))
        loudness = loudness * jnp.repeat(draws, shape[axis_at] // parts).reshape([-1 if axis == axis_at else 1 for axis in range(len(shape))])
    return loudness


def noise(key, dims, width, limit, cuts=(), kind=jnp.bfloat16):
    array = jax.random.normal(key, dims, jnp.float32) * width
    if len(cuts) > 0:
        array = block_scale(key, dims, cuts, -0.22, 0.18) * array
    return jnp.clip(array, min=-limit, max=limit).astype(kind)


def setup_inputs(seed: int = 0, part: int = 0) -> dict:
    key_of = jax.random.split(jax.random.key(seed), 7)
    part_splits = jax.random.split(jax.random.fold_in(key_of[6], part), 7)
    return {
        "object_slices": noise(part_splits[0], (NROWS, SLICES, 2, TC), 0.7, 4.0, ((0, 16),), jnp.float32),
        "probe_field": noise(part_splits[1], (NPROBE * W, MODES, 2, W), 0.35, 2.5, ((0, 16),), jnp.float32),
        "patterns": jnp.clip(2.0 * jax.random.uniform(part_splits[2], (POSITIONS, W, W), jnp.float32) ** block_scale(part_splits[2], (POSITIONS, W, W), ((0, 16),), -0.2, 0.2), 0.0, 2.0),
        "row_offsets": plant(jax.random.randint(part_splits[3], (POSITIONS,), 0, TR), jax.random.fold_in(part_splits[3], 1), 0, TR - 1).astype(jnp.int32),
        "col_offsets": plant(jax.random.randint(part_splits[4], (POSITIONS,), 0, TC - W + 1), jax.random.fold_in(part_splits[4], 1), 0, TC - W).astype(jnp.int32),
        "counts": draw_counts(jax.random.fold_in(jax.random.fold_in(key_of[6], part), 71), part),
    }


KAPPA = 4.0


def kernel_of(extent):
    counter = jnp.arange(extent, dtype=jnp.int32)
    freq_axis = ((counter + extent // 2) % extent - extent // 2).astype(jnp.float32) / extent
    phase = (-math.pi * KAPPA) * (freq_axis[:, None] ** 2 + freq_axis[None, :] ** 2)
    return jnp.cos(phase) + 1j * jnp.sin(phase)


def forward_fft(field):
    return jnp.fft.fft2(field, axes=(0, 2), norm="ortho")


def inverse_fft(field):
    return jnp.fft.ifft2(field, axes=(0, 2), norm="ortho")


def carry_over(field, kernel):
    return inverse_fft(forward_fft(field) * kernel[:, None, :])


def position_terms(window, probe_modes, measured, kernel):
    layers = window.shape[1]
    objects = [window[:, layer_no, 0, :] + 1j * window[:, layer_no, 1, :] for layer_no in range(layers)]
    entering = [probe_modes]
    leaving = probe_modes
    for layer_no in range(layers):
        leaving = entering[layer_no] * objects[layer_no][:, None, :]
        if layer_no + 1 < layers:
            entering.append(carry_over(leaving, kernel))
    far_field = forward_fft(leaving)
    intensity = jnp.sum(jnp.real(far_field) ** 2 + jnp.imag(far_field) ** 2, axis=1)
    upstream = inverse_fft((2.0 * (intensity - measured))[:, None, :] * far_field)
    layer_grads = [None] * layers
    incoming = upstream
    for layer_no in reversed(range(layers)):
        layer_term = jnp.sum(jnp.conj(entering[layer_no]) * upstream, axis=1)
        layer_grads[layer_no] = jnp.stack([jnp.real(layer_term), jnp.imag(layer_term)], axis=1)
        incoming = jnp.conj(objects[layer_no])[:, None, :] * upstream
        if layer_no > 0:
            upstream = carry_over(incoming, jnp.conj(kernel))
    return jnp.stack(layer_grads, axis=1), incoming


def reference(object_slices, probe_field, patterns, row_offsets, col_offsets, counts):
    total_rows = object_slices.shape[0]
    extended = jnp.concatenate([object_slices, object_slices[:W]], axis=0)
    probes = probe_field.reshape(NPROBE, W, MODES, 2, W)
    probe_modes = probes[:, :, :, 0, :] + 1j * probes[:, :, :, 1, :]
    kernel = kernel_of(W)

    def visit(carry, position):
        accumulated, probe_sum = carry
        device = position // MOST
        within = position % MOST
        is_live = (within < counts[device]).astype(jnp.float32)
        row_start = (device * TR + row_offsets[position]).astype(jnp.int32)
        col_start = col_offsets[position].astype(jnp.int32)
        anchor = jnp.zeros((), jnp.int32)
        corner = (row_start, anchor, anchor, col_start)
        window = lax.dynamic_slice(extended, corner, (W, SLICES, 2, W))
        probe_group = device // GROUP_DEV
        patch_grad, probe_term = position_terms(window, probe_modes[probe_group], patterns[position], kernel)
        current = lax.dynamic_slice(accumulated, corner, (W, SLICES, 2, W))
        accumulated = lax.dynamic_update_slice(accumulated, current + is_live * patch_grad, corner)
        probe_part = jnp.stack([jnp.real(probe_term), jnp.imag(probe_term)], axis=2) * is_live
        probe_sum = probe_sum.at[probe_group].add(probe_part)
        return (accumulated, probe_sum), None

    initial = (jnp.zeros(extended.shape, jnp.float32), jnp.zeros((NPROBE, W, MODES, 2, W), jnp.float32))
    (accumulated, probe_sum), _ = lax.scan(visit, initial, jnp.arange(POSITIONS, dtype=jnp.int32))
    object_grad = accumulated[:total_rows].at[:W].add(accumulated[total_rows:])
    return object_grad, probe_sum.reshape(NPROBE * W, MODES, 2, W)
```

```python
import math

import jax
import jax.numpy as jnp
import numpy as np
from jax import lax
from jax.experimental import pallas as pl
from jax.experimental.pallas import tpu as pltpu
from jax.sharding import PartitionSpec as P

GROUP_DEV = 16
KAPPA = 4.0
MODES = 2
SLICES = 2


def block_matrices(extent):
    counter = np.arange(extent)
    dft = np.exp(-2j * np.pi * (counter[:, None] * counter[None, :] % extent) / extent) / math.sqrt(extent)
    freq = ((counter + extent // 2) % extent - extent // 2) / extent
    prop = np.conj(dft) @ (np.exp(-1j * np.pi * KAPPA * freq**2)[:, None] * dft)
    stacked = []
    for matrix in (dft, prop):
        for imag_sign in (1.0, -1.0):
            re, im = matrix.real, imag_sign * matrix.imag
            full = np.block([[re, im], [-im, re]]).astype(np.float32)
            high = full.astype(jnp.bfloat16)
            low = (full - high.astype(np.float32)).astype(jnp.bfloat16)
            stacked += [high, low]
    return np.stack(stacked)


def kernel(rows_ref, cols_ref, counts_ref, own_ref, next_ref, probe_ref, patterns_ref, mats_ref,
           own_out, next_out, probe_out, obj, acc, probe, probe_acc):
    extent = patterns_ref.shape[1]
    tile_rows = own_ref.shape[0] // 8
    halves = 2

    for layer in range(SLICES):
        for half in range(halves):
            for part in range(2):
                source = (layer * halves + half) * 2 + part
                plane = (layer * 2 + part) * halves + half
                obj[plane, :tile_rows] = own_ref[pl.ds(source, tile_rows, stride=8), :]
                obj[plane, tile_rows:] = next_ref[pl.ds(source, extent, stride=8), :]
    for k in range(2 * MODES):
        probe[k] = probe_ref[pl.ds(k, extent, stride=2 * MODES), :]
    acc[...] = jnp.zeros(acc.shape, jnp.float32)
    probe_acc[...] = jnp.zeros(probe_acc.shape, jnp.float32)

    def split(value):
        high = value.astype(jnp.bfloat16)
        low = (value - high.astype(jnp.float32)).astype(jnp.bfloat16)
        return high, low

    def right(fields, kind, conj):
        high_m, low_m = mats_ref[4 * kind + 2 * conj], mats_ref[4 * kind + 2 * conj + 1]
        rows = jnp.concatenate(
            [jnp.concatenate([f[m][0], f[m][1]], axis=1) for f in fields for m in range(MODES)], axis=0)
        high, low = split(rows)
        out = jnp.dot(jnp.concatenate([high, low, high], axis=1), jnp.concatenate([high_m, high_m, low_m], axis=0),
                      preferred_element_type=jnp.float32)
        return [[[out[(i * MODES + m) * extent:(i * MODES + m + 1) * extent, c * extent:(c + 1) * extent]
                  for c in range(2)] for m in range(MODES)] for i in range(len(fields))]

    def left(fields, kind, conj):
        high_m, low_m = mats_ref[4 * kind + 2 * (1 - conj)], mats_ref[4 * kind + 2 * (1 - conj) + 1]
        cols = jnp.concatenate(
            [jnp.concatenate([f[m][0], f[m][1]], axis=0) for f in fields for m in range(MODES)], axis=1)
        high, low = split(cols)
        out = jnp.dot(jnp.concatenate([high_m, high_m, low_m], axis=1), jnp.concatenate([high, low, high], axis=0),
                      preferred_element_type=jnp.float32)
        return [[[out[c * extent:(c + 1) * extent, (i * MODES + m) * extent:(i * MODES + m + 1) * extent]
                  for c in range(2)] for m in range(MODES)] for i in range(len(fields))]

    def both(fields, kind, conj):
        return left(right(fields, kind, conj), kind, conj)

    def times(a, b):
        return [a[0] * b[0] - a[1] * b[1], a[0] * b[1] + a[1] * b[0]]

    def conj_times(a, b):
        return [a[0] * b[0] + a[1] * b[1], a[0] * b[1] - a[1] * b[0]]

    def add(a, b):
        return [a[0] + b[0], a[1] + b[1]]

    lane = lax.broadcasted_iota(jnp.int32, (extent, extent), 1)

    def run(slots):
        corners = [(rows_ref[s], cols_ref[s]) for s in slots]
        objects = []
        for r, c in corners:
            shift = lax.rem(extent - c, extent)
            layers = []
            for layer in range(SLICES):
                parts = []
                for part in range(2):
                    plane = (layer * 2 + part) * halves
                    joined = jnp.where(lane >= c, obj[plane, pl.ds(r, extent), :], obj[plane + 1, pl.ds(r, extent), :])
                    parts.append(pltpu.roll(joined, shift, 1))
                layers.append(parts)
            objects.append(layers)
        fields = [[[probe[2 * m], probe[2 * m + 1]] for m in range(MODES)] for _ in slots]
        n = range(len(slots))
        leaving = [[times(fields[i][m], objects[i][0]) for m in range(MODES)] for i in n]
        entering = both(leaving, 1, 0)
        leaving = [[times(entering[i][m], objects[i][1]) for m in range(MODES)] for i in n]
        far = both(leaving, 0, 0)
        weighted = []
        for i in n:
            intensity = far[i][0][0] ** 2 + far[i][0][1] ** 2
            for m in range(1, MODES):
                intensity += far[i][m][0] ** 2 + far[i][m][1] ** 2
            weight = 2.0 * (intensity - patterns_ref[slots[i]])
            weighted.append([[weight * far[i][m][0], weight * far[i][m][1]] for m in range(MODES)])
        back = both(weighted, 0, 1)
        grads = [[None] * SLICES for _ in n]
        for i in n:
            g = conj_times(entering[i][0], back[i][0])
            for m in range(1, MODES):
                g = add(g, conj_times(entering[i][m], back[i][m]))
            grads[i][1] = g
        incoming = [[conj_times(objects[i][1], back[i][m]) for m in range(MODES)] for i in n]
        back = both(incoming, 1, 1)
        for i in n:
            g = conj_times(fields[i][0], back[i][0])
            for m in range(1, MODES):
                g = add(g, conj_times(fields[i][m], back[i][m]))
            grads[i][0] = g
            for m in range(MODES):
                q = conj_times(objects[i][0], back[i][m])
                probe_acc[2 * m] += q[0]
                probe_acc[2 * m + 1] += q[1]
        for i, (r, c) in enumerate(corners):
            for layer in range(SLICES):
                for part in range(2):
                    plane = (layer * 2 + part) * halves
                    rolled = pltpu.roll(grads[i][layer][part], lax.rem(c, extent), 1)
                    acc[plane, pl.ds(r, extent), :] += jnp.where(lane >= c, rolled, 0.0)
                    acc[plane + 1, pl.ds(r, extent), :] += jnp.where(lane >= c, 0.0, rolled)

    count = counts_ref[0]

    def pair(j, carry):
        run([2 * j, 2 * j + 1])
        return carry

    lax.fori_loop(0, lax.shift_right_logical(count, 1), pair, 0)

    @pl.when(lax.bitwise_and(count, 1) == 1)
    def _():
        run([count - 1])

    for layer in range(SLICES):
        for half in range(halves):
            for part in range(2):
                target = (layer * halves + half) * 2 + part
                plane = (layer * 2 + part) * halves + half
                own_out[pl.ds(target, tile_rows, stride=8), :] = acc[plane, :tile_rows]
                next_out[pl.ds(target, extent, stride=8), :] = acc[plane, tile_rows:]
    for k in range(2 * MODES):
        probe_out[pl.ds(k, extent, stride=2 * MODES), :] = probe_acc[k]


def terms(row_offsets, col_offsets, counts, own, upper, probe, patterns):
    extent = patterns.shape[1]
    rows = own.shape[0] // 8 + extent
    mats = jnp.asarray(block_matrices(extent))
    smem = pl.BlockSpec(memory_space=pltpu.SMEM)
    vmem = pl.BlockSpec(memory_space=pltpu.VMEM)
    return pl.pallas_call(
        kernel,
        out_shape=(
            jax.ShapeDtypeStruct(own.shape, jnp.float32),
            jax.ShapeDtypeStruct(upper.shape, jnp.float32),
            jax.ShapeDtypeStruct(probe.shape, jnp.float32),
        ),
        in_specs=[smem] * 3 + [vmem] * 5,
        out_specs=(vmem, vmem, vmem),
        scratch_shapes=[
            pltpu.VMEM((8, rows, extent), jnp.float32),
            pltpu.VMEM((8, rows, extent), jnp.float32),
            pltpu.VMEM((2 * MODES, extent, extent), jnp.float32),
            pltpu.VMEM((2 * MODES, extent, extent), jnp.float32),
        ],
        compiler_params=pltpu.CompilerParams(vmem_limit_bytes=40 * 1024 * 1024),
    )(row_offsets, col_offsets, counts, own, upper, probe, patterns, mats)


def flat(block):
    rows, k, parts, columns = block.shape
    split_up = block.reshape(rows, k, parts, columns // 128, 128)
    return split_up.transpose(0, 1, 3, 2, 4).reshape(-1, 128)


def unflat(value, shape):
    rows, k, parts, columns = shape
    return value.reshape(rows, k, columns // 128, parts, 128).transpose(0, 1, 3, 2, 4).reshape(shape)


def shards(object_slices, probe_field, patterns, row_offsets, col_offsets, counts):
    size = lax.axis_size("tile")
    groups = [list(range(g, g + GROUP_DEV)) for g in range(0, size, GROUP_DEV)]
    own = flat(object_slices)
    upper = lax.ppermute(own, "tile", [((i + 1) % size, i) for i in range(size)])
    probe = lax.all_gather(flat(probe_field), "tile", axis_index_groups=groups, tiled=True)
    own_grad, upper_grad, probe_grad = terms(row_offsets, col_offsets, counts, own, upper, probe, patterns)
    back = lax.ppermute(upper_grad, "tile", [(i, (i + 1) % size) for i in range(size)])
    probe_sum = lax.psum_scatter(probe_grad, "tile", axis_index_groups=groups, tiled=True)
    return unflat(own_grad + back, object_slices.shape), unflat(probe_sum, probe_field.shape)


def solution(mesh):
    in_specs = (
        P(("groups", "tile"), None, None, None),
        P(("groups", "tile"), None, None, None),
        P(("groups", "tile"), None, None),
        P(("groups", "tile")),
        P(("groups", "tile")),
        P(("groups", "tile")),
    )
    out_specs = (P(("groups", "tile"), None, None, None), P(("groups", "tile"), None, None, None))
    return jax.shard_map(shards, mesh=mesh, in_specs=in_specs, out_specs=out_specs, check_vma=False)
```

```python
import math

import jax
import jax.numpy as jnp
import numpy as np
from jax import lax
from jax.experimental import pallas as pl
from jax.experimental.pallas import tpu as pltpu
from jax.sharding import PartitionSpec as P

GROUP_DEV = 16
KAPPA = 4.0
MODES = 2
SLICES = 2
HALVES = 2


def block_matrices(extent):
    counter = np.arange(extent)
    dft = np.exp(-2j * np.pi * (counter[:, None] * counter[None, :] % extent) / extent) / math.sqrt(extent)
    freq = ((counter + extent // 2) % extent - extent // 2) / extent
    prop = np.conj(dft) @ (np.exp(-1j * np.pi * KAPPA * freq**2)[:, None] * dft)
    stacked = []
    for matrix in (dft, prop):
        for imag_sign in (1.0, -1.0):
            re, im = matrix.real, imag_sign * matrix.imag
            full = np.block([[re, im], [-im, re]]).astype(np.float32)
            high = full.astype(jnp.bfloat16)
            low = (full - high.astype(np.float32)).astype(jnp.bfloat16)
            stacked += [high, low]
    return np.stack(stacked)


def prepare(own_ref, patterns_ref, mats_ref, planes_out, patterns_out, mats_out):
    rows = planes_out.shape[1]
    for layer in range(SLICES):
        for half in range(HALVES):
            for part in range(2):
                source = (layer * HALVES + half) * 2 + part
                plane = (layer * 2 + part) * HALVES + half
                planes_out[plane] = own_ref[pl.ds(source, rows, stride=8), :]
    patterns_out[...] = patterns_ref[...]
    mats_out[...] = mats_ref[...]


def split(value):
    high = value.astype(jnp.bfloat16)
    low = (value - high.astype(jnp.float32)).astype(jnp.bfloat16)
    return high, low


def times(a, b):
    return [a[0] * b[0] - a[1] * b[1], a[0] * b[1] + a[1] * b[0]]


def conj_times(a, b):
    return [a[0] * b[0] + a[1] * b[1], a[0] * b[1] - a[1] * b[0]]


def add(a, b):
    return [a[0] + b[0], a[1] + b[1]]


def kernel(rows_ref, cols_ref, counts_ref, own_ref, next_ref, near_ref, far_ref, patterns_ref, mats_ref,
           own_out, next_out, keep_out, send_out, obj, acc, probe, probe_acc):
    extent = patterns_ref.shape[1]
    tile_rows = own_ref.shape[1]
    share = extent // GROUP_DEV
    lanes = 2 * MODES
    block = share * lanes
    member = lax.rem(lax.axis_index("tile"), GROUP_DEV)

    def member_rows(order, odd):
        bits = odd + 2 * (order // 4) + 4 * (order % 4)
        return pl.ds(pl.multiple_of(lax.bitwise_xor(member, bits) * share, share), share)

    for layer in range(SLICES):
        for half in range(HALVES):
            for part in range(2):
                source = (layer * HALVES + half) * 2 + part
                plane = (layer * 2 + part) * HALVES + half
                obj[plane, :tile_rows] = own_ref[plane]
                obj[plane, tile_rows:] = next_ref[pl.ds(source, extent, stride=8), :]
    for odd, ref in enumerate((near_ref, far_ref)):
        for order in range(GROUP_DEV // 2):
            for k in range(lanes):
                probe[k, member_rows(order, odd), :] = ref[pl.ds(order * block + k, share, stride=lanes), :]
    acc[...] = jnp.zeros(acc.shape, jnp.float32)
    probe_acc[...] = jnp.zeros(probe_acc.shape, jnp.float32)

    def right(field, kind, conj):
        high_m, low_m = mats_ref[4 * kind + 2 * conj], mats_ref[4 * kind + 2 * conj + 1]
        rows = jnp.concatenate([jnp.concatenate(field[m], axis=1) for m in range(MODES)], axis=0)
        high, low = split(rows)
        out = jnp.dot(jnp.concatenate([high, low, high], axis=1), jnp.concatenate([high_m, high_m, low_m], axis=0),
                      preferred_element_type=jnp.float32)
        return [[out[m * extent:(m + 1) * extent, c * extent:(c + 1) * extent] for c in range(2)]
                for m in range(MODES)]

    def left(field, kind, conj):
        high_m, low_m = mats_ref[4 * kind + 2 * (1 - conj)], mats_ref[4 * kind + 2 * (1 - conj) + 1]
        cols = jnp.concatenate([jnp.concatenate(field[m], axis=0) for m in range(MODES)], axis=1)
        high, low = split(cols)
        out = jnp.dot(jnp.concatenate([high_m, high_m, low_m], axis=1), jnp.concatenate([high, low, high], axis=0),
                      preferred_element_type=jnp.float32)
        return [[out[c * extent:(c + 1) * extent, m * extent:(m + 1) * extent] for c in range(2)]
                for m in range(MODES)]

    lane = lax.broadcasted_iota(jnp.int32, (extent, extent), 1)
    modes = range(MODES)

    def window(slot):
        r, c = rows_ref[slot], cols_ref[slot]
        shift = lax.rem(extent - c, extent)
        layers = []
        for layer in range(SLICES):
            parts = []
            for part in range(2):
                plane = (layer * 2 + part) * HALVES
                joined = jnp.where(lane >= c, obj[plane, pl.ds(r, extent), :], obj[plane + 1, pl.ds(r, extent), :])
                parts.append(pltpu.roll(joined, shift, 1))
            layers.append(parts)
        return layers

    def deposit(slot, layer, grad):
        r, c = rows_ref[slot], cols_ref[slot]
        for part in range(2):
            plane = (layer * 2 + part) * HALVES
            rolled = pltpu.roll(grad[part], lax.rem(c, extent), 1)
            acc[plane, pl.ds(r, extent), :] += jnp.where(lane >= c, rolled, 0.0)
            acc[plane + 1, pl.ds(r, extent), :] += jnp.where(lane >= c, 0.0, rolled)

    def steps(slot):
        field = [[probe[2 * m], probe[2 * m + 1]] for m in modes]
        objects = window(slot)
        state = right([times(field[m], objects[0]) for m in modes], 1, 0)
        yield
        entering = left(state, 1, 0)
        yield
        state = right([times(entering[m], objects[1]) for m in modes], 0, 0)
        yield
        state = left(state, 0, 0)
        yield
        intensity = sum(state[m][c] * state[m][c] for m in modes for c in range(2))
        weight = 2.0 * (intensity - patterns_ref[slot])
        state = right([[weight * state[m][c] for c in range(2)] for m in modes], 0, 1)
        yield
        state = left(state, 0, 1)
        yield
        grad = conj_times(entering[0], state[0])
        for m in modes[1:]:
            grad = add(grad, conj_times(entering[m], state[m]))
        deposit(slot, 1, grad)
        state = right([conj_times(objects[1], state[m]) for m in modes], 1, 1)
        yield
        state = left(state, 1, 1)
        yield
        grad = conj_times(field[0], state[0])
        for m in modes[1:]:
            grad = add(grad, conj_times(field[m], state[m]))
        deposit(slot, 0, grad)
        for m in modes:
            term = conj_times(objects[0], state[m])
            probe_acc[2 * m] += term[0]
            probe_acc[2 * m + 1] += term[1]

    def run(slots):
        running = [steps(slot) for slot in slots]
        while running:
            running = [r for r in running if next(r, "done") is None]

    count = counts_ref[0]

    def pair(j, carry):
        run([2 * j, 2 * j + 1])
        return carry

    lax.fori_loop(0, lax.shift_right_logical(count, 1), pair, 0)

    @pl.when(lax.bitwise_and(count, 1) == 1)
    def _():
        run([count - 1])

    for layer in range(SLICES):
        for half in range(HALVES):
            for part in range(2):
                target = (layer * HALVES + half) * 2 + part
                plane = (layer * 2 + part) * HALVES + half
                own_out[pl.ds(target, tile_rows, stride=8), :] = acc[plane, :tile_rows]
                next_out[pl.ds(target, extent, stride=8), :] = acc[plane, tile_rows:]
    for odd, ref in enumerate((keep_out, send_out)):
        for order in range(GROUP_DEV // 2):
            for k in range(lanes):
                ref[pl.ds(order * block + k, share, stride=lanes), :] = probe_acc[k, member_rows(order, odd), :]


def prepared(own, patterns):
    vmem = pl.BlockSpec(memory_space=pltpu.VMEM)
    mats = jnp.asarray(block_matrices(patterns.shape[1]))
    return pl.pallas_call(
        prepare,
        out_shape=(
            jax.ShapeDtypeStruct((8, own.shape[0] // 8, own.shape[1]), jnp.float32),
            jax.ShapeDtypeStruct(patterns.shape, jnp.float32),
            jax.ShapeDtypeStruct(mats.shape, mats.dtype),
        ),
        in_specs=[vmem] * 3,
        out_specs=(vmem,) * 3,
        compiler_params=pltpu.CompilerParams(vmem_limit_bytes=16 * 1024 * 1024),
        cost_estimate=pl.CostEstimate(flops=0, bytes_accessed=6 * 1024 * 1024, transcendentals=0),
    )(own, patterns, mats)


def terms(row_offsets, col_offsets, counts, planes, upper, near, far, patterns, mats):
    extent = patterns.shape[1]
    rows = planes.shape[1] + extent
    smem = pl.BlockSpec(memory_space=pltpu.SMEM)
    vmem = pl.BlockSpec(memory_space=pltpu.VMEM)
    return pl.pallas_call(
        kernel,
        out_shape=(
            jax.ShapeDtypeStruct((planes.shape[1] * 8, extent), jnp.float32),
            jax.ShapeDtypeStruct(upper.shape, jnp.float32),
            jax.ShapeDtypeStruct(near.shape, jnp.float32),
            jax.ShapeDtypeStruct(near.shape, jnp.float32),
        ),
        in_specs=[smem] * 3 + [vmem] * 6,
        out_specs=(vmem,) * 4,
        scratch_shapes=[
            pltpu.VMEM((8, rows, extent), jnp.float32),
            pltpu.VMEM((8, rows, extent), jnp.float32),
            pltpu.VMEM((2 * MODES, extent, extent), jnp.float32),
            pltpu.VMEM((2 * MODES, extent, extent), jnp.float32),
        ],
        compiler_params=pltpu.CompilerParams(vmem_limit_bytes=40 * 1024 * 1024),
    )(row_offsets, col_offsets, counts, planes, upper, near, far, patterns, mats)


def flat(block):
    rows, k, parts, columns = block.shape
    split_up = block.reshape(rows, k, parts, columns // 128, 128)
    return split_up.transpose(0, 1, 3, 2, 4).reshape(-1, 128)


def unflat(value, shape):
    rows, k, parts, columns = shape
    return value.reshape(rows, k, columns // 128, parts, 128).transpose(0, 1, 3, 2, 4).reshape(shape)


def partner(value, bits):
    return lax.ppermute(value, "tile", [(i, i ^ bits) for i in range(lax.axis_size("tile"))])


def gathered(own):
    quarter = jnp.concatenate([own] + [partner(own, 4 * k) for k in range(1, 4)], axis=0)
    near = jnp.concatenate([quarter, partner(quarter, 2)], axis=0)
    return near, partner(near, 1)


def scattered(keep, send):
    total = keep + partner(send, 1)
    half = total.shape[0] // 2
    total = total[:half] + partner(total[half:], 2)
    parts = jnp.split(total, 4, axis=0)
    return parts[0] + (partner(parts[1], 4) + partner(parts[2], 8) + partner(parts[3], 12))


def shards(object_slices, probe_field, patterns, row_offsets, col_offsets, counts):
    size = lax.axis_size("tile")
    own = flat(object_slices)
    upper = lax.ppermute(own, "tile", [((i + 1) % size, i) for i in range(size)])
    near, far = gathered(flat(probe_field))
    planes, patterns, mats = prepared(own, patterns)
    own_grad, upper_grad, keep, send = terms(
        row_offsets, col_offsets, counts, planes, upper, near, far, patterns, mats)
    back = lax.ppermute(upper_grad, "tile", [(i, (i + 1) % size) for i in range(size)])
    probe_sum = scattered(keep, send)
    return unflat(own_grad + back, object_slices.shape), unflat(probe_sum, probe_field.shape)


def solution(mesh):
    in_specs = (
        P(("groups", "tile"), None, None, None),
        P(("groups", "tile"), None, None, None),
        P(("groups", "tile"), None, None),
        P(("groups", "tile")),
        P(("groups", "tile")),
        P(("groups", "tile")),
    )
    out_specs = (P(("groups", "tile"), None, None, None), P(("groups", "tile"), None, None, None))
    return jax.shard_map(shards, mesh=mesh, in_specs=in_specs, out_specs=out_specs, check_vma=False)
```

```python
import math

import jax
import jax.numpy as jnp
import numpy as np
from jax import lax
from jax.experimental import pallas as pl
from jax.experimental.pallas import tpu as pltpu
from jax.sharding import PartitionSpec as P

GROUP_DEV = 16
KAPPA = 4.0
MODES = 2
SLICES = 2
HALVES = 2


def factors(extent):
    counter = np.arange(extent)
    dft = np.exp(-2j * np.pi * (counter[:, None] * counter[None, :] % extent) / extent) / math.sqrt(extent)
    freq = ((counter + extent // 2) % extent - extent // 2) / extent
    prop = np.conj(dft) @ (np.exp(-1j * np.pi * KAPPA * freq**2)[:, None] * dft)
    return np.stack([part for matrix in (dft, prop) for part in (matrix.real, matrix.imag)]).astype(np.float32)


def split(value):
    high = value.astype(jnp.bfloat16)
    low = (value - high.astype(jnp.float32)).astype(jnp.bfloat16)
    return high, low


def prepare(own_ref, patterns_ref, factors_ref, planes_out, patterns_out, mats_out, own, parts, sems):
    copies = [pltpu.make_async_copy(source, target, sems.at[i]) for i, (source, target) in enumerate(
        ((factors_ref, parts), (own_ref, own), (patterns_ref, patterns_out)))]
    for copy in copies:
        copy.start()
    copies[0].wait()
    extent = parts.shape[1]
    for kind in range(2):
        real, imag = split(parts[2 * kind]), split(parts[2 * kind + 1])
        for conj in range(2):
            for k in range(2):
                mat = 4 * kind + 2 * conj + k
                upper, lower = (-imag[k], imag[k]) if conj else (imag[k], -imag[k])
                mats_out[mat, :extent, :extent] = real[k]
                mats_out[mat, :extent, extent:] = upper
                mats_out[mat, extent:, :extent] = lower
                mats_out[mat, extent:, extent:] = real[k]
    copies[1].wait()
    rows = planes_out.shape[1]
    for layer in range(SLICES):
        for half in range(HALVES):
            for part in range(2):
                source = (layer * HALVES + half) * 2 + part
                plane = (layer * 2 + part) * HALVES + half
                planes_out[plane] = own[pl.ds(source, rows, stride=8), :]
    copies[2].wait()


def times(a, b):
    return [a[0] * b[0] - a[1] * b[1], a[0] * b[1] + a[1] * b[0]]


def conj_times(a, b):
    return [a[0] * b[0] + a[1] * b[1], a[0] * b[1] - a[1] * b[0]]


def add(a, b):
    return [a[0] + b[0], a[1] + b[1]]


def kernel(scalars_ref, own_ref, next_ref, probe_ref, patterns_ref, mats_ref,
           own_out, next_out, probe_out, obj, acc, probe, probe_acc):
    most, extent = patterns_ref.shape[:2]
    tile_rows = own_ref.shape[1]
    lanes = 2 * MODES
    modes = range(MODES)

    for layer in range(SLICES):
        for half in range(HALVES):
            for part in range(2):
                source = (layer * HALVES + half) * 2 + part
                plane = (layer * 2 + part) * HALVES + half
                obj[plane, :tile_rows] = own_ref[plane]
                obj[plane, tile_rows:] = next_ref[pl.ds(source, extent, stride=8), :]
    for k in range(lanes):
        probe[k] = probe_ref[pl.ds(k, extent, stride=lanes), :]
    acc[...] = jnp.zeros(acc.shape, jnp.float32)
    probe_acc[...] = jnp.zeros(probe_acc.shape, jnp.float32)

    def right(fields, kind, conj):
        high_m, low_m = mats_ref[4 * kind + 2 * conj], mats_ref[4 * kind + 2 * conj + 1]
        rows = jnp.concatenate([jnp.concatenate(f[m], axis=1) for f in fields for m in modes], axis=0)
        high, low = split(rows)
        out = jnp.dot(jnp.concatenate([high, low, high], axis=1), jnp.concatenate([high_m, high_m, low_m], axis=0),
                      preferred_element_type=jnp.float32)
        return [[[out[(i * MODES + m) * extent:(i * MODES + m + 1) * extent, c * extent:(c + 1) * extent]
                  for c in range(2)] for m in modes] for i in range(len(fields))]

    def left(fields, kind, conj):
        high_m, low_m = mats_ref[4 * kind + 2 * (1 - conj)], mats_ref[4 * kind + 2 * (1 - conj) + 1]
        cols = jnp.concatenate([jnp.concatenate(f[m], axis=0) for f in fields for m in modes], axis=1)
        high, low = split(cols)
        out = jnp.dot(jnp.concatenate([high_m, high_m, low_m], axis=1), jnp.concatenate([high, low, high], axis=0),
                      preferred_element_type=jnp.float32)
        return [[[out[c * extent:(c + 1) * extent, (i * MODES + m) * extent:(i * MODES + m + 1) * extent]
                  for c in range(2)] for m in modes] for i in range(len(fields))]

    lane = lax.broadcasted_iota(jnp.int32, (extent, extent), 1)

    def window(slot):
        r, c = scalars_ref[slot], scalars_ref[most + slot]
        shift = lax.rem(extent - c, extent)
        layers = []
        for layer in range(SLICES):
            parts = []
            for part in range(2):
                plane = (layer * 2 + part) * HALVES
                joined = jnp.where(lane >= c, obj[plane, pl.ds(r, extent), :], obj[plane + 1, pl.ds(r, extent), :])
                parts.append(pltpu.roll(joined, shift, 1))
            layers.append(parts)
        return layers

    def deposit(slot, layer, grad):
        r, c = scalars_ref[slot], scalars_ref[most + slot]
        for part in range(2):
            plane = (layer * 2 + part) * HALVES
            rolled = pltpu.roll(grad[part], lax.rem(c, extent), 1)
            acc[plane, pl.ds(r, extent), :] += jnp.where(lane >= c, rolled, 0.0)
            acc[plane + 1, pl.ds(r, extent), :] += jnp.where(lane >= c, 0.0, rolled)

    def steps(slots):
        n = range(len(slots))
        field = [[probe[2 * m], probe[2 * m + 1]] for m in modes]
        objects = [window(slot) for slot in slots]
        state = right([[times(field[m], objects[i][0]) for m in modes] for i in n], 1, 0)
        yield
        entering = left(state, 1, 0)
        yield
        state = right([[times(entering[i][m], objects[i][1]) for m in modes] for i in n], 0, 0)
        yield
        state = left(state, 0, 0)
        yield
        weight = [2.0 * (sum(state[i][m][c] * state[i][m][c] for m in modes for c in range(2)) - patterns_ref[slots[i]])
                  for i in n]
        state = right([[[weight[i] * state[i][m][c] for c in range(2)] for m in modes] for i in n], 0, 1)
        yield
        state = left(state, 0, 1)
        yield
        for i in n:
            grad = conj_times(entering[i][0], state[i][0])
            for m in modes[1:]:
                grad = add(grad, conj_times(entering[i][m], state[i][m]))
            deposit(slots[i], 1, grad)
        state = right([[conj_times(objects[i][1], state[i][m]) for m in modes] for i in n], 1, 1)
        yield
        state = left(state, 1, 1)
        yield
        for i in n:
            grad = conj_times(field[0], state[i][0])
            for m in modes[1:]:
                grad = add(grad, conj_times(field[m], state[i][m]))
            deposit(slots[i], 0, grad)
        for m in modes:
            term = conj_times(objects[0][0], state[0][m])
            for i in n[1:]:
                term = add(term, conj_times(objects[i][0], state[i][m]))
            probe_acc[2 * m] += term[0]
            probe_acc[2 * m + 1] += term[1]

    def run(*sets):
        running = [steps(slots) for slots in sets]
        while running:
            running = [r for r in running if next(r, "done") is None]

    count = scalars_ref[2 * most]
    fours = lax.shift_right_logical(count, 2)

    def four(j, carry):
        run([4 * j, 4 * j + 1], [4 * j + 2, 4 * j + 3])
        return carry

    lax.fori_loop(0, fours, four, 0)

    @pl.when(lax.bitwise_and(count, 2) == 2)
    def _():
        run([4 * fours], [4 * fours + 1])

    @pl.when(lax.bitwise_and(count, 1) == 1)
    def _():
        run([count - 1])

    for layer in range(SLICES):
        for half in range(HALVES):
            for part in range(2):
                target = (layer * HALVES + half) * 2 + part
                plane = (layer * 2 + part) * HALVES + half
                own_out[pl.ds(target, tile_rows, stride=8), :] = acc[plane, :tile_rows]
                next_out[pl.ds(target, extent, stride=8), :] = acc[plane, tile_rows:]
    for k in range(lanes):
        probe_out[pl.ds(k, extent, stride=lanes), :] = probe_acc[k]


def prepared(own, patterns):
    extent = patterns.shape[1]
    vmem = pl.BlockSpec(memory_space=pltpu.VMEM)
    parts = jnp.asarray(factors(extent))
    return pl.pallas_call(
        prepare,
        out_shape=(
            jax.ShapeDtypeStruct((8, own.shape[0] // 8, own.shape[1]), jnp.float32),
            jax.ShapeDtypeStruct(patterns.shape, jnp.float32),
            jax.ShapeDtypeStruct((8, 2 * extent, 2 * extent), jnp.bfloat16),
        ),
        in_specs=[pl.BlockSpec(memory_space=pltpu.HBM)] * 3,
        out_specs=(vmem,) * 3,
        scratch_shapes=[
            pltpu.VMEM(own.shape, jnp.float32),
            pltpu.VMEM(parts.shape, jnp.float32),
            pltpu.SemaphoreType.DMA((3,)),
        ],
        compiler_params=pltpu.CompilerParams(vmem_limit_bytes=16 * 1024 * 1024),
        cost_estimate=pl.CostEstimate(flops=0, bytes_accessed=6 * 1024 * 1024, transcendentals=0),
    )(own, patterns, parts)


def terms(scalars, planes, upper, probe, patterns, mats):
    extent = patterns.shape[1]
    rows = planes.shape[1] + extent
    smem = pl.BlockSpec(memory_space=pltpu.SMEM)
    vmem = pl.BlockSpec(memory_space=pltpu.VMEM)
    return pl.pallas_call(
        kernel,
        out_shape=(
            jax.ShapeDtypeStruct((planes.shape[1] * 8, extent), jnp.float32),
            jax.ShapeDtypeStruct(upper.shape, jnp.float32),
            jax.ShapeDtypeStruct(probe.shape, jnp.float32),
        ),
        in_specs=[smem] + [vmem] * 5,
        out_specs=(vmem,) * 3,
        scratch_shapes=[
            pltpu.VMEM((8, rows, extent), jnp.float32),
            pltpu.VMEM((8, rows, extent), jnp.float32),
            pltpu.VMEM((2 * MODES, extent, extent), jnp.float32),
            pltpu.VMEM((2 * MODES, extent, extent), jnp.float32),
        ],
        compiler_params=pltpu.CompilerParams(vmem_limit_bytes=40 * 1024 * 1024),
    )(scalars, planes, upper, probe, patterns, mats)


def flat(block):
    rows, k, parts, columns = block.shape
    split_up = block.reshape(rows, k, parts, columns // 128, 128)
    return split_up.transpose(0, 1, 3, 2, 4).reshape(-1, 128)


def unflat(value, shape):
    rows, k, parts, columns = shape
    return value.reshape(rows, k, columns // 128, parts, 128).transpose(0, 1, 3, 2, 4).reshape(shape)


def shards(object_slices, probe_field, patterns, row_offsets, col_offsets, counts):
    size = lax.axis_size("tile")
    groups = [list(range(g, g + GROUP_DEV)) for g in range(0, size, GROUP_DEV)]
    own = flat(object_slices)
    mine = flat(probe_field)
    copies = jnp.broadcast_to(mine[None], (GROUP_DEV,) + mine.shape)
    probe = lax.all_to_all(copies, "tile", 0, 0, axis_index_groups=groups).reshape(-1, mine.shape[1])
    upper = lax.ppermute(own, "tile", [((i + 1) % size, i) for i in range(size)])
    own, patterns, probe = lax.optimization_barrier((own, patterns, probe))
    planes, patterns, mats = prepared(own, patterns)
    scalars = jnp.concatenate([row_offsets, col_offsets, counts])
    own_grad, upper_grad, probe_grad = terms(scalars, planes, upper, probe, patterns, mats)
    back = lax.ppermute(upper_grad, "tile", [(i, (i + 1) % size) for i in range(size)])
    blocks = lax.all_to_all(probe_grad.reshape(copies.shape), "tile", 0, 0, axis_index_groups=groups)
    return unflat(own_grad + back, object_slices.shape), unflat(jnp.sum(blocks, axis=0), probe_field.shape)


def solution(mesh):
    in_specs = (
        P(("groups", "tile"), None, None, None),
        P(("groups", "tile"), None, None, None),
        P(("groups", "tile"), None, None),
        P(("groups", "tile")),
        P(("groups", "tile")),
        P(("groups", "tile")),
    )
    out_specs = (P(("groups", "tile"), None, None, None), P(("groups", "tile"), None, None, None))
    return jax.shard_map(shards, mesh=mesh, in_specs=in_specs, out_specs=out_specs, check_vma=False)
```

```python
import math

import jax
import jax.numpy as jnp
import numpy as np
from jax import lax
from jax.experimental import pallas as pl
from jax.experimental.pallas import tpu as pltpu
from jax.sharding import PartitionSpec as P

GROUP_DEV = 16
KAPPA = 4.0
MODES = 2
SLICES = 2
HALVES = 2


def factors(extent):
    counter = np.arange(extent)
    dft = np.exp(-2j * np.pi * (counter[:, None] * counter[None, :] % extent) / extent) / math.sqrt(extent)
    freq = ((counter + extent // 2) % extent - extent // 2) / extent
    prop = np.conj(dft) @ (np.exp(-1j * np.pi * KAPPA * freq**2)[:, None] * dft)
    return np.stack([part for matrix in (dft, prop) for part in (matrix.real, matrix.imag)]).astype(np.float32)


def split(value):
    high = value.astype(jnp.bfloat16)
    low = (value - high.astype(jnp.float32)).astype(jnp.bfloat16)
    return high, low


def prepare(own_ref, patterns_ref, factors_ref, planes_out, patterns_out, mats_out, own, parts, sems):
    copies = [pltpu.make_async_copy(source, target, sems.at[i]) for i, (source, target) in enumerate(
        ((factors_ref, parts), (own_ref, own), (patterns_ref, patterns_out)))]
    for copy in copies:
        copy.start()
    copies[0].wait()
    extent = parts.shape[1]
    for kind in range(2):
        real, imag = split(parts[2 * kind]), split(parts[2 * kind + 1])
        for conj in range(2):
            for k in range(2):
                mat = 4 * kind + 2 * conj + k
                upper, lower = (-imag[k], imag[k]) if conj else (imag[k], -imag[k])
                mats_out[mat, :extent, :extent] = real[k]
                mats_out[mat, :extent, extent:] = upper
                mats_out[mat, extent:, :extent] = lower
                mats_out[mat, extent:, extent:] = real[k]
    copies[1].wait()
    rows = planes_out.shape[1]
    for layer in range(SLICES):
        for half in range(HALVES):
            for part in range(2):
                source = (layer * HALVES + half) * 2 + part
                plane = (layer * 2 + part) * HALVES + half
                planes_out[plane] = own[pl.ds(source, rows, stride=8), :]
    copies[2].wait()


def times(a, b):
    return [a[0] * b[0] - a[1] * b[1], a[0] * b[1] + a[1] * b[0]]


def conj_times(a, b):
    return [a[0] * b[0] + a[1] * b[1], a[0] * b[1] - a[1] * b[0]]


def add(a, b):
    return [a[0] + b[0], a[1] + b[1]]


def kernel(scalars_ref, own_ref, low_ref, high_ref, near_ref, far_ref, patterns_ref, mats_ref,
           own_out, low_out, high_out, keep_out, send_out, obj, acc, probe, probe_acc):
    most, extent = patterns_ref.shape[:2]
    share = extent // GROUP_DEV
    middle = extent // 2
    member = lax.rem(lax.axis_index("tile"), GROUP_DEV)
    tile_rows = own_ref.shape[1]
    lanes = 2 * MODES
    block = share * lanes
    modes = range(MODES)

    def member_rows(order, odd):
        bits = odd + 2 * (order >> 2) + 4 * (order >> 1 & 1) + 8 * (order & 1)
        return pl.ds(pl.multiple_of(lax.bitwise_xor(member, bits) * share, share), share)

    for layer in range(SLICES):
        for half in range(HALVES):
            for part in range(2):
                source = (layer * HALVES + half) * 2 + part
                plane = (layer * 2 + part) * HALVES + half
                obj[plane, :tile_rows] = own_ref[plane]
                obj[plane, tile_rows:tile_rows + middle] = low_ref[pl.ds(source, middle, stride=8), :]
                obj[plane, tile_rows + middle:] = high_ref[pl.ds(source, extent - middle, stride=8), :]
    for odd, ref in enumerate((near_ref, far_ref)):
        for order in range(GROUP_DEV // 2):
            for k in range(lanes):
                probe[k, member_rows(order, odd), :] = ref[pl.ds(order * block + k, share, stride=lanes), :]
    acc[...] = jnp.zeros(acc.shape, jnp.float32)
    probe_acc[...] = jnp.zeros(probe_acc.shape, jnp.float32)

    def right(fields, kind, conj):
        high_m, low_m = mats_ref[4 * kind + 2 * conj], mats_ref[4 * kind + 2 * conj + 1]
        rows = jnp.concatenate([jnp.concatenate(f[m], axis=1) for f in fields for m in modes], axis=0)
        high, low = split(rows)
        out = jnp.dot(jnp.concatenate([high, low, high], axis=1), jnp.concatenate([high_m, high_m, low_m], axis=0),
                      preferred_element_type=jnp.float32)
        return [[[out[(i * MODES + m) * extent:(i * MODES + m + 1) * extent, c * extent:(c + 1) * extent]
                  for c in range(2)] for m in modes] for i in range(len(fields))]

    def left(fields, kind, conj):
        high_m, low_m = mats_ref[4 * kind + 2 * (1 - conj)], mats_ref[4 * kind + 2 * (1 - conj) + 1]
        cols = jnp.concatenate([jnp.concatenate(f[m], axis=0) for f in fields for m in modes], axis=1)
        high, low = split(cols)
        out = jnp.dot(jnp.concatenate([high_m, high_m, low_m], axis=1), jnp.concatenate([high, low, high], axis=0),
                      preferred_element_type=jnp.float32)
        return [[[out[c * extent:(c + 1) * extent, (i * MODES + m) * extent:(i * MODES + m + 1) * extent]
                  for c in range(2)] for m in modes] for i in range(len(fields))]

    lane = lax.broadcasted_iota(jnp.int32, (extent, extent), 1)

    def window(slot):
        r, c = scalars_ref[slot], scalars_ref[most + slot]
        shift = lax.rem(extent - c, extent)
        layers = []
        for layer in range(SLICES):
            parts = []
            for part in range(2):
                plane = (layer * 2 + part) * HALVES
                joined = jnp.where(lane >= c, obj[plane, pl.ds(r, extent), :], obj[plane + 1, pl.ds(r, extent), :])
                parts.append(pltpu.roll(joined, shift, 1))
            layers.append(parts)
        return layers

    def deposit(slot, layer, grad):
        r, c = scalars_ref[slot], scalars_ref[most + slot]
        for part in range(2):
            plane = (layer * 2 + part) * HALVES
            rolled = pltpu.roll(grad[part], lax.rem(c, extent), 1)
            acc[plane, pl.ds(r, extent), :] += jnp.where(lane >= c, rolled, 0.0)
            acc[plane + 1, pl.ds(r, extent), :] += jnp.where(lane >= c, 0.0, rolled)

    def steps(slots):
        n = range(len(slots))
        field = [[probe[2 * m], probe[2 * m + 1]] for m in modes]
        objects = [window(slot) for slot in slots]
        state = right([[times(field[m], objects[i][0]) for m in modes] for i in n], 1, 0)
        yield
        entering = left(state, 1, 0)
        yield
        state = right([[times(entering[i][m], objects[i][1]) for m in modes] for i in n], 0, 0)
        yield
        state = left(state, 0, 0)
        yield
        weight = [2.0 * (sum(state[i][m][c] * state[i][m][c] for m in modes for c in range(2)) - patterns_ref[slots[i]])
                  for i in n]
        state = right([[[weight[i] * state[i][m][c] for c in range(2)] for m in modes] for i in n], 0, 1)
        yield
        state = left(state, 0, 1)
        yield
        for i in n:
            grad = conj_times(entering[i][0], state[i][0])
            for m in modes[1:]:
                grad = add(grad, conj_times(entering[i][m], state[i][m]))
            deposit(slots[i], 1, grad)
        state = right([[conj_times(objects[i][1], state[i][m]) for m in modes] for i in n], 1, 1)
        yield
        state = left(state, 1, 1)
        yield
        for i in n:
            grad = conj_times(field[0], state[i][0])
            for m in modes[1:]:
                grad = add(grad, conj_times(field[m], state[i][m]))
            deposit(slots[i], 0, grad)
        for m in modes:
            term = conj_times(objects[0][0], state[0][m])
            for i in n[1:]:
                term = add(term, conj_times(objects[i][0], state[i][m]))
            probe_acc[2 * m] += term[0]
            probe_acc[2 * m + 1] += term[1]

    def run(*sets):
        running = [steps(slots) for slots in sets]
        while running:
            running = [r for r in running if next(r, "done") is None]

    count = scalars_ref[2 * most]
    fours = lax.shift_right_logical(count, 2)

    def four(j, carry):
        run([4 * j, 4 * j + 1], [4 * j + 2, 4 * j + 3])
        return carry

    lax.fori_loop(0, fours, four, 0)

    @pl.when(lax.bitwise_and(count, 2) == 2)
    def _():
        run([4 * fours], [4 * fours + 1])

    @pl.when(lax.bitwise_and(count, 1) == 1)
    def _():
        run([count - 1])

    for layer in range(SLICES):
        for half in range(HALVES):
            for part in range(2):
                target = (layer * HALVES + half) * 2 + part
                plane = (layer * 2 + part) * HALVES + half
                own_out[pl.ds(target, tile_rows, stride=8), :] = acc[plane, :tile_rows]
                low_out[pl.ds(target, middle, stride=8), :] = acc[plane, tile_rows:tile_rows + middle]
                high_out[pl.ds(target, extent - middle, stride=8), :] = acc[plane, tile_rows + middle:]
    for odd, ref in enumerate((keep_out, send_out)):
        for order in range(GROUP_DEV // 2):
            for k in range(lanes):
                ref[pl.ds(order * block + k, share, stride=lanes), :] = probe_acc[k, member_rows(order, odd), :]


def prepared(own, patterns):
    extent = patterns.shape[1]
    vmem = pl.BlockSpec(memory_space=pltpu.VMEM)
    parts = jnp.asarray(factors(extent))
    return pl.pallas_call(
        prepare,
        out_shape=(
            jax.ShapeDtypeStruct((8, own.shape[0] // 8, own.shape[1]), jnp.float32),
            jax.ShapeDtypeStruct(patterns.shape, jnp.float32),
            jax.ShapeDtypeStruct((8, 2 * extent, 2 * extent), jnp.bfloat16),
        ),
        in_specs=[pl.BlockSpec(memory_space=pltpu.HBM)] * 3,
        out_specs=(vmem,) * 3,
        scratch_shapes=[
            pltpu.VMEM(own.shape, jnp.float32),
            pltpu.VMEM(parts.shape, jnp.float32),
            pltpu.SemaphoreType.DMA((3,)),
        ],
        compiler_params=pltpu.CompilerParams(vmem_limit_bytes=16 * 1024 * 1024),
        cost_estimate=pl.CostEstimate(flops=0, bytes_accessed=6 * 1024 * 1024, transcendentals=0),
    )(own, patterns, parts)


def terms(scalars, planes, low, high, near, far, patterns, mats):
    extent = patterns.shape[1]
    rows = planes.shape[1] + extent
    smem = pl.BlockSpec(memory_space=pltpu.SMEM)
    vmem = pl.BlockSpec(memory_space=pltpu.VMEM)
    return pl.pallas_call(
        kernel,
        out_shape=(
            jax.ShapeDtypeStruct((planes.shape[1] * 8, extent), jnp.float32),
            jax.ShapeDtypeStruct(low.shape, jnp.float32),
            jax.ShapeDtypeStruct(high.shape, jnp.float32),
            jax.ShapeDtypeStruct(near.shape, jnp.float32),
            jax.ShapeDtypeStruct(far.shape, jnp.float32),
        ),
        in_specs=[smem] + [vmem] * 7,
        out_specs=(vmem,) * 5,
        scratch_shapes=[
            pltpu.VMEM((8, rows, extent), jnp.float32),
            pltpu.VMEM((8, rows, extent), jnp.float32),
            pltpu.VMEM((2 * MODES, extent, extent), jnp.float32),
            pltpu.VMEM((2 * MODES, extent, extent), jnp.float32),
        ],
        compiler_params=pltpu.CompilerParams(vmem_limit_bytes=40 * 1024 * 1024),
    )(scalars, planes, low, high, near, far, patterns, mats)


def flat(block):
    rows, k, parts, columns = block.shape
    split_up = block.reshape(rows, k, parts, columns // 128, 128)
    return split_up.transpose(0, 1, 3, 2, 4).reshape(-1, 128)


def unflat(value, shape):
    rows, k, parts, columns = shape
    return value.reshape(rows, k, columns // 128, parts, 128).transpose(0, 1, 3, 2, 4).reshape(shape)


def partner(value, bits):
    return lax.ppermute(value, "tile", [(i, i ^ bits) for i in range(lax.axis_size("tile"))])


def halved(value):
    return value[:value.shape[0] // 2], value[value.shape[0] // 2:]


def shards(object_slices, probe_field, patterns, row_offsets, col_offsets, counts):
    size = lax.axis_size("tile")
    down = [((i + 1) % size, i) for i in range(size)]
    up = [(i, (i + 1) % size) for i in range(size)]
    own = flat(object_slices)
    mine = flat(probe_field)
    scalars = jnp.concatenate([row_offsets, col_offsets, counts])

    low, high = halved(own)
    low = lax.ppermute(low, "tile", down)
    quarter = jnp.concatenate([mine, partner(mine, 8), partner(mine, 4), partner(mine, 12)], axis=0)
    high, quarter, patterns, own = lax.optimization_barrier((high, quarter, patterns, own))
    near = jnp.concatenate([quarter, partner(quarter, 2)], axis=0)
    high = lax.ppermute(high, "tile", down)
    planes, patterns, mats = prepared(own, patterns)
    far = partner(near, 1)

    own_grad, low, high, keep, send = terms(scalars, planes, low, high, near, far, patterns, mats)

    total = keep + partner(send, 1)
    low = lax.ppermute(low, "tile", up)
    for bits in (2, 4):
        keep, send = halved(total)
        total = keep + partner(send, bits)
    high = lax.ppermute(high, "tile", up)
    keep, send = halved(total)
    send = partner(send, 8)
    object_grad = own_grad + jnp.concatenate([low, high], axis=0)
    object_grad, send = lax.optimization_barrier((object_grad, send))
    return unflat(object_grad, object_slices.shape), unflat(keep + send, probe_field.shape)


def solution(mesh):
    in_specs = (
        P(("groups", "tile"), None, None, None),
        P(("groups", "tile"), None, None, None),
        P(("groups", "tile"), None, None),
        P(("groups", "tile")),
        P(("groups", "tile")),
        P(("groups", "tile")),
    )
    out_specs = (P(("groups", "tile"), None, None, None), P(("groups", "tile"), None, None, None))
    return jax.shard_map(shards, mesh=mesh, in_specs=in_specs, out_specs=out_specs, check_vma=False)
```

```python
import math

import jax
import jax.numpy as jnp
import numpy as np
from jax import lax
from jax.experimental import pallas as pl
from jax.experimental.pallas import tpu as pltpu
from jax.sharding import PartitionSpec as P

GROUP_DEV = 16
KAPPA = 4.0
MODES = 2
SLICES = 2
HALVES = 2
AHEAD = (0, 8, 4, 12, 2, 10, 6, 14)
BACK = (0, 2, 8, 10, 4, 6, 12, 14)


def factors(extent):
    counter = np.arange(extent)
    dft = np.exp(-2j * np.pi * (counter[:, None] * counter[None, :] % extent) / extent) / math.sqrt(extent)
    freq = ((counter + extent // 2) % extent - extent // 2) / extent
    prop = np.conj(dft) @ (np.exp(-1j * np.pi * KAPPA * freq**2)[:, None] * dft)
    return np.stack([part for matrix in (dft, prop) for part in (matrix.real, matrix.imag)]).astype(np.float32)


def split(value):
    high = value.astype(jnp.bfloat16)
    low = (value - high.astype(jnp.float32)).astype(jnp.bfloat16)
    return high, low


def prepare(own_ref, patterns_ref, factors_ref, planes_out, patterns_out, mats_out, own, parts, sems):
    copies = [pltpu.make_async_copy(source, target, sems.at[i]) for i, (source, target) in enumerate(
        ((factors_ref, parts), (own_ref, own), (patterns_ref, patterns_out)))]
    for copy in copies:
        copy.start()
    copies[0].wait()
    extent = parts.shape[1]
    for kind in range(2):
        real, imag = split(parts[2 * kind]), split(parts[2 * kind + 1])
        for conj in range(2):
            for k in range(2):
                mat = 4 * kind + 2 * conj + k
                upper, lower = (-imag[k], imag[k]) if conj else (imag[k], -imag[k])
                mats_out[mat, :extent, :extent] = real[k]
                mats_out[mat, :extent, extent:] = upper
                mats_out[mat, extent:, :extent] = lower
                mats_out[mat, extent:, extent:] = real[k]
    copies[1].wait()
    rows = planes_out.shape[1]
    for layer in range(SLICES):
        for half in range(HALVES):
            for part in range(2):
                source = (layer * HALVES + half) * 2 + part
                plane = (layer * 2 + part) * HALVES + half
                planes_out[plane] = own[pl.ds(source, rows, stride=8), :]
    copies[2].wait()


def times(a, b):
    return [a[0] * b[0] - a[1] * b[1], a[0] * b[1] + a[1] * b[0]]


def conj_times(a, b):
    return [a[0] * b[0] + a[1] * b[1], a[0] * b[1] - a[1] * b[0]]


def add(a, b):
    return [a[0] + b[0], a[1] + b[1]]


def member_rows(member, order, share):
    return pl.ds(pl.multiple_of(lax.bitwise_xor(member, order) * share, share), share)


def place(probe_ref, keep_out, send_out):
    lanes, extent = probe_ref.shape[:2]
    share = extent // GROUP_DEV
    member = lax.rem(lax.axis_index("tile"), GROUP_DEV)
    for odd, ref in enumerate((keep_out, send_out)):
        for block, order in enumerate(BACK):
            for k in range(lanes):
                rows = pl.ds(block * share * lanes + k, share, stride=lanes)
                ref[rows, :] = probe_ref[k, member_rows(member, order + odd, share), :]


def kernel(scalars_ref, own_ref, next_ref, near_ref, far_ref, patterns_ref, mats_ref,
           own_out, next_out, probe_acc, obj, acc, probe):
    most, extent = patterns_ref.shape[:2]
    share = extent // GROUP_DEV
    member = lax.rem(lax.axis_index("tile"), GROUP_DEV)
    tile_rows = own_ref.shape[1]
    lanes = 2 * MODES
    modes = range(MODES)

    for layer in range(SLICES):
        for half in range(HALVES):
            for part in range(2):
                source = (layer * HALVES + half) * 2 + part
                plane = (layer * 2 + part) * HALVES + half
                obj[plane, :tile_rows] = own_ref[plane]
                obj[plane, tile_rows:] = next_ref[pl.ds(source, extent, stride=8), :]
    for odd, ref in enumerate((near_ref, far_ref)):
        for block, order in enumerate(AHEAD):
            for k in range(lanes):
                rows = pl.ds(block * share * lanes + k, share, stride=lanes)
                probe[k, member_rows(member, order + odd, share), :] = ref[rows, :]
    acc[...] = jnp.zeros(acc.shape, jnp.float32)
    probe_acc[...] = jnp.zeros(probe_acc.shape, jnp.float32)

    def right(fields, kind, conj):
        high_m, low_m = mats_ref[4 * kind + 2 * conj], mats_ref[4 * kind + 2 * conj + 1]
        rows = jnp.concatenate([jnp.concatenate(f[m], axis=1) for f in fields for m in modes], axis=0)
        high, low = split(rows)
        out = jnp.dot(jnp.concatenate([high, low, high], axis=1), jnp.concatenate([high_m, high_m, low_m], axis=0),
                      preferred_element_type=jnp.float32)
        return [[[out[(i * MODES + m) * extent:(i * MODES + m + 1) * extent, c * extent:(c + 1) * extent]
                  for c in range(2)] for m in modes] for i in range(len(fields))]

    def left(fields, kind, conj):
        high_m, low_m = mats_ref[4 * kind + 2 * (1 - conj)], mats_ref[4 * kind + 2 * (1 - conj) + 1]
        cols = jnp.concatenate([jnp.concatenate(f[m], axis=0) for f in fields for m in modes], axis=1)
        high, low = split(cols)
        out = jnp.dot(jnp.concatenate([high_m, high_m, low_m], axis=1), jnp.concatenate([high, low, high], axis=0),
                      preferred_element_type=jnp.float32)
        return [[[out[c * extent:(c + 1) * extent, (i * MODES + m) * extent:(i * MODES + m + 1) * extent]
                  for c in range(2)] for m in modes] for i in range(len(fields))]

    lane = lax.broadcasted_iota(jnp.int32, (extent, extent), 1)

    def window(slot):
        r, c = scalars_ref[slot], scalars_ref[most + slot]
        shift = lax.rem(extent - c, extent)
        layers = []
        for layer in range(SLICES):
            parts = []
            for part in range(2):
                plane = (layer * 2 + part) * HALVES
                joined = jnp.where(lane >= c, obj[plane, pl.ds(r, extent), :], obj[plane + 1, pl.ds(r, extent), :])
                parts.append(pltpu.roll(joined, shift, 1))
            layers.append(parts)
        return layers

    def deposit(slot, layer, grad):
        r, c = scalars_ref[slot], scalars_ref[most + slot]
        for part in range(2):
            plane = (layer * 2 + part) * HALVES
            rolled = pltpu.roll(grad[part], lax.rem(c, extent), 1)
            acc[plane, pl.ds(r, extent), :] += jnp.where(lane >= c, rolled, 0.0)
            acc[plane + 1, pl.ds(r, extent), :] += jnp.where(lane >= c, 0.0, rolled)

    def steps(slots):
        n = range(len(slots))
        field = [[probe[2 * m], probe[2 * m + 1]] for m in modes]
        objects = [window(slot) for slot in slots]
        state = right([[times(field[m], objects[i][0]) for m in modes] for i in n], 1, 0)
        yield
        entering = left(state, 1, 0)
        yield
        state = right([[times(entering[i][m], objects[i][1]) for m in modes] for i in n], 0, 0)
        yield
        state = left(state, 0, 0)
        yield
        weight = [2.0 * (sum(state[i][m][c] * state[i][m][c] for m in modes for c in range(2)) - patterns_ref[slots[i]])
                  for i in n]
        state = right([[[weight[i] * state[i][m][c] for c in range(2)] for m in modes] for i in n], 0, 1)
        yield
        state = left(state, 0, 1)
        yield
        for i in n:
            grad = conj_times(entering[i][0], state[i][0])
            for m in modes[1:]:
                grad = add(grad, conj_times(entering[i][m], state[i][m]))
            deposit(slots[i], 1, grad)
        state = right([[conj_times(objects[i][1], state[i][m]) for m in modes] for i in n], 1, 1)
        yield
        state = left(state, 1, 1)
        yield
        for i in n:
            grad = conj_times(field[0], state[i][0])
            for m in modes[1:]:
                grad = add(grad, conj_times(field[m], state[i][m]))
            deposit(slots[i], 0, grad)
        for m in modes:
            term = conj_times(objects[0][0], state[0][m])
            for i in n[1:]:
                term = add(term, conj_times(objects[i][0], state[i][m]))
            probe_acc[2 * m] += term[0]
            probe_acc[2 * m + 1] += term[1]

    def run(*sets):
        running = [steps(slots) for slots in sets]
        while running:
            running = [r for r in running if next(r, "done") is None]

    count = scalars_ref[2 * most]
    fours = lax.shift_right_logical(count, 2)

    def four(j, carry):
        run([4 * j, 4 * j + 1], [4 * j + 2, 4 * j + 3])
        return carry

    lax.fori_loop(0, fours, four, 0)

    @pl.when(lax.bitwise_and(count, 2) == 2)
    def _():
        run([4 * fours], [4 * fours + 1])

    @pl.when(lax.bitwise_and(count, 1) == 1)
    def _():
        run([count - 1])

    for layer in range(SLICES):
        for half in range(HALVES):
            for part in range(2):
                target = (layer * HALVES + half) * 2 + part
                plane = (layer * 2 + part) * HALVES + half
                own_out[pl.ds(target, tile_rows, stride=8), :] = acc[plane, :tile_rows]
                next_out[pl.ds(target, extent, stride=8), :] = acc[plane, tile_rows:]


def prepared(own, patterns):
    extent = patterns.shape[1]
    vmem = pl.BlockSpec(memory_space=pltpu.VMEM)
    parts = jnp.asarray(factors(extent))
    return pl.pallas_call(
        prepare,
        out_shape=(
            jax.ShapeDtypeStruct((8, own.shape[0] // 8, own.shape[1]), jnp.float32),
            jax.ShapeDtypeStruct(patterns.shape, jnp.float32),
            jax.ShapeDtypeStruct((8, 2 * extent, 2 * extent), jnp.bfloat16),
        ),
        in_specs=[pl.BlockSpec(memory_space=pltpu.HBM)] * 3,
        out_specs=(vmem,) * 3,
        scratch_shapes=[
            pltpu.VMEM(own.shape, jnp.float32),
            pltpu.VMEM(parts.shape, jnp.float32),
            pltpu.SemaphoreType.DMA((3,)),
        ],
        compiler_params=pltpu.CompilerParams(vmem_limit_bytes=16 * 1024 * 1024),
        cost_estimate=pl.CostEstimate(flops=0, bytes_accessed=6 * 1024 * 1024, transcendentals=0),
    )(own, patterns, parts)


def terms(scalars, planes, upper, near, far, patterns, mats):
    extent = patterns.shape[1]
    rows = planes.shape[1] + extent
    smem = pl.BlockSpec(memory_space=pltpu.SMEM)
    vmem = pl.BlockSpec(memory_space=pltpu.VMEM)
    return pl.pallas_call(
        kernel,
        out_shape=(
            jax.ShapeDtypeStruct((planes.shape[1] * 8, extent), jnp.float32),
            jax.ShapeDtypeStruct(upper.shape, jnp.float32),
            jax.ShapeDtypeStruct((2 * MODES, extent, extent), jnp.float32),
        ),
        in_specs=[smem] + [vmem] * 6,
        out_specs=(vmem,) * 3,
        scratch_shapes=[
            pltpu.VMEM((8, rows, extent), jnp.float32),
            pltpu.VMEM((8, rows, extent), jnp.float32),
            pltpu.VMEM((2 * MODES, extent, extent), jnp.float32),
        ],
        compiler_params=pltpu.CompilerParams(vmem_limit_bytes=40 * 1024 * 1024),
    )(scalars, planes, upper, near, far, patterns, mats)


def placed(probe_grad, shape):
    vmem = pl.BlockSpec(memory_space=pltpu.VMEM)
    return pl.pallas_call(
        place,
        out_shape=(jax.ShapeDtypeStruct(shape, jnp.float32),) * 2,
        in_specs=[vmem],
        out_specs=(vmem,) * 2,
        compiler_params=pltpu.CompilerParams(vmem_limit_bytes=4 * 1024 * 1024),
    )(probe_grad)


def flat(block):
    rows, k, parts, columns = block.shape
    split_up = block.reshape(rows, k, parts, columns // 128, 128)
    return split_up.transpose(0, 1, 3, 2, 4).reshape(-1, 128)


def unflat(value, shape):
    rows, k, parts, columns = shape
    return value.reshape(rows, k, columns // 128, parts, 128).transpose(0, 1, 3, 2, 4).reshape(shape)


def partner(value, bits):
    return lax.ppermute(value, "tile", [(i, i ^ bits) for i in range(lax.axis_size("tile"))])


def halved(value):
    return value[:value.shape[0] // 2], value[value.shape[0] // 2:]


def shards(object_slices, probe_field, patterns, row_offsets, col_offsets, counts):
    size = lax.axis_size("tile")
    own = flat(object_slices)
    scalars = jnp.concatenate([row_offsets, col_offsets, counts])

    upper = lax.ppermute(own, "tile", [((i + 1) % size, i) for i in range(size)])
    near = flat(probe_field)
    for bits in (8, 4):
        near = jnp.concatenate([near, partner(near, bits)], axis=0)
    near, patterns, own = lax.optimization_barrier((near, patterns, own))
    near = jnp.concatenate([near, partner(near, 2)], axis=0)
    planes, patterns, mats = prepared(own, patterns)
    near, planes, patterns, mats, scalars = lax.optimization_barrier((near, planes, patterns, mats, scalars))
    far = partner(near, 1)

    own_grad, back, probe_grad = terms(scalars, planes, upper, near, far, patterns, mats)

    back = lax.ppermute(back, "tile", [(i, (i + 1) % size) for i in range(size)])
    keep, send = placed(probe_grad, near.shape)
    total = keep + partner(send, 1)
    for bits in (4, 8):
        keep, send = halved(total)
        total = keep + partner(send, bits)
    back, total = lax.optimization_barrier((back, total))
    keep, send = halved(total)
    send = partner(send, 2)
    object_grad = own_grad + back
    object_grad, send = lax.optimization_barrier((object_grad, send))
    return unflat(object_grad, object_slices.shape), unflat(keep + send, probe_field.shape)


def solution(mesh):
    in_specs = (
        P(("groups", "tile"), None, None, None),
        P(("groups", "tile"), None, None, None),
        P(("groups", "tile"), None, None),
        P(("groups", "tile")),
        P(("groups", "tile")),
        P(("groups", "tile")),
    )
    out_specs = (P(("groups", "tile"), None, None, None), P(("groups", "tile"), None, None, None))
    return jax.shard_map(shards, mesh=mesh, in_specs=in_specs, out_specs=out_specs, check_vma=False)
```

```python
import math

import jax
import jax.numpy as jnp
import numpy as np
from jax import lax
from jax.experimental import pallas as pl
from jax.experimental.pallas import tpu as pltpu
from jax.sharding import PartitionSpec as P

GROUP_DEV = 16
KAPPA = 4.0
MODES = 2
SLICES = 2
HALVES = 2


def factors(extent):
    counter = np.arange(extent)
    dft = np.exp(-2j * np.pi * (counter[:, None] * counter[None, :] % extent) / extent) / math.sqrt(extent)
    freq = ((counter + extent // 2) % extent - extent // 2) / extent
    prop = np.conj(dft) @ (np.exp(-1j * np.pi * KAPPA * freq**2)[:, None] * dft)
    return np.stack([part for matrix in (dft, prop) for part in (matrix.real, matrix.imag)]).astype(np.float32)


def split(value):
    high = value.astype(jnp.bfloat16)
    low = (value - high.astype(jnp.float32)).astype(jnp.bfloat16)
    return high, low


def prepare(own_ref, patterns_ref, factors_ref, planes_out, patterns_out, mats_out, own, parts, sems):
    copies = [pltpu.make_async_copy(source, target, sems.at[i]) for i, (source, target) in enumerate(
        ((factors_ref, parts), (own_ref, own), (patterns_ref, patterns_out)))]
    for copy in copies:
        copy.start()
    copies[0].wait()
    extent = parts.shape[1]
    for kind in range(2):
        real, imag = split(parts[2 * kind]), split(parts[2 * kind + 1])
        for conj in range(2):
            for k in range(2):
                mat = 4 * kind + 2 * conj + k
                upper, lower = (-imag[k], imag[k]) if conj else (imag[k], -imag[k])
                mats_out[mat, :extent, :extent] = real[k]
                mats_out[mat, :extent, extent:] = upper
                mats_out[mat, extent:, :extent] = lower
                mats_out[mat, extent:, extent:] = real[k]
    copies[1].wait()
    rows = planes_out.shape[1]
    for layer in range(SLICES):
        for half in range(HALVES):
            for part in range(2):
                source = (layer * HALVES + half) * 2 + part
                plane = (layer * 2 + part) * HALVES + half
                planes_out[plane] = own[pl.ds(source, rows, stride=8), :]
    copies[2].wait()


def times(a, b):
    return [a[0] * b[0] - a[1] * b[1], a[0] * b[1] + a[1] * b[0]]


def conj_times(a, b):
    return [a[0] * b[0] + a[1] * b[1], a[0] * b[1] - a[1] * b[0]]


def add(a, b):
    return [a[0] + b[0], a[1] + b[1]]


def member_rows(number, odd, share):
    core = lax.bitwise_xor(lax.rem(lax.axis_index("tile"), 2), odd)
    return pl.ds(pl.multiple_of((2 * number + core) * share, share), share)


def place(probe_ref, keep_out, send_out):
    lanes, extent = probe_ref.shape[:2]
    share = extent // GROUP_DEV
    for odd, ref in enumerate((keep_out, send_out)):
        for number in range(GROUP_DEV // 2):
            for k in range(lanes):
                rows = pl.ds(number * share * lanes + k, share, stride=lanes)
                ref[rows, :] = probe_ref[k, member_rows(number, odd, share), :]


def kernel(scalars_ref, own_ref, next_ref, near_ref, far_ref, patterns_ref, mats_ref,
           own_out, next_out, probe_acc, obj, acc, probe):
    most, extent = patterns_ref.shape[:2]
    share = extent // GROUP_DEV
    tile_rows = own_ref.shape[1]
    lanes = 2 * MODES
    modes = range(MODES)

    for layer in range(SLICES):
        for half in range(HALVES):
            for part in range(2):
                source = (layer * HALVES + half) * 2 + part
                plane = (layer * 2 + part) * HALVES + half
                obj[plane, :tile_rows] = own_ref[plane]
                obj[plane, tile_rows:] = next_ref[pl.ds(source, extent, stride=8), :]
    for odd, ref in enumerate((near_ref, far_ref)):
        for number in range(GROUP_DEV // 2):
            for k in range(lanes):
                rows = pl.ds(number * share * lanes + k, share, stride=lanes)
                probe[k, member_rows(number, odd, share), :] = ref[rows, :]
    acc[...] = jnp.zeros(acc.shape, jnp.float32)
    probe_acc[...] = jnp.zeros(probe_acc.shape, jnp.float32)

    def right(fields, kind, conj):
        high_m, low_m = mats_ref[4 * kind + 2 * conj], mats_ref[4 * kind + 2 * conj + 1]
        rows = jnp.concatenate([jnp.concatenate(f[m], axis=1) for f in fields for m in modes], axis=0)
        high, low = split(rows)
        out = jnp.dot(jnp.concatenate([high, low, high], axis=1), jnp.concatenate([high_m, high_m, low_m], axis=0),
                      preferred_element_type=jnp.float32)
        return [[[out[(i * MODES + m) * extent:(i * MODES + m + 1) * extent, c * extent:(c + 1) * extent]
                  for c in range(2)] for m in modes] for i in range(len(fields))]

    def left(fields, kind, conj):
        high_m, low_m = mats_ref[4 * kind + 2 * (1 - conj)], mats_ref[4 * kind + 2 * (1 - conj) + 1]
        cols = jnp.concatenate([jnp.concatenate(f[m], axis=0) for f in fields for m in modes], axis=1)
        high, low = split(cols)
        out = jnp.dot(jnp.concatenate([high_m, high_m, low_m], axis=1), jnp.concatenate([high, low, high], axis=0),
                      preferred_element_type=jnp.float32)
        return [[[out[c * extent:(c + 1) * extent, (i * MODES + m) * extent:(i * MODES + m + 1) * extent]
                  for c in range(2)] for m in modes] for i in range(len(fields))]

    lane = lax.broadcasted_iota(jnp.int32, (extent, extent), 1)

    def window(slot):
        r, c = scalars_ref[slot], scalars_ref[most + slot]
        shift = lax.rem(extent - c, extent)
        layers = []
        for layer in range(SLICES):
            parts = []
            for part in range(2):
                plane = (layer * 2 + part) * HALVES
                joined = jnp.where(lane >= c, obj[plane, pl.ds(r, extent), :], obj[plane + 1, pl.ds(r, extent), :])
                parts.append(pltpu.roll(joined, shift, 1))
            layers.append(parts)
        return layers

    def deposit(slot, layer, grad):
        r, c = scalars_ref[slot], scalars_ref[most + slot]
        for part in range(2):
            plane = (layer * 2 + part) * HALVES
            rolled = pltpu.roll(grad[part], lax.rem(c, extent), 1)
            acc[plane, pl.ds(r, extent), :] += jnp.where(lane >= c, rolled, 0.0)
            acc[plane + 1, pl.ds(r, extent), :] += jnp.where(lane >= c, 0.0, rolled)

    def steps(slots):
        n = range(len(slots))
        field = [[probe[2 * m], probe[2 * m + 1]] for m in modes]
        objects = [window(slot) for slot in slots]
        state = right([[times(field[m], objects[i][0]) for m in modes] for i in n], 1, 0)
        yield
        entering = left(state, 1, 0)
        yield
        state = right([[times(entering[i][m], objects[i][1]) for m in modes] for i in n], 0, 0)
        yield
        state = left(state, 0, 0)
        yield
        weight = [2.0 * (sum(state[i][m][c] * state[i][m][c] for m in modes for c in range(2)) - patterns_ref[slots[i]])
                  for i in n]
        state = right([[[weight[i] * state[i][m][c] for c in range(2)] for m in modes] for i in n], 0, 1)
        yield
        state = left(state, 0, 1)
        yield
        for i in n:
            grad = conj_times(entering[i][0], state[i][0])
            for m in modes[1:]:
                grad = add(grad, conj_times(entering[i][m], state[i][m]))
            deposit(slots[i], 1, grad)
        state = right([[conj_times(objects[i][1], state[i][m]) for m in modes] for i in n], 1, 1)
        yield
        state = left(state, 1, 1)
        yield
        for i in n:
            grad = conj_times(field[0], state[i][0])
            for m in modes[1:]:
                grad = add(grad, conj_times(field[m], state[i][m]))
            deposit(slots[i], 0, grad)
        for m in modes:
            term = conj_times(objects[0][0], state[0][m])
            for i in n[1:]:
                term = add(term, conj_times(objects[i][0], state[i][m]))
            probe_acc[2 * m] += term[0]
            probe_acc[2 * m + 1] += term[1]

    def run(*sets):
        running = [steps(slots) for slots in sets]
        while running:
            running = [r for r in running if next(r, "done") is None]

    count = scalars_ref[2 * most]
    fours = lax.shift_right_logical(count, 2)

    def four(j, carry):
        run([4 * j, 4 * j + 1], [4 * j + 2, 4 * j + 3])
        return carry

    lax.fori_loop(0, fours, four, 0)

    @pl.when(lax.bitwise_and(count, 2) == 2)
    def _():
        run([4 * fours], [4 * fours + 1])

    @pl.when(lax.bitwise_and(count, 1) == 1)
    def _():
        run([count - 1])

    for layer in range(SLICES):
        for half in range(HALVES):
            for part in range(2):
                target = (layer * HALVES + half) * 2 + part
                plane = (layer * 2 + part) * HALVES + half
                own_out[pl.ds(target, tile_rows, stride=8), :] = acc[plane, :tile_rows]
                next_out[pl.ds(target, extent, stride=8), :] = acc[plane, tile_rows:]


def prepared(own, patterns):
    extent = patterns.shape[1]
    vmem = pl.BlockSpec(memory_space=pltpu.VMEM)
    parts = jnp.asarray(factors(extent))
    return pl.pallas_call(
        prepare,
        out_shape=(
            jax.ShapeDtypeStruct((8, own.shape[0] // 8, own.shape[1]), jnp.float32),
            jax.ShapeDtypeStruct(patterns.shape, jnp.float32),
            jax.ShapeDtypeStruct((8, 2 * extent, 2 * extent), jnp.bfloat16),
        ),
        in_specs=[pl.BlockSpec(memory_space=pltpu.HBM)] * 3,
        out_specs=(vmem,) * 3,
        scratch_shapes=[
            pltpu.VMEM(own.shape, jnp.float32),
            pltpu.VMEM(parts.shape, jnp.float32),
            pltpu.SemaphoreType.DMA((3,)),
        ],
        compiler_params=pltpu.CompilerParams(vmem_limit_bytes=16 * 1024 * 1024),
        cost_estimate=pl.CostEstimate(flops=0, bytes_accessed=6 * 1024 * 1024, transcendentals=0),
    )(own, patterns, parts)


def terms(scalars, planes, upper, near, far, patterns, mats):
    extent = patterns.shape[1]
    rows = planes.shape[1] + extent
    smem = pl.BlockSpec(memory_space=pltpu.SMEM)
    vmem = pl.BlockSpec(memory_space=pltpu.VMEM)
    return pl.pallas_call(
        kernel,
        out_shape=(
            jax.ShapeDtypeStruct((planes.shape[1] * 8, extent), jnp.float32),
            jax.ShapeDtypeStruct(upper.shape, jnp.float32),
            jax.ShapeDtypeStruct((2 * MODES, extent, extent), jnp.float32),
        ),
        in_specs=[smem] + [vmem] * 6,
        out_specs=(vmem,) * 3,
        scratch_shapes=[
            pltpu.VMEM((8, rows, extent), jnp.float32),
            pltpu.VMEM((8, rows, extent), jnp.float32),
            pltpu.VMEM((2 * MODES, extent, extent), jnp.float32),
        ],
        compiler_params=pltpu.CompilerParams(vmem_limit_bytes=40 * 1024 * 1024),
    )(scalars, planes, upper, near, far, patterns, mats)


def placed(probe_grad, shape):
    vmem = pl.BlockSpec(memory_space=pltpu.VMEM)
    return pl.pallas_call(
        place,
        out_shape=(jax.ShapeDtypeStruct(shape, jnp.float32),) * 2,
        in_specs=[vmem],
        out_specs=(vmem,) * 2,
        compiler_params=pltpu.CompilerParams(vmem_limit_bytes=4 * 1024 * 1024),
    )(probe_grad)


def flat(block):
    rows, k, parts, columns = block.shape
    split_up = block.reshape(rows, k, parts, columns // 128, 128)
    return split_up.transpose(0, 1, 3, 2, 4).reshape(-1, 128)


def unflat(value, shape):
    rows, k, parts, columns = shape
    return value.reshape(rows, k, columns // 128, parts, 128).transpose(0, 1, 3, 2, 4).reshape(shape)


def shards(object_slices, probe_field, patterns, row_offsets, col_offsets, counts):
    size = lax.axis_size("tile")
    cores = [(i, i ^ 1) for i in range(size)]
    alike = [list(range(g + core, g + GROUP_DEV, 2)) for g in range(0, size, GROUP_DEV) for core in range(2)]
    own = flat(object_slices)
    mine = flat(probe_field)
    scalars = jnp.concatenate([row_offsets, col_offsets, counts])

    upper = lax.ppermute(own, "tile", [((i + 1) % size, i) for i in range(size)])
    copies = jnp.broadcast_to(mine[None], (GROUP_DEV // 2,) + mine.shape)
    near = lax.all_to_all(copies, "tile", 0, 0, axis_index_groups=alike).reshape(-1, mine.shape[1])
    far = lax.ppermute(near, "tile", cores)
    planes, patterns, mats = prepared(own, patterns)

    own_grad, back, probe_grad = terms(scalars, planes, upper, near, far, patterns, mats)

    back = lax.ppermute(back, "tile", [(i, (i + 1) % size) for i in range(size)])
    keep, send = placed(probe_grad, near.shape)
    total = keep + lax.ppermute(send, "tile", cores)
    blocks = lax.all_to_all(total.reshape(copies.shape), "tile", 0, 0, axis_index_groups=alike)
    object_grad = own_grad + back
    return unflat(object_grad, object_slices.shape), unflat(jnp.sum(blocks, axis=0), probe_field.shape)


def solution(mesh):
    in_specs = (
        P(("groups", "tile"), None, None, None),
        P(("groups", "tile"), None, None, None),
        P(("groups", "tile"), None, None),
        P(("groups", "tile")),
        P(("groups", "tile")),
        P(("groups", "tile")),
    )
    out_specs = (P(("groups", "tile"), None, None, None), P(("groups", "tile"), None, None, None))
    return jax.shard_map(shards, mesh=mesh, in_specs=in_specs, out_specs=out_specs, check_vma=False)
```

```python
import functools
import math

import jax
import jax.numpy as jnp
import numpy as np
from jax import lax
from jax.experimental import pallas as pl
from jax.experimental.pallas import tpu as pltpu
from jax.sharding import PartitionSpec as P

GROUP_DEV = 16
KAPPA = 4.0
MODES = 2
SLICES = 2
HALVES = 2
AHEAD = (0, 8, 4, 12, 2, 10, 6, 14)
BACK = (0, 2, 8, 10, 4, 6, 12, 14)


def factors(extent):
    counter = np.arange(extent)
    dft = np.exp(-2j * np.pi * (counter[:, None] * counter[None, :] % extent) / extent) / math.sqrt(extent)
    freq = ((counter + extent // 2) % extent - extent // 2) / extent
    prop = np.conj(dft) @ (np.exp(-1j * np.pi * KAPPA * freq**2)[:, None] * dft)
    return np.stack([part for matrix in (dft, prop) for part in (matrix.real, matrix.imag)]).astype(np.float32)


def split(value):
    high = value.astype(jnp.bfloat16)
    low = (value - high.astype(jnp.float32)).astype(jnp.bfloat16)
    return high, low


def prepare(own_ref, patterns_ref, factors_ref, own_out, patterns_out, mats_out, parts, sems):
    copies = [pltpu.make_async_copy(source, target, sems.at[i]) for i, (source, target) in enumerate(
        ((factors_ref, parts), (own_ref, own_out), (patterns_ref, patterns_out)))]
    for copy in copies:
        copy.start()
    copies[0].wait()
    extent = parts.shape[1]
    for kind in range(2):
        real, imag = split(parts[2 * kind]), split(parts[2 * kind + 1])
        for conj in range(2):
            for k in range(2):
                mat = 4 * kind + 2 * conj + k
                upper, lower = (-imag[k], imag[k]) if conj else (imag[k], -imag[k])
                mats_out[mat, :extent, :extent] = real[k]
                mats_out[mat, :extent, extent:] = upper
                mats_out[mat, extent:, :extent] = lower
                mats_out[mat, extent:, extent:] = real[k]
    copies[1].wait()
    copies[2].wait()


def times(a, b):
    return [a[0] * b[0] - a[1] * b[1], a[0] * b[1] + a[1] * b[0]]


def conj_times(a, b):
    return [a[0] * b[0] + a[1] * b[1], a[0] * b[1] - a[1] * b[0]]


def add(a, b):
    return [a[0] + b[0], a[1] + b[1]]


def member_rows(member, order, share):
    return pl.ds(pl.multiple_of(lax.bitwise_xor(member, order) * share, share), share)


def place(probe_ref, keep_out, send_out):
    lanes, extent = probe_ref.shape[:2]
    share = extent // GROUP_DEV
    member = lax.rem(lax.axis_index("tile"), GROUP_DEV)
    for odd, ref in enumerate((keep_out, send_out)):
        for block, order in enumerate(BACK):
            for k in range(lanes):
                rows = pl.ds(block * share * lanes + k, share, stride=lanes)
                ref[rows, :] = probe_ref[k, member_rows(member, order + odd, share), :]


def kernel(own_core, scalars_ref, paired_ref, own_ref, other_ref, above_own_ref, above_other_ref, near_ref, far_ref,
           patterns_ref, odd_ref, mats_ref, start_ref, keep_out, send_out, probe_acc, obj, acc, probe):
    most, extent = patterns_ref.shape[:2]
    share = extent // GROUP_DEV
    place_in_tile = lax.axis_index("tile")
    member = lax.rem(place_in_tile, GROUP_DEV)
    is_own = lax.rem(place_in_tile, 2) == own_core
    tile_rows = own_ref.shape[0] // 8
    lanes = 2 * MODES
    modes = range(MODES)

    def tiles(low, high, into):
        for layer in range(SLICES):
            for half in range(HALVES):
                for part in range(2):
                    source = (layer * HALVES + half) * 2 + part
                    plane = (layer * 2 + part) * HALVES + half
                    into(plane, slice(0, tile_rows), low, pl.ds(source, tile_rows, stride=8))
                    into(plane, slice(tile_rows, tile_rows + extent), high, pl.ds(source, extent, stride=8))

    def load(plane, rows, ref, strided):
        obj[plane, rows] = ref[strided, :]

    def store(plane, rows, ref, strided):
        ref[strided, :] = acc[plane, rows]

    @pl.when(is_own)
    def _():
        tiles(own_ref, above_own_ref, load)

    @pl.when(jnp.logical_not(is_own))
    def _():
        tiles(other_ref, above_other_ref, load)

    for odd, ref in enumerate((near_ref, far_ref)):
        for block, order in enumerate(AHEAD):
            for k in range(lanes):
                rows = pl.ds(block * share * lanes + k, share, stride=lanes)
                probe[k, member_rows(member, order + odd, share), :] = ref[rows, :]
    acc[...] = jnp.zeros(acc.shape, jnp.float32)
    probe_acc[...] = jnp.zeros(probe_acc.shape, jnp.float32) if start_ref is None else start_ref[...]

    def right(fields, kind, conj):
        high_m, low_m = mats_ref[4 * kind + 2 * conj], mats_ref[4 * kind + 2 * conj + 1]
        rows = jnp.concatenate([jnp.concatenate(f[m], axis=1) for f in fields for m in modes], axis=0)
        high, low = split(rows)
        out = jnp.dot(jnp.concatenate([high, low, high], axis=1), jnp.concatenate([high_m, high_m, low_m], axis=0),
                      preferred_element_type=jnp.float32)
        return [[[out[(i * MODES + m) * extent:(i * MODES + m + 1) * extent, c * extent:(c + 1) * extent]
                  for c in range(2)] for m in modes] for i in range(len(fields))]

    def left(fields, kind, conj):
        high_m, low_m = mats_ref[4 * kind + 2 * (1 - conj)], mats_ref[4 * kind + 2 * (1 - conj) + 1]
        cols = jnp.concatenate([jnp.concatenate(f[m], axis=0) for f in fields for m in modes], axis=1)
        high, low = split(cols)
        out = jnp.dot(jnp.concatenate([high_m, high_m, low_m], axis=1), jnp.concatenate([high, low, high], axis=0),
                      preferred_element_type=jnp.float32)
        return [[[out[c * extent:(c + 1) * extent, (i * MODES + m) * extent:(i * MODES + m + 1) * extent]
                  for c in range(2)] for m in modes] for i in range(len(fields))]

    lane = lax.broadcasted_iota(jnp.int32, (extent, extent), 1)

    def corner(slot):
        own, odd = 2 * slot, 2 * slot + 1
        return (jnp.where(is_own, scalars_ref[own], paired_ref[odd]),
                jnp.where(is_own, scalars_ref[most + own], paired_ref[most + odd]))

    def window(slot):
        r, c = corner(slot)
        shift = lax.rem(extent - c, extent)
        layers = []
        for layer in range(SLICES):
            parts = []
            for part in range(2):
                plane = (layer * 2 + part) * HALVES
                joined = jnp.where(lane >= c, obj[plane, pl.ds(r, extent), :], obj[plane + 1, pl.ds(r, extent), :])
                parts.append(pltpu.roll(joined, shift, 1))
            layers.append(parts)
        return layers

    def deposit(slot, layer, grad):
        r, c = corner(slot)
        for part in range(2):
            plane = (layer * 2 + part) * HALVES
            rolled = pltpu.roll(grad[part], lax.rem(c, extent), 1)
            acc[plane, pl.ds(r, extent), :] += jnp.where(lane >= c, rolled, 0.0)
            acc[plane + 1, pl.ds(r, extent), :] += jnp.where(lane >= c, 0.0, rolled)

    def steps(slots):
        n = range(len(slots))
        field = [[probe[2 * m], probe[2 * m + 1]] for m in modes]
        objects = [window(slot) for slot in slots]
        state = right([[times(field[m], objects[i][0]) for m in modes] for i in n], 1, 0)
        yield
        entering = left(state, 1, 0)
        yield
        state = right([[times(entering[i][m], objects[i][1]) for m in modes] for i in n], 0, 0)
        yield
        state = left(state, 0, 0)
        yield
        weight = []
        for i in n:
            intensity = sum(state[i][m][c] * state[i][m][c] for m in modes for c in range(2))
            measured = jnp.where(is_own, patterns_ref[2 * slots[i]], odd_ref[slots[i]])
            weight.append(jnp.where(slots[i] < count, 2.0 * (intensity - measured), 0.0))
        state = right([[[weight[i] * state[i][m][c] for c in range(2)] for m in modes] for i in n], 0, 1)
        yield
        state = left(state, 0, 1)
        yield
        for i in n:
            grad = conj_times(entering[i][0], state[i][0])
            for m in modes[1:]:
                grad = add(grad, conj_times(entering[i][m], state[i][m]))
            deposit(slots[i], 1, grad)
        state = right([[conj_times(objects[i][1], state[i][m]) for m in modes] for i in n], 1, 1)
        yield
        state = left(state, 1, 1)
        yield
        for i in n:
            grad = conj_times(field[0], state[i][0])
            for m in modes[1:]:
                grad = add(grad, conj_times(field[m], state[i][m]))
            deposit(slots[i], 0, grad)
        for m in modes:
            term = conj_times(objects[0][0], state[0][m])
            for i in n[1:]:
                term = add(term, conj_times(objects[i][0], state[i][m]))
            probe_acc[2 * m] += term[0]
            probe_acc[2 * m + 1] += term[1]

    def run(*sets):
        running = [steps(slots) for slots in sets]
        while running:
            running = [r for r in running if next(r, "done") is None]

    count = jnp.where(is_own, lax.shift_right_logical(scalars_ref[2 * most] + 1, 1),
                      lax.shift_right_logical(paired_ref[2 * most], 1))
    fours = lax.shift_right_logical(count + 1, 2)
    left_over = count - 4 * fours

    def four(j, carry):
        run([4 * j, 4 * j + 1], [4 * j + 2, 4 * j + 3])
        return carry

    lax.fori_loop(0, fours, four, 0)

    @pl.when(left_over == 2)
    def _():
        run([4 * fours], [4 * fours + 1])

    @pl.when(left_over == 1)
    def _():
        run([4 * fours])

    @pl.when(is_own)
    def _():
        tiles(keep_out, send_out, store)

    @pl.when(jnp.logical_not(is_own))
    def _():
        tiles(send_out, keep_out, store)


def prepared(own, patterns):
    extent = patterns.shape[1]
    vmem = pl.BlockSpec(memory_space=pltpu.VMEM)
    parts = jnp.asarray(factors(extent))
    return pl.pallas_call(
        prepare,
        out_shape=(
            jax.ShapeDtypeStruct(own.shape, jnp.float32),
            jax.ShapeDtypeStruct(patterns.shape, jnp.float32),
            jax.ShapeDtypeStruct((8, 2 * extent, 2 * extent), jnp.bfloat16),
        ),
        in_specs=[pl.BlockSpec(memory_space=pl.ANY)] * 3,
        out_specs=(vmem,) * 3,
        scratch_shapes=[pltpu.VMEM(parts.shape, jnp.float32), pltpu.SemaphoreType.DMA((3,))],
        compiler_params=pltpu.CompilerParams(vmem_limit_bytes=16 * 1024 * 1024),
        cost_estimate=pl.CostEstimate(flops=0, bytes_accessed=6 * 1024 * 1024, transcendentals=0),
    )(own, patterns, parts)


def terms(own_core, scalars, paired, own, other, above_own, above_other, near, far, patterns, odd, mats, start=None):
    extent = patterns.shape[1]
    rows = own.shape[0] // 8 + extent
    smem = pl.BlockSpec(memory_space=pltpu.SMEM)
    vmem = pl.BlockSpec(memory_space=pltpu.VMEM)
    operands = [scalars, paired, own, other, above_own, above_other, near, far, patterns, odd, mats]
    if start is None:
        def body(*refs):
            return kernel(own_core, *refs[:len(operands)], None, *refs[len(operands):])
    else:
        operands.append(start)
        body = functools.partial(kernel, own_core)
    return pl.pallas_call(
        body,
        out_shape=(
            jax.ShapeDtypeStruct(own.shape, jnp.float32),
            jax.ShapeDtypeStruct(own.shape, jnp.float32),
            jax.ShapeDtypeStruct((2 * MODES, extent, extent), jnp.float32),
        ),
        in_specs=[smem] * 2 + [vmem] * (len(operands) - 2),
        out_specs=(vmem,) * 3,
        scratch_shapes=[
            pltpu.VMEM((8, rows, extent), jnp.float32),
            pltpu.VMEM((8, rows, extent), jnp.float32),
            pltpu.VMEM((2 * MODES, extent, extent), jnp.float32),
        ],
        compiler_params=pltpu.CompilerParams(vmem_limit_bytes=32 * 1024 * 1024),
        cost_estimate=pl.CostEstimate(flops=8 * 10**9, bytes_accessed=4 * 1024 * 1024, transcendentals=0),
    )(*operands)


def placed(probe_grad, shape):
    vmem = pl.BlockSpec(memory_space=pltpu.VMEM)
    return pl.pallas_call(
        place,
        out_shape=(jax.ShapeDtypeStruct(shape, jnp.float32),) * 2,
        in_specs=[vmem],
        out_specs=(vmem,) * 2,
        compiler_params=pltpu.CompilerParams(vmem_limit_bytes=4 * 1024 * 1024),
    )(probe_grad)


def flat(block):
    rows, k, parts, columns = block.shape
    split_up = block.reshape(rows, k, parts, columns // 128, 128)
    return split_up.transpose(0, 1, 3, 2, 4).reshape(-1, 128)


def unflat(value, shape):
    rows, k, parts, columns = shape
    return value.reshape(rows, k, columns // 128, parts, 128).transpose(0, 1, 3, 2, 4).reshape(shape)


def partner(value, bits):
    return lax.ppermute(value, "tile", [(i, i ^ bits) for i in range(lax.axis_size("tile"))])


def halved(value):
    return value[:value.shape[0] // 2], value[value.shape[0] // 2:]


def shards(object_slices, probe_field, patterns, row_offsets, col_offsets, counts):
    size = lax.axis_size("tile")
    own = flat(object_slices)
    scalars = jnp.concatenate([row_offsets, col_offsets, counts])

    near = flat(probe_field)
    for bits in (8, 4):
        near = jnp.concatenate([near, partner(near, bits)], axis=0)
    near = jnp.concatenate([near, partner(near, 2)], axis=0)
    other = partner(own, 1)
    paired = partner(scalars, 1)
    odd = partner(patterns.reshape((-1, 2) + patterns.shape[1:])[:, 1], 1)
    near, late = lax.optimization_barrier((near, own))
    above = lax.ppermute(late, "tile", [(i, (i - 2) % size if i % 2 == 0 else i) for i in range(size)])
    own, patterns, mats = prepared(own, patterns)
    far = partner(near, 1)

    keep, send, probe_grad = terms(
        0, scalars, paired, own, other, other, own, near, far, patterns, odd, mats)
    got = partner(send, 1)
    above, probe_grad = lax.optimization_barrier((above, probe_grad))
    passed, got = lax.optimization_barrier((partner(above, 1), got))
    keep_late, send_late, probe_grad = terms(
        1, scalars, paired, own, other, passed, above, near, far, patterns, odd, mats, probe_grad)

    carried = keep_late + partner(send_late, 1)
    object_grad = keep + got
    carried = lax.ppermute(carried, "tile", [(i, (i + 2) % size if i % 2 == 0 else i) for i in range(size)])
    grad_keep, grad_send = placed(probe_grad, near.shape)
    total = grad_keep + partner(grad_send, 1)
    for bits in (4, 8):
        grad_keep, grad_send = halved(total)
        total = grad_keep + partner(grad_send, bits)
    grad_keep, grad_send = halved(total)
    grad_send = partner(grad_send, 2)
    object_grad = object_grad + carried
    object_grad, grad_send = lax.optimization_barrier((object_grad, grad_send))
    return unflat(object_grad, object_slices.shape), unflat(grad_keep + grad_send, probe_field.shape)


def solution(mesh):
    in_specs = (
        P(("groups", "tile"), None, None, None),
        P(("groups", "tile"), None, None, None),
        P(("groups", "tile"), None, None),
        P(("groups", "tile")),
        P(("groups", "tile")),
        P(("groups", "tile")),
    )
    out_specs = (P(("groups", "tile"), None, None, None), P(("groups", "tile"), None, None, None))
    return jax.shard_map(shards, mesh=mesh, in_specs=in_specs, out_specs=out_specs, check_vma=False)
```

```python
import math

import jax
import jax.numpy as jnp
import numpy as np
from jax import lax
from jax.experimental import pallas as pl
from jax.experimental.pallas import tpu as pltpu
from jax.sharding import PartitionSpec as P

GROUP_DEV = 16
KAPPA = 4.0
MODES = 2
SLICES = 2
HALVES = 2
AHEAD = (0, 8, 4, 12, 2, 10, 6, 14)
BACK = (0, 2, 8, 10, 4, 6, 12, 14)


def factors(extent):
    counter = np.arange(extent)
    dft = np.exp(-2j * np.pi * (counter[:, None] * counter[None, :] % extent) / extent) / math.sqrt(extent)
    freq = ((counter + extent // 2) % extent - extent // 2) / extent
    prop = np.conj(dft) @ (np.exp(-1j * np.pi * KAPPA * freq**2)[:, None] * dft)
    return np.stack([part for matrix in (dft, prop) for part in (matrix.real, matrix.imag)]).astype(np.float32)


def prepare(own_ref, patterns_ref, factors_ref, planes_out, patterns_out, mats_out, own, parts, sems):
    copies = [pltpu.make_async_copy(source, target, sems.at[i]) for i, (source, target) in enumerate(
        ((factors_ref, parts), (own_ref, own), (patterns_ref, patterns_out)))]
    for copy in copies:
        copy.start()
    copies[0].wait()
    extent = parts.shape[1]
    for kind in range(2):
        real, imag = parts[2 * kind], parts[2 * kind + 1]
        for conj in range(2):
            mat = 2 * kind + conj
            upper, lower = (-imag, imag) if conj else (imag, -imag)
            mats_out[mat, :extent, :extent] = real
            mats_out[mat, :extent, extent:] = upper
            mats_out[mat, extent:, :extent] = lower
            mats_out[mat, extent:, extent:] = real
    copies[1].wait()
    rows = planes_out.shape[1]
    for layer in range(SLICES):
        for half in range(HALVES):
            for part in range(2):
                source = (layer * HALVES + half) * 2 + part
                plane = (layer * 2 + part) * HALVES + half
                planes_out[plane] = own[pl.ds(source, rows, stride=8), :]
    copies[2].wait()


def times(a, b):
    return [a[0] * b[0] - a[1] * b[1], a[0] * b[1] + a[1] * b[0]]


def conj_times(a, b):
    return [a[0] * b[0] + a[1] * b[1], a[0] * b[1] - a[1] * b[0]]


def add(a, b):
    return [a[0] + b[0], a[1] + b[1]]


def member_rows(member, order, share):
    return pl.ds(pl.multiple_of(lax.bitwise_xor(member, order) * share, share), share)


def place(probe_ref, keep_out, send_out):
    lanes, extent = probe_ref.shape[:2]
    share = extent // GROUP_DEV
    member = lax.rem(lax.axis_index("tile"), GROUP_DEV)
    for odd, ref in enumerate((keep_out, send_out)):
        for block, order in enumerate(BACK):
            for k in range(lanes):
                rows = pl.ds(block * share * lanes + k, share, stride=lanes)
                ref[rows, :] = probe_ref[k, member_rows(member, order + odd, share), :]


def kernel(scalars_ref, own_ref, low_ref, high_ref, near_ref, far_ref, patterns_ref, mats_ref,
           own_out, next_out, probe_acc, obj, acc, probe):
    most, extent = patterns_ref.shape[:2]
    share = extent // GROUP_DEV
    member = lax.rem(lax.axis_index("tile"), GROUP_DEV)
    tile_rows = own_ref.shape[1]
    middle = extent // 2
    lanes = 2 * MODES
    modes = range(MODES)

    for layer in range(SLICES):
        for half in range(HALVES):
            for part in range(2):
                source = (layer * HALVES + half) * 2 + part
                plane = (layer * 2 + part) * HALVES + half
                obj[plane, :tile_rows] = own_ref[plane]
                obj[plane, tile_rows:tile_rows + middle] = low_ref[pl.ds(source, middle, stride=8), :]
                obj[plane, tile_rows + middle:] = high_ref[pl.ds(source, extent - middle, stride=8), :]
    for odd, ref in enumerate((near_ref, far_ref)):
        for block, order in enumerate(AHEAD):
            for k in range(lanes):
                rows = pl.ds(block * share * lanes + k, share, stride=lanes)
                probe[k, member_rows(member, order + odd, share), :] = ref[rows, :]
    acc[...] = jnp.zeros(acc.shape, jnp.float32)
    probe_acc[...] = jnp.zeros(probe_acc.shape, jnp.float32)

    def product(first, second):
        return jnp.dot(first, second, precision=lax.Precision.HIGH, preferred_element_type=jnp.float32)

    def right(fields, kind, conj):
        rows = jnp.concatenate([jnp.concatenate(f[m], axis=1) for f in fields for m in modes], axis=0)
        out = product(rows, mats_ref[2 * kind + conj])
        return [[[out[(i * MODES + m) * extent:(i * MODES + m + 1) * extent, c * extent:(c + 1) * extent]
                  for c in range(2)] for m in modes] for i in range(len(fields))]

    def left(fields, kind, conj):
        cols = jnp.concatenate([jnp.concatenate(f[m], axis=0) for f in fields for m in modes], axis=1)
        out = product(mats_ref[2 * kind + 1 - conj], cols)
        return [[[out[c * extent:(c + 1) * extent, (i * MODES + m) * extent:(i * MODES + m + 1) * extent]
                  for c in range(2)] for m in modes] for i in range(len(fields))]

    lane = lax.broadcasted_iota(jnp.int32, (extent, extent), 1)

    def window(slot):
        r, c = scalars_ref[slot], scalars_ref[most + slot]
        shift = lax.rem(extent - c, extent)
        layers = []
        for layer in range(SLICES):
            parts = []
            for part in range(2):
                plane = (layer * 2 + part) * HALVES
                joined = jnp.where(lane >= c, obj[plane, pl.ds(r, extent), :], obj[plane + 1, pl.ds(r, extent), :])
                parts.append(pltpu.roll(joined, shift, 1))
            layers.append(parts)
        return layers

    def deposit(slot, layer, grad):
        r, c = scalars_ref[slot], scalars_ref[most + slot]
        for part in range(2):
            plane = (layer * 2 + part) * HALVES
            rolled = pltpu.roll(grad[part], lax.rem(c, extent), 1)
            acc[plane, pl.ds(r, extent), :] += jnp.where(lane >= c, rolled, 0.0)
            acc[plane + 1, pl.ds(r, extent), :] += jnp.where(lane >= c, 0.0, rolled)

    def steps(slots):
        n = range(len(slots))
        field = [[probe[2 * m], probe[2 * m + 1]] for m in modes]
        objects = [window(slot) for slot in slots]
        state = right([[times(field[m], objects[i][0]) for m in modes] for i in n], 1, 0)
        yield
        entering = left(state, 1, 0)
        yield
        state = right([[times(entering[i][m], objects[i][1]) for m in modes] for i in n], 0, 0)
        yield
        state = left(state, 0, 0)
        yield
        weight = [2.0 * (sum(state[i][m][c] * state[i][m][c] for m in modes for c in range(2)) - patterns_ref[slots[i]])
                  for i in n]
        state = right([[[weight[i] * state[i][m][c] for c in range(2)] for m in modes] for i in n], 0, 1)
        yield
        state = left(state, 0, 1)
        yield
        for i in n:
            grad = conj_times(entering[i][0], state[i][0])
            for m in modes[1:]:
                grad = add(grad, conj_times(entering[i][m], state[i][m]))
            deposit(slots[i], 1, grad)
        state = right([[conj_times(objects[i][1], state[i][m]) for m in modes] for i in n], 1, 1)
        yield
        state = left(state, 1, 1)
        yield
        for i in n:
            grad = conj_times(field[0], state[i][0])
            for m in modes[1:]:
                grad = add(grad, conj_times(field[m], state[i][m]))
            deposit(slots[i], 0, grad)
        for m in modes:
            term = conj_times(objects[0][0], state[0][m])
            for i in n[1:]:
                term = add(term, conj_times(objects[i][0], state[i][m]))
            probe_acc[2 * m] += term[0]
            probe_acc[2 * m + 1] += term[1]

    def run(*sets):
        running = [steps(slots) for slots in sets]
        while running:
            running = [r for r in running if next(r, "done") is None]

    count = scalars_ref[2 * most]
    fours = lax.shift_right_logical(count, 2)

    def four(j, carry):
        run([4 * j, 4 * j + 1], [4 * j + 2, 4 * j + 3])
        return carry

    lax.fori_loop(0, fours, four, 0)

    @pl.when(lax.bitwise_and(count, 2) == 2)
    def _():
        run([4 * fours], [4 * fours + 1])

    @pl.when(lax.bitwise_and(count, 1) == 1)
    def _():
        run([count - 1])

    for layer in range(SLICES):
        for half in range(HALVES):
            for part in range(2):
                target = (layer * HALVES + half) * 2 + part
                plane = (layer * 2 + part) * HALVES + half
                own_out[pl.ds(target, tile_rows, stride=8), :] = acc[plane, :tile_rows]
                next_out[pl.ds(target, extent, stride=8), :] = acc[plane, tile_rows:]


def prepared(own, patterns):
    extent = patterns.shape[1]
    vmem = pl.BlockSpec(memory_space=pltpu.VMEM)
    parts = jnp.asarray(factors(extent))
    return pl.pallas_call(
        prepare,
        out_shape=(
            jax.ShapeDtypeStruct((8, own.shape[0] // 8, own.shape[1]), jnp.float32),
            jax.ShapeDtypeStruct(patterns.shape, jnp.float32),
            jax.ShapeDtypeStruct((4, 2 * extent, 2 * extent), jnp.float32),
        ),
        in_specs=[pl.BlockSpec(memory_space=pltpu.HBM)] * 3,
        out_specs=(vmem,) * 3,
        scratch_shapes=[
            pltpu.VMEM(own.shape, jnp.float32),
            pltpu.VMEM(parts.shape, jnp.float32),
            pltpu.SemaphoreType.DMA((3,)),
        ],
        compiler_params=pltpu.CompilerParams(vmem_limit_bytes=16 * 1024 * 1024),
        cost_estimate=pl.CostEstimate(flops=0, bytes_accessed=6 * 1024 * 1024, transcendentals=0),
    )(own, patterns, parts)


def terms(scalars, planes, low, high, near, far, patterns, mats):
    extent = patterns.shape[1]
    rows = planes.shape[1] + extent
    smem = pl.BlockSpec(memory_space=pltpu.SMEM)
    vmem = pl.BlockSpec(memory_space=pltpu.VMEM)
    return pl.pallas_call(
        kernel,
        out_shape=(
            jax.ShapeDtypeStruct((planes.shape[1] * 8, extent), jnp.float32),
            jax.ShapeDtypeStruct((extent * 8, extent), jnp.float32),
            jax.ShapeDtypeStruct((2 * MODES, extent, extent), jnp.float32),
        ),
        in_specs=[smem] + [vmem] * 7,
        out_specs=(vmem,) * 3,
        scratch_shapes=[
            pltpu.VMEM((8, rows, extent), jnp.float32),
            pltpu.VMEM((8, rows, extent), jnp.float32),
            pltpu.VMEM((2 * MODES, extent, extent), jnp.float32),
        ],
        compiler_params=pltpu.CompilerParams(vmem_limit_bytes=40 * 1024 * 1024),
    )(scalars, planes, low, high, near, far, patterns, mats)


def placed(probe_grad, shape):
    vmem = pl.BlockSpec(memory_space=pltpu.VMEM)
    return pl.pallas_call(
        place,
        out_shape=(jax.ShapeDtypeStruct(shape, jnp.float32),) * 2,
        in_specs=[vmem],
        out_specs=(vmem,) * 2,
        compiler_params=pltpu.CompilerParams(vmem_limit_bytes=4 * 1024 * 1024),
    )(probe_grad)


def flat(block):
    rows, k, parts, columns = block.shape
    split_up = block.reshape(rows, k, parts, columns // 128, 128)
    return split_up.transpose(0, 1, 3, 2, 4).reshape(-1, 128)


def unflat(value, shape):
    rows, k, parts, columns = shape
    return value.reshape(rows, k, columns // 128, parts, 128).transpose(0, 1, 3, 2, 4).reshape(shape)


def partner(value, bits):
    return lax.ppermute(value, "tile", [(i, i ^ bits) for i in range(lax.axis_size("tile"))])


def halved(value):
    return value[:value.shape[0] // 2], value[value.shape[0] // 2:]


def probe_share(probe_grad, shape):
    keep, send = placed(probe_grad, shape)
    total = keep + partner(send, 1)
    for bits in (4, 8):
        keep, send = halved(total)
        total = keep + partner(send, bits)
    keep, send = halved(total)
    return keep + partner(send, 2)


def shards(object_slices, probe_field, patterns, row_offsets, col_offsets, counts):
    size = lax.axis_size("tile")
    down = [((i + 1) % size, i) for i in range(size)]
    own = flat(object_slices)
    low, high = halved(own)
    scalars = jnp.concatenate([row_offsets, col_offsets, counts])

    low = lax.ppermute(low, "tile", down)
    mine = flat(probe_field)
    quarter = jnp.concatenate([mine, partner(mine, 8), partner(mine, 4), partner(mine, 12)], axis=0)
    high, quarter, patterns, own = lax.optimization_barrier((high, quarter, patterns, own))
    near = jnp.concatenate([quarter, partner(quarter, 2)], axis=0)
    high = lax.ppermute(high, "tile", down)
    planes, patterns, mats = prepared(own, patterns)
    far = partner(near, 1)

    own_grad, back, probe_grad = terms(scalars, planes, low, high, near, far, patterns, mats)

    back = lax.ppermute(back, "tile", [(i, (i + 1) % size) for i in range(size)])
    probe_sum = lax.cond(
        counts[0] > 0,
        lambda grad: probe_share(grad, near.shape),
        lambda grad: jnp.zeros((near.shape[0] // 8, near.shape[1]), jnp.float32),
        probe_grad)
    object_grad = own_grad + back
    return unflat(object_grad, object_slices.shape), unflat(probe_sum, probe_field.shape)


def solution(mesh):
    in_specs = (
        P(("groups", "tile"), None, None, None),
        P(("groups", "tile"), None, None, None),
        P(("groups", "tile"), None, None),
        P(("groups", "tile")),
        P(("groups", "tile")),
        P(("groups", "tile")),
    )
    out_specs = (P(("groups", "tile"), None, None, None), P(("groups", "tile"), None, None, None))
    return jax.shard_map(shards, mesh=mesh, in_specs=in_specs, out_specs=out_specs, check_vma=False)
```

```python
import math

import jax
import jax.numpy as jnp
import numpy as np
from jax import lax
from jax.experimental import pallas as pl
from jax.experimental.pallas import tpu as pltpu
from jax.sharding import PartitionSpec as P

GROUP_DEV = 16
KAPPA = 4.0
MODES = 2
SLICES = 2
HALVES = 2
AHEAD = (0, 8, 4, 12, 2, 10, 6, 14)
BACK = (0, 2, 8, 10, 4, 6, 12, 14)


def factors(extent):
    counter = np.arange(extent)
    half = extent // 2
    dft = np.exp(-2j * np.pi * (counter[:, None] * counter[None, :] % extent) / extent) / math.sqrt(extent)
    freq = ((counter + extent // 2) % extent - extent // 2) / extent
    prop = np.conj(dft) @ (np.exp(-1j * np.pi * KAPPA * freq**2)[:, None] * dft)
    whole = [part for matrix in (dft, prop) for part in (matrix.real, matrix.imag)]
    same, cross = prop[:half, :half], prop[:half, half:]
    even, odd = dft[0::2, :half], dft[1::2, :half]
    halves = [even, odd, np.conj(even.T), np.conj(odd.T),
              (same + cross) / 2, (same - cross) / 2, np.conj(same + cross) / 2, np.conj(same - cross) / 2]
    halves = [np.block([[m.real, -m.imag], [m.imag, m.real]]) for m in halves]
    return np.stack(whole + halves).astype(np.float32)


def split(value):
    high = value.astype(jnp.bfloat16)
    low = (value - high.astype(jnp.float32)).astype(jnp.bfloat16)
    return high, low


def prepare(own_ref, patterns_ref, factors_ref, planes_out, patterns_out, mats_out, half_out, own, parts, sems):
    copies = [pltpu.make_async_copy(source, target, sems.at[i]) for i, (source, target) in enumerate(
        ((factors_ref, parts), (own_ref, own), (patterns_ref, patterns_out)))]
    for copy in copies:
        copy.start()
    copies[0].wait()
    extent = parts.shape[1]
    for kind in range(2):
        real, imag = split(parts[2 * kind]), split(parts[2 * kind + 1])
        for conj in range(2):
            for k in range(2):
                mat = 4 * kind + 2 * conj + k
                upper, lower = (-imag[k], imag[k]) if conj else (imag[k], -imag[k])
                mats_out[mat, :extent, :extent] = real[k]
                mats_out[mat, :extent, extent:] = upper
                mats_out[mat, extent:, :extent] = lower
                mats_out[mat, extent:, extent:] = real[k]
    for k in range(half_out.shape[0]):
        high, low = split(parts[4 + k])
        half_out[k, :extent, :extent] = high
        half_out[k, :extent, extent:] = high
        half_out[k, extent:, :extent] = low
        half_out[k, extent:, extent:] = low
    copies[1].wait()
    rows = planes_out.shape[1]
    for layer in range(SLICES):
        for half in range(HALVES):
            for part in range(2):
                source = (layer * HALVES + half) * 2 + part
                plane = (layer * 2 + part) * HALVES + half
                planes_out[plane] = own[pl.ds(source, rows, stride=8), :]
    copies[2].wait()


def times(a, b):
    return [a[0] * b[0] - a[1] * b[1], a[0] * b[1] + a[1] * b[0]]


def conj_times(a, b):
    return [a[0] * b[0] + a[1] * b[1], a[0] * b[1] - a[1] * b[0]]


def add(a, b):
    return [a[0] + b[0], a[1] + b[1]]


def member_rows(member, order, share):
    return pl.ds(pl.multiple_of(lax.bitwise_xor(member, order) * share, share), share)


def place(probe_ref, keep_out, send_out):
    lanes, extent = probe_ref.shape[:2]
    share = extent // GROUP_DEV
    member = lax.rem(lax.axis_index("tile"), GROUP_DEV)
    for odd, ref in enumerate((keep_out, send_out)):
        for block, order in enumerate(BACK):
            for k in range(lanes):
                rows = pl.ds(block * share * lanes + k, share, stride=lanes)
                ref[rows, :] = probe_ref[k, member_rows(member, order + odd, share), :]


def kernel(scalars_ref, own_ref, low_ref, high_ref, near_ref, far_ref, patterns_ref, mats_ref,
           half_ref, own_out, next_out, probe_acc, obj, acc, probe):
    most, extent = patterns_ref.shape[:2]
    share = extent // GROUP_DEV
    member = lax.rem(lax.axis_index("tile"), GROUP_DEV)
    tile_rows = own_ref.shape[1]
    middle = extent // 2
    lanes = 2 * MODES
    modes = range(MODES)

    for layer in range(SLICES):
        for half in range(HALVES):
            for part in range(2):
                source = (layer * HALVES + half) * 2 + part
                plane = (layer * 2 + part) * HALVES + half
                obj[plane, :tile_rows] = own_ref[plane]
                obj[plane, tile_rows:tile_rows + middle] = low_ref[pl.ds(source, middle, stride=8), :]
                obj[plane, tile_rows + middle:] = high_ref[pl.ds(source, extent - middle, stride=8), :]
    for odd, ref in enumerate((near_ref, far_ref)):
        for block, order in enumerate(AHEAD):
            for k in range(lanes):
                rows = pl.ds(block * share * lanes + k, share, stride=lanes)
                probe[k, member_rows(member, order + odd, share), :] = ref[rows, :]
    acc[...] = jnp.zeros(acc.shape, jnp.float32)
    probe_acc[...] = jnp.zeros(probe_acc.shape, jnp.float32)

    def right(fields, kind, conj):
        high_m, low_m = mats_ref[4 * kind + 2 * conj], mats_ref[4 * kind + 2 * conj + 1]
        rows = jnp.concatenate([jnp.concatenate(f[m], axis=1) for f in fields for m in modes], axis=0)
        high, low = split(rows)
        out = jnp.dot(jnp.concatenate([high, low, high], axis=1), jnp.concatenate([high_m, high_m, low_m], axis=0),
                      preferred_element_type=jnp.float32)
        return [[[out[(i * MODES + m) * extent:(i * MODES + m + 1) * extent, c * extent:(c + 1) * extent]
                  for c in range(2)] for m in modes] for i in range(len(fields))]

    def left(fields, kind, conj):
        middle = extent // 2
        cols = [jnp.concatenate([f[m][c] for f in fields for m in modes], axis=1) for c in range(2)]
        upper, lower = [c[:middle] for c in cols], [c[middle:] for c in cols]
        if kind == 1 or not conj:
            upper, lower = add(upper, lower), [u - v for u, v in zip(upper, lower)]
        halves = []
        for k, pieces in enumerate((upper, lower)):
            high, low = split(jnp.concatenate(pieces, axis=0))
            out = jnp.dot(half_ref[4 * kind + 2 * conj + k], jnp.concatenate([high, low], axis=0),
                          preferred_element_type=jnp.float32)
            out = out[:extent] + out[extent:]
            halves.append([out[:middle], out[middle:]])
        upper, lower = halves
        if kind == 1 or conj:
            upper, lower = add(upper, lower), [u - v for u, v in zip(upper, lower)]
        out = [jnp.concatenate([upper[c], lower[c]], axis=0) for c in range(2)]
        return [[[out[c][:, (i * MODES + m) * extent:(i * MODES + m + 1) * extent] for c in range(2)]
                 for m in modes] for i in range(len(fields))]

    lane = lax.broadcasted_iota(jnp.int32, (extent, extent), 1)

    def window(slot):
        r, c = scalars_ref[slot], scalars_ref[most + slot]
        shift = lax.rem(extent - c, extent)
        layers = []
        for layer in range(SLICES):
            parts = []
            for part in range(2):
                plane = (layer * 2 + part) * HALVES
                joined = jnp.where(lane >= c, obj[plane, pl.ds(r, extent), :], obj[plane + 1, pl.ds(r, extent), :])
                parts.append(pltpu.roll(joined, shift, 1))
            layers.append(parts)
        return layers

    def deposit(slot, layer, grad):
        r, c = scalars_ref[slot], scalars_ref[most + slot]
        for part in range(2):
            plane = (layer * 2 + part) * HALVES
            rolled = pltpu.roll(grad[part], lax.rem(c, extent), 1)
            acc[plane, pl.ds(r, extent), :] += jnp.where(lane >= c, rolled, 0.0)
            acc[plane + 1, pl.ds(r, extent), :] += jnp.where(lane >= c, 0.0, rolled)

    def measured(slot):
        return jnp.concatenate([patterns_ref[slot, pl.ds(k, extent // 2, stride=2), :] for k in range(2)], axis=0)

    def steps(slots):
        n = range(len(slots))
        field = [[probe[2 * m], probe[2 * m + 1]] for m in modes]
        objects = [window(slot) for slot in slots]
        state = right([[times(field[m], objects[i][0]) for m in modes] for i in n], 1, 0)
        yield
        entering = left(state, 1, 0)
        yield
        state = right([[times(entering[i][m], objects[i][1]) for m in modes] for i in n], 0, 0)
        yield
        state = left(state, 0, 0)
        yield
        weight = [2.0 * (sum(state[i][m][c] * state[i][m][c] for m in modes for c in range(2)) - measured(slots[i]))
                  for i in n]
        state = right([[[weight[i] * state[i][m][c] for c in range(2)] for m in modes] for i in n], 0, 1)
        yield
        state = left(state, 0, 1)
        yield
        for i in n:
            grad = conj_times(entering[i][0], state[i][0])
            for m in modes[1:]:
                grad = add(grad, conj_times(entering[i][m], state[i][m]))
            deposit(slots[i], 1, grad)
        state = right([[conj_times(objects[i][1], state[i][m]) for m in modes] for i in n], 1, 1)
        yield
        state = left(state, 1, 1)
        yield
        for i in n:
            grad = conj_times(field[0], state[i][0])
            for m in modes[1:]:
                grad = add(grad, conj_times(field[m], state[i][m]))
            deposit(slots[i], 0, grad)
        for m in modes:
            term = conj_times(objects[0][0], state[0][m])
            for i in n[1:]:
                term = add(term, conj_times(objects[i][0], state[i][m]))
            probe_acc[2 * m] += term[0]
            probe_acc[2 * m + 1] += term[1]

    def run(*sets):
        running = [steps(slots) for slots in sets]
        while running:
            running = [r for r in running if next(r, "done") is None]

    count = scalars_ref[2 * most]
    fours = lax.shift_right_logical(count, 2)

    def four(j, carry):
        run([4 * j, 4 * j + 1], [4 * j + 2, 4 * j + 3])
        return carry

    lax.fori_loop(0, fours, four, 0)

    @pl.when(lax.bitwise_and(count, 2) == 2)
    def _():
        run([4 * fours], [4 * fours + 1])

    @pl.when(lax.bitwise_and(count, 1) == 1)
    def _():
        run([count - 1])

    for layer in range(SLICES):
        for half in range(HALVES):
            for part in range(2):
                target = (layer * HALVES + half) * 2 + part
                plane = (layer * 2 + part) * HALVES + half
                own_out[pl.ds(target, tile_rows, stride=8), :] = acc[plane, :tile_rows]
                next_out[pl.ds(target, extent, stride=8), :] = acc[plane, tile_rows:]


def prepared(own, patterns):
    extent = patterns.shape[1]
    vmem = pl.BlockSpec(memory_space=pltpu.VMEM)
    parts = jnp.asarray(factors(extent))
    return pl.pallas_call(
        prepare,
        out_shape=(
            jax.ShapeDtypeStruct((8, own.shape[0] // 8, own.shape[1]), jnp.float32),
            jax.ShapeDtypeStruct(patterns.shape, jnp.float32),
            jax.ShapeDtypeStruct((8, 2 * extent, 2 * extent), jnp.bfloat16),
            jax.ShapeDtypeStruct((8, 2 * extent, 2 * extent), jnp.bfloat16),
        ),
        in_specs=[pl.BlockSpec(memory_space=pltpu.HBM)] * 3,
        out_specs=(vmem,) * 4,
        scratch_shapes=[
            pltpu.VMEM(own.shape, jnp.float32),
            pltpu.VMEM(parts.shape, jnp.float32),
            pltpu.SemaphoreType.DMA((3,)),
        ],
        compiler_params=pltpu.CompilerParams(vmem_limit_bytes=16 * 1024 * 1024),
        cost_estimate=pl.CostEstimate(flops=0, bytes_accessed=6 * 1024 * 1024, transcendentals=0),
    )(own, patterns, parts)


def terms(scalars, planes, low, high, near, far, patterns, mats):
    extent = patterns.shape[1]
    rows = planes.shape[1] + extent
    smem = pl.BlockSpec(memory_space=pltpu.SMEM)
    vmem = pl.BlockSpec(memory_space=pltpu.VMEM)
    return pl.pallas_call(
        kernel,
        out_shape=(
            jax.ShapeDtypeStruct((planes.shape[1] * 8, extent), jnp.float32),
            jax.ShapeDtypeStruct((extent * 8, extent), jnp.float32),
            jax.ShapeDtypeStruct((2 * MODES, extent, extent), jnp.float32),
        ),
        in_specs=[smem] + [vmem] * 8,
        out_specs=(vmem,) * 3,
        scratch_shapes=[
            pltpu.VMEM((8, rows, extent), jnp.float32),
            pltpu.VMEM((8, rows, extent), jnp.float32),
            pltpu.VMEM((2 * MODES, extent, extent), jnp.float32),
        ],
        compiler_params=pltpu.CompilerParams(vmem_limit_bytes=40 * 1024 * 1024),
    )(scalars, planes, low, high, near, far, patterns, *mats)


def placed(probe_grad, shape):
    vmem = pl.BlockSpec(memory_space=pltpu.VMEM)
    return pl.pallas_call(
        place,
        out_shape=(jax.ShapeDtypeStruct(shape, jnp.float32),) * 2,
        in_specs=[vmem],
        out_specs=(vmem,) * 2,
        compiler_params=pltpu.CompilerParams(vmem_limit_bytes=4 * 1024 * 1024),
    )(probe_grad)


def flat(block):
    rows, k, parts, columns = block.shape
    split_up = block.reshape(rows, k, parts, columns // 128, 128)
    return split_up.transpose(0, 1, 3, 2, 4).reshape(-1, 128)


def unflat(value, shape):
    rows, k, parts, columns = shape
    return value.reshape(rows, k, columns // 128, parts, 128).transpose(0, 1, 3, 2, 4).reshape(shape)


def partner(value, bits):
    return lax.ppermute(value, "tile", [(i, i ^ bits) for i in range(lax.axis_size("tile"))])


def halved(value):
    return value[:value.shape[0] // 2], value[value.shape[0] // 2:]


def probe_share(probe_grad, shape):
    keep, send = placed(probe_grad, shape)
    total = keep + partner(send, 1)
    for bits in (4, 8):
        keep, send = halved(total)
        total = keep + partner(send, bits)
    keep, send = halved(total)
    return keep + partner(send, 2)


def shards(object_slices, probe_field, patterns, row_offsets, col_offsets, counts):
    size = lax.axis_size("tile")
    down = [((i + 1) % size, i) for i in range(size)]
    own = flat(object_slices)
    low, high = halved(own)
    scalars = jnp.concatenate([row_offsets, col_offsets, counts])

    low = lax.ppermute(low, "tile", down)
    mine = flat(probe_field)
    quarter = jnp.concatenate([mine, partner(mine, 8), partner(mine, 4), partner(mine, 12)], axis=0)
    high, quarter, patterns, own = lax.optimization_barrier((high, quarter, patterns, own))
    near = jnp.concatenate([quarter, partner(quarter, 2)], axis=0)
    high = lax.ppermute(high, "tile", down)
    planes, patterns, *mats = prepared(own, patterns)
    far = partner(near, 1)

    own_grad, back, probe_grad = terms(scalars, planes, low, high, near, far, patterns, mats)

    back = lax.ppermute(back, "tile", [(i, (i + 1) % size) for i in range(size)])
    probe_sum = lax.cond(
        counts[0] > 0,
        lambda grad: probe_share(grad, near.shape),
        lambda grad: jnp.zeros((near.shape[0] // 8, near.shape[1]), jnp.float32),
        probe_grad)
    object_grad = own_grad + back
    return unflat(object_grad, object_slices.shape), unflat(probe_sum, probe_field.shape)


def solution(mesh):
    in_specs = (
        P(("groups", "tile"), None, None, None),
        P(("groups", "tile"), None, None, None),
        P(("groups", "tile"), None, None),
        P(("groups", "tile")),
        P(("groups", "tile")),
        P(("groups", "tile")),
    )
    out_specs = (P(("groups", "tile"), None, None, None), P(("groups", "tile"), None, None, None))
    return jax.shard_map(shards, mesh=mesh, in_specs=in_specs, out_specs=out_specs, check_vma=False)
```

```python
import functools
import math

import jax
import jax.numpy as jnp
import numpy as np
from jax import lax
from jax.experimental import pallas as pl
from jax.experimental.pallas import tpu as pltpu
from jax.sharding import PartitionSpec as P

GROUP_DEV = 16
KAPPA = 4.0
MODES = 2
SLICES = 2
HALVES = 2
AHEAD = (0, 8, 4, 12, 2, 10, 6, 14)
BACK = (0, 2, 8, 10, 4, 6, 12, 14)


def factors(extent):
    counter = np.arange(extent)
    half = extent // 2
    dft = np.exp(-2j * np.pi * (counter[:, None] * counter[None, :] % extent) / extent) / math.sqrt(extent)
    freq = ((counter + extent // 2) % extent - extent // 2) / extent
    prop = np.conj(dft) @ (np.exp(-1j * np.pi * KAPPA * freq**2)[:, None] * dft)
    whole = [part for matrix in (dft, prop) for part in (matrix.real, matrix.imag)]
    same, cross = prop[:half, :half], prop[:half, half:]
    even, odd = dft[0::2, :half], dft[1::2, :half]
    halves = [even, odd, np.conj(even.T), np.conj(odd.T),
              (same + cross) / 2, (same - cross) / 2, np.conj(same + cross) / 2, np.conj(same - cross) / 2]
    halves = [np.block([[m.real, -m.imag], [m.imag, m.real]]) for m in halves]
    return np.stack(whole + halves).astype(np.float32)


def split(value):
    high = value.astype(jnp.bfloat16)
    low = (value - high.astype(jnp.float32)).astype(jnp.bfloat16)
    return high, low


def prepare(own_ref, patterns_ref, factors_ref, planes_out, patterns_out, mats_out, half_out, own, parts, sems):
    copies = [pltpu.make_async_copy(source, target, sems.at[i]) for i, (source, target) in enumerate(
        ((factors_ref, parts), (own_ref, own), (patterns_ref, patterns_out)))]
    for copy in copies:
        copy.start()
    copies[0].wait()
    extent = parts.shape[1]
    for kind in range(2):
        real, imag = split(parts[2 * kind]), split(parts[2 * kind + 1])
        for conj in range(2):
            for k in range(2):
                mat = 4 * kind + 2 * conj + k
                upper, lower = (-imag[k], imag[k]) if conj else (imag[k], -imag[k])
                mats_out[mat, :extent, :extent] = real[k]
                mats_out[mat, :extent, extent:] = upper
                mats_out[mat, extent:, :extent] = lower
                mats_out[mat, extent:, extent:] = real[k]
    for k in range(half_out.shape[0]):
        high, low = split(parts[4 + k])
        half_out[k, :extent, :extent] = high
        half_out[k, :extent, extent:] = high
        half_out[k, extent:, :extent] = low
        half_out[k, extent:, extent:] = low
    copies[1].wait()
    rows = planes_out.shape[1]
    for layer in range(SLICES):
        for half in range(HALVES):
            for part in range(2):
                source = (layer * HALVES + half) * 2 + part
                plane = (layer * 2 + part) * HALVES + half
                planes_out[plane] = own[pl.ds(source, rows, stride=8), :]
    copies[2].wait()


def times(a, b):
    return [a[0] * b[0] - a[1] * b[1], a[0] * b[1] + a[1] * b[0]]


def conj_times(a, b):
    return [a[0] * b[0] + a[1] * b[1], a[0] * b[1] - a[1] * b[0]]


def add(a, b):
    return [a[0] + b[0], a[1] + b[1]]


def member_rows(member, order, share):
    return pl.ds(pl.multiple_of(lax.bitwise_xor(member, order) * share, share), share)


def place(probe_ref, keep_out, send_out):
    lanes, extent = probe_ref.shape[:2]
    share = extent // GROUP_DEV
    member = lax.rem(lax.axis_index("tile"), GROUP_DEV)
    for odd, ref in enumerate((keep_out, send_out)):
        for block, order in enumerate(BACK):
            for k in range(lanes):
                rows = pl.ds(block * share * lanes + k, share, stride=lanes)
                ref[rows, :] = probe_ref[k, member_rows(member, order + odd, share), :]


def kernel(call, scalars_ref, patterns_ref, mats_ref, half_ref, *refs):
    most, extent = patterns_ref.shape[:2]
    middle = extent // 2
    tile_rows = extent
    lanes = 2 * MODES
    modes = range(MODES)
    if call == 0:
        own_ref, low_ref, near_ref, far_ref, obj, acc, probe, probe_acc = refs
    elif call == 1:
        high_ref, old_obj, old_acc, probe, old_probe_acc, obj, acc, probe_acc, high_out = refs
    else:
        obj, old_acc, probe, old_probe_acc, own_out, low_out, probe_acc, acc = refs

    def pieces():
        for layer in range(SLICES):
            for half in range(HALVES):
                for part in range(2):
                    yield (layer * 2 + part) * HALVES + half, (layer * HALVES + half) * 2 + part

    if call == 0:
        share = extent // GROUP_DEV
        member = lax.rem(lax.axis_index("tile"), GROUP_DEV)
        for plane, source in pieces():
            obj[plane, :tile_rows] = own_ref[plane]
            obj[plane, tile_rows:tile_rows + middle] = low_ref[pl.ds(source, middle, stride=8), :]
            obj[plane, tile_rows + middle:] = jnp.zeros((extent - middle, extent), jnp.float32)
        for odd, ref in enumerate((near_ref, far_ref)):
            for block, order in enumerate(AHEAD):
                for k in range(lanes):
                    rows = pl.ds(block * share * lanes + k, share, stride=lanes)
                    probe[k, member_rows(member, order + odd, share), :] = ref[rows, :]
        acc[...] = jnp.zeros(acc.shape, jnp.float32)
        probe_acc[...] = jnp.zeros(probe_acc.shape, jnp.float32)
    else:
        if call == 1:
            for plane, source in pieces():
                obj[plane, :tile_rows + middle] = old_obj[plane, :tile_rows + middle]
                obj[plane, tile_rows + middle:] = high_ref[pl.ds(source, extent - middle, stride=8), :]
        acc[...] = old_acc[...]
        probe_acc[...] = old_probe_acc[...]

    def right(fields, kind, conj):
        high_m, low_m = mats_ref[4 * kind + 2 * conj], mats_ref[4 * kind + 2 * conj + 1]
        rows = jnp.concatenate([jnp.concatenate(f[m], axis=1) for f in fields for m in modes], axis=0)
        high, low = split(rows)
        out = jnp.dot(jnp.concatenate([high, low, high], axis=1), jnp.concatenate([high_m, high_m, low_m], axis=0),
                      preferred_element_type=jnp.float32)
        return [[[out[(i * MODES + m) * extent:(i * MODES + m + 1) * extent, c * extent:(c + 1) * extent]
                  for c in range(2)] for m in modes] for i in range(len(fields))]

    def left(fields, kind, conj):
        middle = extent // 2
        cols = [jnp.concatenate([f[m][c] for f in fields for m in modes], axis=1) for c in range(2)]
        upper, lower = [c[:middle] for c in cols], [c[middle:] for c in cols]
        if kind == 1 or not conj:
            upper, lower = add(upper, lower), [u - v for u, v in zip(upper, lower)]
        halves = []
        for k, pieces in enumerate((upper, lower)):
            high, low = split(jnp.concatenate(pieces, axis=0))
            out = jnp.dot(half_ref[4 * kind + 2 * conj + k], jnp.concatenate([high, low], axis=0),
                          preferred_element_type=jnp.float32)
            out = out[:extent] + out[extent:]
            halves.append([out[:middle], out[middle:]])
        upper, lower = halves
        if kind == 1 or conj:
            upper, lower = add(upper, lower), [u - v for u, v in zip(upper, lower)]
        out = [jnp.concatenate([upper[c], lower[c]], axis=0) for c in range(2)]
        return [[[out[c][:, (i * MODES + m) * extent:(i * MODES + m + 1) * extent] for c in range(2)]
                 for m in modes] for i in range(len(fields))]

    lane = lax.broadcasted_iota(jnp.int32, (extent, extent), 1)

    low_count = scalars_ref[3 * most]
    ending = lax.shift_right_logical(low_count, 3) * 4
    beginning = lax.shift_right_logical(low_count - ending, 2) * 4
    first = (0, beginning + ending, beginning)[call]
    count = (beginning, scalars_ref[3 * most + 1] - beginning - ending, ending)[call]

    def numbered(slot):
        return scalars_ref[2 * most + jnp.minimum(first + slot, most - 1)]

    def corner(slot):
        return scalars_ref[numbered(slot)], scalars_ref[most + numbered(slot)]

    def window(slot):
        r, c = corner(slot)
        shift = lax.rem(extent - c, extent)
        layers = []
        for layer in range(SLICES):
            parts = []
            for part in range(2):
                plane = (layer * 2 + part) * HALVES
                joined = jnp.where(lane >= c, obj[plane, pl.ds(r, extent), :], obj[plane + 1, pl.ds(r, extent), :])
                parts.append(pltpu.roll(joined, shift, 1))
            layers.append(parts)
        return layers

    def deposit(slot, layer, grad):
        r, c = corner(slot)
        for part in range(2):
            plane = (layer * 2 + part) * HALVES
            rolled = pltpu.roll(grad[part], lax.rem(c, extent), 1)
            acc[plane, pl.ds(r, extent), :] += jnp.where(lane >= c, rolled, 0.0)
            acc[plane + 1, pl.ds(r, extent), :] += jnp.where(lane >= c, 0.0, rolled)

    def measured(slot):
        return jnp.concatenate([patterns_ref[numbered(slot), pl.ds(k, extent // 2, stride=2), :] for k in range(2)], axis=0)

    def steps(slots):
        n = range(len(slots))
        field = [[probe[2 * m], probe[2 * m + 1]] for m in modes]
        objects = [window(slot) for slot in slots]
        state = right([[times(field[m], objects[i][0]) for m in modes] for i in n], 1, 0)
        yield
        entering = left(state, 1, 0)
        yield
        state = right([[times(entering[i][m], objects[i][1]) for m in modes] for i in n], 0, 0)
        yield
        state = left(state, 0, 0)
        yield
        weight = []
        for i in n:
            intensity = sum(state[i][m][c] * state[i][m][c] for m in modes for c in range(2))
            weight.append(jnp.where(slots[i] < count, 2.0 * (intensity - measured(slots[i])), 0.0))
        state = right([[[weight[i] * state[i][m][c] for c in range(2)] for m in modes] for i in n], 0, 1)
        yield
        state = left(state, 0, 1)
        yield
        for i in n:
            grad = conj_times(entering[i][0], state[i][0])
            for m in modes[1:]:
                grad = add(grad, conj_times(entering[i][m], state[i][m]))
            deposit(slots[i], 1, grad)
        state = right([[conj_times(objects[i][1], state[i][m]) for m in modes] for i in n], 1, 1)
        yield
        state = left(state, 1, 1)
        yield
        for i in n:
            grad = conj_times(field[0], state[i][0])
            for m in modes[1:]:
                grad = add(grad, conj_times(field[m], state[i][m]))
            deposit(slots[i], 0, grad)
        for m in modes:
            term = conj_times(objects[0][0], state[0][m])
            for i in n[1:]:
                term = add(term, conj_times(objects[i][0], state[i][m]))
            probe_acc[2 * m] += term[0]
            probe_acc[2 * m + 1] += term[1]

    def run(*sets):
        running = [steps(slots) for slots in sets]
        while running:
            running = [r for r in running if next(r, "done") is None]

    fours = lax.shift_right_logical(count + 1, 2)
    left_over = count - 4 * fours

    def four(j, carry):
        run([4 * j, 4 * j + 1], [4 * j + 2, 4 * j + 3])
        return carry

    lax.fori_loop(0, fours, four, 0)

    if call == 1:
        @pl.when(left_over == 2)
        def _():
            run([4 * fours], [4 * fours + 1])

        @pl.when(left_over == 1)
        def _():
            run([4 * fours])

        for plane, target in pieces():
            high_out[pl.ds(target, extent - middle, stride=8), :] = acc[plane, tile_rows + middle:]
    elif call == 2:
        for plane, target in pieces():
            own_out[pl.ds(target, tile_rows, stride=8), :] = acc[plane, :tile_rows]
            low_out[pl.ds(target, middle, stride=8), :] = acc[plane, tile_rows:tile_rows + middle]


def prepared(own, patterns):
    extent = patterns.shape[1]
    vmem = pl.BlockSpec(memory_space=pltpu.VMEM)
    parts = jnp.asarray(factors(extent))
    return pl.pallas_call(
        prepare,
        out_shape=(
            jax.ShapeDtypeStruct((8, own.shape[0] // 8, own.shape[1]), jnp.float32),
            jax.ShapeDtypeStruct(patterns.shape, jnp.float32),
            jax.ShapeDtypeStruct((8, 2 * extent, 2 * extent), jnp.bfloat16),
            jax.ShapeDtypeStruct((8, 2 * extent, 2 * extent), jnp.bfloat16),
        ),
        in_specs=[pl.BlockSpec(memory_space=pltpu.HBM)] * 3,
        out_specs=(vmem,) * 4,
        scratch_shapes=[
            pltpu.VMEM(own.shape, jnp.float32),
            pltpu.VMEM(parts.shape, jnp.float32),
            pltpu.SemaphoreType.DMA((3,)),
        ],
        compiler_params=pltpu.CompilerParams(vmem_limit_bytes=16 * 1024 * 1024),
        cost_estimate=pl.CostEstimate(flops=0, bytes_accessed=6 * 1024 * 1024, transcendentals=0),
    )(own, patterns, parts)


def terms(call, scalars, patterns, mats, *operands):
    extent = patterns.shape[1]
    smem = pl.BlockSpec(memory_space=pltpu.SMEM)
    vmem = pl.BlockSpec(memory_space=pltpu.VMEM)
    rows = pltpu.VMEM((8, 2 * extent, extent), jnp.float32)
    planes = jax.ShapeDtypeStruct((8, 2 * extent, extent), jnp.float32)
    probe = jax.ShapeDtypeStruct((2 * MODES, extent, extent), jnp.float32)
    whole = jax.ShapeDtypeStruct((8 * extent, extent), jnp.float32)
    half = jax.ShapeDtypeStruct((4 * extent, extent), jnp.float32)
    outs = ((planes, planes, probe, probe), (planes, planes, probe, half), (whole, half, probe))[call]
    operands = (scalars, patterns, *mats, *operands)
    return pl.pallas_call(
        functools.partial(kernel, call),
        out_shape=outs,
        in_specs=[smem] + [vmem] * (len(operands) - 1),
        out_specs=(vmem,) * len(outs),
        scratch_shapes=[rows] if call == 2 else [],
        compiler_params=pltpu.CompilerParams(vmem_limit_bytes=32 * 1024 * 1024),
        cost_estimate=pl.CostEstimate(flops=8 * 10**9, bytes_accessed=8 * 1024 * 1024, transcendentals=0),
    )(*operands)


def placed(probe_grad, shape):
    vmem = pl.BlockSpec(memory_space=pltpu.VMEM)
    return pl.pallas_call(
        place,
        out_shape=(jax.ShapeDtypeStruct(shape, jnp.float32),) * 2,
        in_specs=[vmem],
        out_specs=(vmem,) * 2,
        compiler_params=pltpu.CompilerParams(vmem_limit_bytes=4 * 1024 * 1024),
    )(probe_grad)


def flat(block):
    rows, k, parts, columns = block.shape
    split_up = block.reshape(rows, k, parts, columns // 128, 128)
    return split_up.transpose(0, 1, 3, 2, 4).reshape(-1, 128)


def unflat(value, shape):
    rows, k, parts, columns = shape
    return value.reshape(rows, k, columns // 128, parts, 128).transpose(0, 1, 3, 2, 4).reshape(shape)


def partner(value, bits):
    return lax.ppermute(value, "tile", [(i, i ^ bits) for i in range(lax.axis_size("tile"))])


def halved(value):
    return value[:value.shape[0] // 2], value[value.shape[0] // 2:]


def probe_share(probe_grad, shape):
    keep, send = placed(probe_grad, shape)
    total = keep + partner(send, 1)
    for bits in (4, 8):
        keep, send = halved(total)
        total = keep + partner(send, bits)
    keep, send = halved(total)
    return keep + partner(send, 2)


def plan(row_offsets, col_offsets, counts, extent):
    number = jnp.arange(row_offsets.shape[0], dtype=jnp.int32)
    live = number < counts[0]
    key = jnp.where(live, row_offsets, 2 * extent) * row_offsets.shape[0] + number
    rank = jnp.sum((key[None, :] < key[:, None]).astype(jnp.int32), axis=1)
    order = jnp.sum(jnp.where(rank[None, :] == number[:, None], number[None, :], 0), axis=1)
    low = jnp.sum((live & (row_offsets <= extent // 2)).astype(jnp.int32))
    return jnp.concatenate([row_offsets, col_offsets, order, low[None], counts])


def shards(object_slices, probe_field, patterns, row_offsets, col_offsets, counts):
    size = lax.axis_size("tile")
    down = [((i + 1) % size, i) for i in range(size)]
    up = [(i, (i + 1) % size) for i in range(size)]
    own = flat(object_slices)
    low, high = halved(own)
    scalars = plan(row_offsets, col_offsets, counts, patterns.shape[1])

    low = lax.ppermute(low, "tile", down)
    mine = flat(probe_field)
    quarter = jnp.concatenate([mine, partner(mine, 8), partner(mine, 4), partner(mine, 12)], axis=0)
    quarter, patterns, own, scalars = lax.optimization_barrier((quarter, patterns, own, scalars))
    planes, patterns, *mats = prepared(own, patterns)
    near = jnp.concatenate([quarter, partner(quarter, 2)], axis=0)
    high, near, patterns = lax.optimization_barrier((high, near, patterns))
    high = lax.ppermute(high, "tile", down)
    far = partner(near, 1)

    obj, acc, probe, probe_grad = terms(0, scalars, patterns, mats, planes, low, near, far)
    obj, acc, probe_grad, high = terms(1, scalars, patterns, mats, high, obj, acc, probe, probe_grad)
    high = lax.ppermute(high, "tile", up)
    own_grad, low, probe_grad = terms(2, scalars, patterns, mats, obj, acc, probe, probe_grad)

    high, low = lax.optimization_barrier((high, low))
    low = lax.ppermute(low, "tile", up)
    probe_sum = lax.cond(
        counts[0] > 0,
        lambda grad: probe_share(grad, near.shape),
        lambda grad: jnp.zeros((near.shape[0] // 8, near.shape[1]), jnp.float32),
        probe_grad)
    object_grad = own_grad + jnp.concatenate([low, high], axis=0)
    return unflat(object_grad, object_slices.shape), unflat(probe_sum, probe_field.shape)


def solution(mesh):
    in_specs = (
        P(("groups", "tile"), None, None, None),
        P(("groups", "tile"), None, None, None),
        P(("groups", "tile"), None, None),
        P(("groups", "tile")),
        P(("groups", "tile")),
        P(("groups", "tile")),
    )
    out_specs = (P(("groups", "tile"), None, None, None), P(("groups", "tile"), None, None, None))
    return jax.shard_map(shards, mesh=mesh, in_specs=in_specs, out_specs=out_specs, check_vma=False)
```

```python
import functools
import math

import jax
import jax.numpy as jnp
import numpy as np
from jax import lax
from jax.experimental import pallas as pl
from jax.experimental.pallas import tpu as pltpu
from jax.sharding import PartitionSpec as P

GROUP_DEV = 16
KAPPA = 4.0
MODES = 2
SLICES = 2
HALVES = 2
AHEAD = (0, 8, 4, 12, 2, 10, 6, 14)
BACK = (0, 2, 8, 10, 4, 6, 12, 14)


def factors(extent):
    counter = np.arange(extent)
    half = extent // 2
    dft = np.exp(-2j * np.pi * (counter[:, None] * counter[None, :] % extent) / extent) / math.sqrt(extent)
    freq = ((counter + extent // 2) % extent - extent // 2) / extent
    prop = np.conj(dft) @ (np.exp(-1j * np.pi * KAPPA * freq**2)[:, None] * dft)
    whole = [part for matrix in (dft, prop) for part in (matrix.real, matrix.imag)]
    same, cross = prop[:half, :half], prop[:half, half:]
    even, odd = dft[0::2, :half], dft[1::2, :half]
    halves = [even, odd, np.conj(even.T), np.conj(odd.T),
              (same + cross) / 2, (same - cross) / 2, np.conj(same + cross) / 2, np.conj(same - cross) / 2]
    halves = [np.block([[m.real, -m.imag], [m.imag, m.real]]) for m in halves]
    return np.stack(whole + halves).astype(np.float32)


def split(value):
    high = value.astype(jnp.bfloat16)
    low = (value - high.astype(jnp.float32)).astype(jnp.bfloat16)
    return high, low


def prepare(own_ref, patterns_ref, factors_ref, planes_out, patterns_out, mats_out, half_out, own, parts, sems):
    copies = [pltpu.make_async_copy(source, target, sems.at[i]) for i, (source, target) in enumerate(
        ((factors_ref, parts), (own_ref, own), (patterns_ref, patterns_out)))]
    for copy in copies:
        copy.start()
    copies[0].wait()
    extent = parts.shape[1]
    for kind in range(2):
        real, imag = split(parts[2 * kind]), split(parts[2 * kind + 1])
        for conj in range(2):
            for k in range(2):
                mat = 4 * kind + 2 * conj + k
                upper, lower = (-imag[k], imag[k]) if conj else (imag[k], -imag[k])
                mats_out[mat, :extent, :extent] = real[k]
                mats_out[mat, :extent, extent:] = upper
                mats_out[mat, extent:, :extent] = lower
                mats_out[mat, extent:, extent:] = real[k]
    for k in range(half_out.shape[0]):
        high, low = split(parts[4 + k])
        half_out[k, :extent, :extent] = high
        half_out[k, :extent, extent:] = high
        half_out[k, extent:, :extent] = low
        half_out[k, extent:, extent:] = low
    copies[1].wait()
    rows = planes_out.shape[1]
    for layer in range(SLICES):
        for half in range(HALVES):
            for part in range(2):
                source = (layer * HALVES + half) * 2 + part
                plane = (layer * 2 + part) * HALVES + half
                planes_out[plane] = own[pl.ds(source, rows, stride=8), :]
    copies[2].wait()


def times(a, b):
    return [a[0] * b[0] - a[1] * b[1], a[0] * b[1] + a[1] * b[0]]


def conj_times(a, b):
    return [a[0] * b[0] + a[1] * b[1], a[0] * b[1] - a[1] * b[0]]


def add(a, b):
    return [a[0] + b[0], a[1] + b[1]]


def member_rows(member, order, share):
    return pl.ds(pl.multiple_of(lax.bitwise_xor(member, order) * share, share), share)


def place(probe_ref, keep_out, send_out):
    lanes, extent = probe_ref.shape[:2]
    share = extent // GROUP_DEV
    member = lax.rem(lax.axis_index("tile"), GROUP_DEV)
    for odd, ref in enumerate((keep_out, send_out)):
        for block in range(GROUP_DEV // 2):
            there = lax.bitwise_xor(lax.rem(member + block // 2 * 4, GROUP_DEV), 2 * (block % 2) + odd)
            for k in range(lanes):
                rows = pl.ds(block * share * lanes + k, share, stride=lanes)
                ref[rows, :] = probe_ref[k, pl.ds(pl.multiple_of(there * share, share), share), :]


def kernel(call, scalars_ref, patterns_ref, mats_ref, half_ref, *refs):
    most, extent = patterns_ref.shape[:2]
    middle = extent // 2
    tile_rows = extent
    lanes = 2 * MODES
    modes = range(MODES)
    if call == 0:
        own_ref, low_ref, near_ref, far_ref, obj, acc, probe, probe_acc = refs
    elif call == 1:
        high_ref, old_obj, old_acc, probe, old_probe_acc, obj, acc, probe_acc, high_out = refs
    else:
        obj, old_acc, probe, old_probe_acc, own_out, low_out, probe_acc, acc = refs

    def pieces():
        for layer in range(SLICES):
            for half in range(HALVES):
                for part in range(2):
                    yield (layer * 2 + part) * HALVES + half, (layer * HALVES + half) * 2 + part

    if call == 0:
        share = extent // GROUP_DEV
        member = lax.rem(lax.axis_index("tile"), GROUP_DEV)
        for plane, source in pieces():
            obj[plane, :tile_rows] = own_ref[plane]
            obj[plane, tile_rows:tile_rows + middle] = low_ref[pl.ds(source, middle, stride=8), :]
            obj[plane, tile_rows + middle:] = jnp.zeros((extent - middle, extent), jnp.float32)
        for odd, ref in enumerate((near_ref, far_ref)):
            for block, order in enumerate(AHEAD):
                for k in range(lanes):
                    rows = pl.ds(block * share * lanes + k, share, stride=lanes)
                    probe[k, member_rows(member, order + odd, share), :] = ref[rows, :]
        acc[...] = jnp.zeros(acc.shape, jnp.float32)
        probe_acc[...] = jnp.zeros(probe_acc.shape, jnp.float32)
    else:
        if call == 1:
            for plane, source in pieces():
                obj[plane, :tile_rows + middle] = old_obj[plane, :tile_rows + middle]
                obj[plane, tile_rows + middle:] = high_ref[pl.ds(source, extent - middle, stride=8), :]
        acc[...] = old_acc[...]
        probe_acc[...] = old_probe_acc[...]

    def right(fields, kind, conj):
        high_m, low_m = mats_ref[4 * kind + 2 * conj], mats_ref[4 * kind + 2 * conj + 1]
        rows = jnp.concatenate([jnp.concatenate(f[m], axis=1) for f in fields for m in modes], axis=0)
        high, low = split(rows)
        out = jnp.dot(jnp.concatenate([high, low, high], axis=1), jnp.concatenate([high_m, high_m, low_m], axis=0),
                      preferred_element_type=jnp.float32)
        return [[[out[(i * MODES + m) * extent:(i * MODES + m + 1) * extent, c * extent:(c + 1) * extent]
                  for c in range(2)] for m in modes] for i in range(len(fields))]

    def left(fields, kind, conj):
        middle = extent // 2
        cols = [jnp.concatenate([f[m][c] for f in fields for m in modes], axis=1) for c in range(2)]
        upper, lower = [c[:middle] for c in cols], [c[middle:] for c in cols]
        if kind == 1 or not conj:
            upper, lower = add(upper, lower), [u - v for u, v in zip(upper, lower)]
        halves = []
        for k, pieces in enumerate((upper, lower)):
            high, low = split(jnp.concatenate(pieces, axis=0))
            out = jnp.dot(half_ref[4 * kind + 2 * conj + k], jnp.concatenate([high, low], axis=0),
                          preferred_element_type=jnp.float32)
            out = out[:extent] + out[extent:]
            halves.append([out[:middle], out[middle:]])
        upper, lower = halves
        if kind == 1 or conj:
            upper, lower = add(upper, lower), [u - v for u, v in zip(upper, lower)]
        out = [jnp.concatenate([upper[c], lower[c]], axis=0) for c in range(2)]
        return [[[out[c][:, (i * MODES + m) * extent:(i * MODES + m + 1) * extent] for c in range(2)]
                 for m in modes] for i in range(len(fields))]

    lane = lax.broadcasted_iota(jnp.int32, (extent, extent), 1)

    low_count = scalars_ref[3 * most]
    ending = lax.shift_right_logical(low_count, 3) * 4
    beginning = lax.shift_right_logical(low_count - ending, 2) * 4
    first = (0, beginning + ending, beginning)[call]
    count = (beginning, scalars_ref[3 * most + 1] - beginning - ending, ending)[call]

    def numbered(slot):
        return scalars_ref[2 * most + jnp.minimum(first + slot, most - 1)]

    def corner(slot):
        return scalars_ref[numbered(slot)], scalars_ref[most + numbered(slot)]

    def window(slot):
        r, c = corner(slot)
        shift = lax.rem(extent - c, extent)
        layers = []
        for layer in range(SLICES):
            parts = []
            for part in range(2):
                plane = (layer * 2 + part) * HALVES
                joined = jnp.where(lane >= c, obj[plane, pl.ds(r, extent), :], obj[plane + 1, pl.ds(r, extent), :])
                parts.append(pltpu.roll(joined, shift, 1))
            layers.append(parts)
        return layers

    def deposit(slot, layer, grad):
        r, c = corner(slot)
        for part in range(2):
            plane = (layer * 2 + part) * HALVES
            rolled = pltpu.roll(grad[part], lax.rem(c, extent), 1)
            acc[plane, pl.ds(r, extent), :] += jnp.where(lane >= c, rolled, 0.0)
            acc[plane + 1, pl.ds(r, extent), :] += jnp.where(lane >= c, 0.0, rolled)

    def measured(slot):
        return jnp.concatenate([patterns_ref[numbered(slot), pl.ds(k, extent // 2, stride=2), :] for k in range(2)], axis=0)

    def steps(slots):
        n = range(len(slots))
        field = [[probe[2 * m], probe[2 * m + 1]] for m in modes]
        objects = [window(slot) for slot in slots]
        state = right([[times(field[m], objects[i][0]) for m in modes] for i in n], 1, 0)
        yield
        entering = left(state, 1, 0)
        yield
        state = right([[times(entering[i][m], objects[i][1]) for m in modes] for i in n], 0, 0)
        yield
        state = left(state, 0, 0)
        yield
        weight = []
        for i in n:
            intensity = sum(state[i][m][c] * state[i][m][c] for m in modes for c in range(2))
            weight.append(jnp.where(slots[i] < count, 2.0 * (intensity - measured(slots[i])), 0.0))
        state = right([[[weight[i] * state[i][m][c] for c in range(2)] for m in modes] for i in n], 0, 1)
        yield
        state = left(state, 0, 1)
        yield
        for i in n:
            grad = conj_times(entering[i][0], state[i][0])
            for m in modes[1:]:
                grad = add(grad, conj_times(entering[i][m], state[i][m]))
            deposit(slots[i], 1, grad)
        state = right([[conj_times(objects[i][1], state[i][m]) for m in modes] for i in n], 1, 1)
        yield
        state = left(state, 1, 1)
        yield
        for i in n:
            grad = conj_times(field[0], state[i][0])
            for m in modes[1:]:
                grad = add(grad, conj_times(field[m], state[i][m]))
            deposit(slots[i], 0, grad)
        for m in modes:
            term = conj_times(objects[0][0], state[0][m])
            for i in n[1:]:
                term = add(term, conj_times(objects[i][0], state[i][m]))
            probe_acc[2 * m] += term[0]
            probe_acc[2 * m + 1] += term[1]

    def run(*sets):
        running = [steps(slots) for slots in sets]
        while running:
            running = [r for r in running if next(r, "done") is None]

    fours = lax.shift_right_logical(count + 1, 2)
    left_over = count - 4 * fours

    def four(j, carry):
        run([4 * j, 4 * j + 1], [4 * j + 2, 4 * j + 3])
        return carry

    lax.fori_loop(0, fours, four, 0)

    if call == 1:
        @pl.when(left_over == 2)
        def _():
            run([4 * fours], [4 * fours + 1])

        @pl.when(left_over == 1)
        def _():
            run([4 * fours])

        for plane, target in pieces():
            high_out[pl.ds(target, extent - middle, stride=8), :] = acc[plane, tile_rows + middle:]
    elif call == 2:
        for plane, target in pieces():
            own_out[pl.ds(target, tile_rows, stride=8), :] = acc[plane, :tile_rows]
            low_out[pl.ds(target, middle, stride=8), :] = acc[plane, tile_rows:tile_rows + middle]


def prepared(own, patterns):
    extent = patterns.shape[1]
    vmem = pl.BlockSpec(memory_space=pltpu.VMEM)
    parts = jnp.asarray(factors(extent))
    return pl.pallas_call(
        prepare,
        out_shape=(
            jax.ShapeDtypeStruct((8, own.shape[0] // 8, own.shape[1]), jnp.float32),
            jax.ShapeDtypeStruct(patterns.shape, jnp.float32),
            jax.ShapeDtypeStruct((8, 2 * extent, 2 * extent), jnp.bfloat16),
            jax.ShapeDtypeStruct((8, 2 * extent, 2 * extent), jnp.bfloat16),
        ),
        in_specs=[pl.BlockSpec(memory_space=pltpu.HBM)] * 3,
        out_specs=(vmem,) * 4,
        scratch_shapes=[
            pltpu.VMEM(own.shape, jnp.float32),
            pltpu.VMEM(parts.shape, jnp.float32),
            pltpu.SemaphoreType.DMA((3,)),
        ],
        compiler_params=pltpu.CompilerParams(vmem_limit_bytes=16 * 1024 * 1024),
        cost_estimate=pl.CostEstimate(flops=0, bytes_accessed=6 * 1024 * 1024, transcendentals=0),
    )(own, patterns, parts)


def terms(call, scalars, patterns, mats, *operands):
    extent = patterns.shape[1]
    smem = pl.BlockSpec(memory_space=pltpu.SMEM)
    vmem = pl.BlockSpec(memory_space=pltpu.VMEM)
    rows = pltpu.VMEM((8, 2 * extent, extent), jnp.float32)
    planes = jax.ShapeDtypeStruct((8, 2 * extent, extent), jnp.float32)
    probe = jax.ShapeDtypeStruct((2 * MODES, extent, extent), jnp.float32)
    whole = jax.ShapeDtypeStruct((8 * extent, extent), jnp.float32)
    half = jax.ShapeDtypeStruct((4 * extent, extent), jnp.float32)
    outs = ((planes, planes, probe, probe), (planes, planes, probe, half), (whole, half, probe))[call]
    operands = (scalars, patterns, *mats, *operands)
    return pl.pallas_call(
        functools.partial(kernel, call),
        out_shape=outs,
        in_specs=[smem] + [vmem] * (len(operands) - 1),
        out_specs=(vmem,) * len(outs),
        scratch_shapes=[rows] if call == 2 else [],
        compiler_params=pltpu.CompilerParams(vmem_limit_bytes=32 * 1024 * 1024),
        cost_estimate=pl.CostEstimate(flops=8 * 10**9, bytes_accessed=8 * 1024 * 1024, transcendentals=0),
    )(*operands)


def placed(probe_grad, shape):
    vmem = pl.BlockSpec(memory_space=pltpu.VMEM)
    return pl.pallas_call(
        place,
        out_shape=(jax.ShapeDtypeStruct(shape, jnp.float32),) * 2,
        in_specs=[vmem],
        out_specs=(vmem,) * 2,
        compiler_params=pltpu.CompilerParams(vmem_limit_bytes=4 * 1024 * 1024),
    )(probe_grad)


def flat(block):
    rows, k, parts, columns = block.shape
    split_up = block.reshape(rows, k, parts, columns // 128, 128)
    return split_up.transpose(0, 1, 3, 2, 4).reshape(-1, 128)


def unflat(value, shape):
    rows, k, parts, columns = shape
    return value.reshape(rows, k, columns // 128, parts, 128).transpose(0, 1, 3, 2, 4).reshape(shape)


def partner(value, bits):
    return lax.ppermute(value, "tile", [(i, i ^ bits) for i in range(lax.axis_size("tile"))])


def halved(value):
    return value[:value.shape[0] // 2], value[value.shape[0] // 2:]


def places_on(value, distance):
    members = range(lax.axis_size("tile"))
    return lax.ppermute(value, "tile", [
        (i, i // GROUP_DEV * GROUP_DEV + (i + distance) % GROUP_DEV) for i in members])


def plan(row_offsets, col_offsets, counts, extent):
    number = jnp.arange(row_offsets.shape[0], dtype=jnp.int32)
    live = number < counts[0]
    key = jnp.where(live, row_offsets, 2 * extent) * row_offsets.shape[0] + number
    rank = jnp.sum((key[None, :] < key[:, None]).astype(jnp.int32), axis=1)
    order = jnp.sum(jnp.where(rank[None, :] == number[:, None], number[None, :], 0), axis=1)
    low = jnp.sum((live & (row_offsets <= extent // 2)).astype(jnp.int32))
    return jnp.concatenate([row_offsets, col_offsets, order, low[None], counts])


def shards(object_slices, probe_field, patterns, row_offsets, col_offsets, counts):
    size = lax.axis_size("tile")
    down = [((i + 1) % size, i) for i in range(size)]
    up = [(i, (i + 1) % size) for i in range(size)]
    own = flat(object_slices)
    low, high = halved(own)

    low = lax.ppermute(low, "tile", down)
    mine = flat(probe_field)
    quarter = jnp.concatenate([mine, partner(mine, 8), partner(mine, 4), partner(mine, 12)], axis=0)
    quarter, patterns, own, offsets = lax.optimization_barrier(
        (quarter, patterns, own, (row_offsets, col_offsets, counts)))
    scalars = plan(*offsets, patterns.shape[1])
    planes, patterns, *mats = prepared(own, patterns)
    near = jnp.concatenate([quarter, partner(quarter, 2)], axis=0)
    high, near, patterns, scalars = lax.optimization_barrier((high, near, patterns, scalars))
    high = lax.ppermute(high, "tile", down)
    far = partner(near, 1)

    obj, acc, probe, probe_grad = terms(0, scalars, patterns, mats, planes, low, near, far)
    obj, acc, probe_grad, high = terms(1, scalars, patterns, mats, high, obj, acc, probe, probe_grad)
    high = lax.ppermute(high, "tile", up)
    own_grad, low, probe_grad = terms(2, scalars, patterns, mats, obj, acc, probe, probe_grad)

    low = lax.ppermute(low, "tile", up)
    keep, send = placed(probe_grad, near.shape)
    total = keep + partner(send, 1)
    high, total = lax.optimization_barrier((high, total))
    blocks = jnp.split(total, 4, axis=0)
    total = blocks[0] + sum(places_on(block, 4 * k) for k, block in enumerate(blocks) if k > 0)
    keep, send = halved(total)
    send = partner(send, 2)
    low, send = lax.optimization_barrier((low, send))
    object_grad = own_grad + jnp.concatenate([low, high], axis=0)
    return unflat(object_grad, object_slices.shape), unflat(keep + send, probe_field.shape)


def solution(mesh):
    in_specs = (
        P(("groups", "tile"), None, None, None),
        P(("groups", "tile"), None, None, None),
        P(("groups", "tile"), None, None),
        P(("groups", "tile")),
        P(("groups", "tile")),
        P(("groups", "tile")),
    )
    out_specs = (P(("groups", "tile"), None, None, None), P(("groups", "tile"), None, None, None))
    return jax.shard_map(shards, mesh=mesh, in_specs=in_specs, out_specs=out_specs, check_vma=False)
```

```python
import math

import jax
import jax.numpy as jnp
import numpy as np
from jax import lax
from jax.experimental import pallas as pl
from jax.experimental.pallas import tpu as pltpu
from jax.sharding import PartitionSpec as P

GROUP_DEV = 16
KAPPA = 4.0
MODES = 2
SLICES = 2
HALVES = 2
AHEAD = (0, 8, 4, 12, 2, 10, 6, 14)


def factors(extent):
    counter = np.arange(extent)
    half = extent // 2
    dft = np.exp(-2j * np.pi * (counter[:, None] * counter[None, :] % extent) / extent) / math.sqrt(extent)
    freq = ((counter + extent // 2) % extent - extent // 2) / extent
    prop = np.conj(dft) @ (np.exp(-1j * np.pi * KAPPA * freq**2)[:, None] * dft)
    whole = [part for matrix in (dft, prop) for part in (matrix.real, matrix.imag)]
    same, cross = prop[:half, :half], prop[:half, half:]
    even, odd = dft[0::2, :half], dft[1::2, :half]
    halves = [even, odd, np.conj(even.T), np.conj(odd.T),
              (same + cross) / 2, (same - cross) / 2, np.conj(same + cross) / 2, np.conj(same - cross) / 2]
    halves = [np.block([[m.real, -m.imag], [m.imag, m.real]]) for m in halves]
    return np.stack(whole + halves).astype(np.float32)


def split(value):
    high = value.astype(jnp.bfloat16)
    low = (value - high.astype(jnp.float32)).astype(jnp.bfloat16)
    return high, low


def prepare(own_ref, patterns_ref, factors_ref, planes_out, patterns_out, mats_out, half_out, own, parts, sems):
    copies = [pltpu.make_async_copy(source, target, sems.at[i]) for i, (source, target) in enumerate(
        ((factors_ref, parts), (own_ref, own), (patterns_ref, patterns_out)))]
    for copy in copies:
        copy.start()
    copies[0].wait()
    extent = parts.shape[1]
    for kind in range(2):
        real, imag = split(parts[2 * kind]), split(parts[2 * kind + 1])
        for conj in range(2):
            for k in range(2):
                mat = 4 * kind + 2 * conj + k
                upper, lower = (-imag[k], imag[k]) if conj else (imag[k], -imag[k])
                mats_out[mat, :extent, :extent] = real[k]
                mats_out[mat, :extent, extent:] = upper
                mats_out[mat, extent:, :extent] = lower
                mats_out[mat, extent:, extent:] = real[k]
    for k in range(half_out.shape[0]):
        high, low = split(parts[4 + k])
        half_out[k, :extent, :extent] = high
        half_out[k, :extent, extent:] = high
        half_out[k, extent:, :extent] = low
        half_out[k, extent:, extent:] = low
    copies[1].wait()
    rows = planes_out.shape[1]
    for layer in range(SLICES):
        for half in range(HALVES):
            for part in range(2):
                source = (layer * HALVES + half) * 2 + part
                plane = (layer * 2 + part) * HALVES + half
                planes_out[plane] = own[pl.ds(source, rows, stride=8), :]
    copies[2].wait()


def times(a, b):
    return [a[0] * b[0] - a[1] * b[1], a[0] * b[1] + a[1] * b[0]]


def conj_times(a, b):
    return [a[0] * b[0] + a[1] * b[1], a[0] * b[1] - a[1] * b[0]]


def add(a, b):
    return [a[0] + b[0], a[1] + b[1]]


def member_rows(member, order, share):
    return pl.ds(pl.multiple_of(lax.bitwise_xor(member, order) * share, share), share)


def place(probe_ref, keep_out, send_out):
    lanes, extent = probe_ref.shape[:2]
    share = extent // GROUP_DEV
    member = lax.rem(lax.axis_index("tile"), GROUP_DEV)
    for odd, ref in enumerate((keep_out, send_out)):
        for block in range(GROUP_DEV // 2):
            there = lax.bitwise_xor(lax.rem(member + block // 2 * 4, GROUP_DEV), 2 * (block % 2) + odd)
            for k in range(lanes):
                rows = pl.ds(block * share * lanes + k, share, stride=lanes)
                ref[rows, :] = probe_ref[k, pl.ds(pl.multiple_of(there * share, share), share), :]


def kernel(scalars_ref, own_ref, low_ref, high_ref, near_ref, far_ref, patterns_ref, mats_ref,
           half_ref, own_out, next_out, probe_acc, obj, acc, probe):
    most, extent = patterns_ref.shape[:2]
    share = extent // GROUP_DEV
    member = lax.rem(lax.axis_index("tile"), GROUP_DEV)
    tile_rows = own_ref.shape[1]
    middle = extent // 2
    lanes = 2 * MODES
    modes = range(MODES)

    for layer in range(SLICES):
        for half in range(HALVES):
            for part in range(2):
                source = (layer * HALVES + half) * 2 + part
                plane = (layer * 2 + part) * HALVES + half
                obj[plane, :tile_rows] = own_ref[plane]
                obj[plane, tile_rows:tile_rows + middle] = low_ref[pl.ds(source, middle, stride=8), :]
                obj[plane, tile_rows + middle:] = high_ref[pl.ds(source, extent - middle, stride=8), :]
    for odd, ref in enumerate((near_ref, far_ref)):
        for block, order in enumerate(AHEAD):
            for k in range(lanes):
                rows = pl.ds(block * share * lanes + k, share, stride=lanes)
                probe[k, member_rows(member, order + odd, share), :] = ref[rows, :]
    acc[...] = jnp.zeros(acc.shape, jnp.float32)
    probe_acc[...] = jnp.zeros(probe_acc.shape, jnp.float32)

    def right(fields, kind, conj):
        high_m, low_m = mats_ref[4 * kind + 2 * conj], mats_ref[4 * kind + 2 * conj + 1]
        rows = jnp.concatenate([jnp.concatenate(f[m], axis=1) for f in fields for m in modes], axis=0)
        high, low = split(rows)
        out = jnp.dot(jnp.concatenate([high, low, high], axis=1), jnp.concatenate([high_m, high_m, low_m], axis=0),
                      preferred_element_type=jnp.float32)
        return [[[out[(i * MODES + m) * extent:(i * MODES + m + 1) * extent, c * extent:(c + 1) * extent]
                  for c in range(2)] for m in modes] for i in range(len(fields))]

    def left(fields, kind, conj):
        middle = extent // 2
        cols = [jnp.concatenate([f[m][c] for f in fields for m in modes], axis=1) for c in range(2)]
        upper, lower = [c[:middle] for c in cols], [c[middle:] for c in cols]
        if kind == 1 or not conj:
            upper, lower = add(upper, lower), [u - v for u, v in zip(upper, lower)]
        halves = []
        for k, pieces in enumerate((upper, lower)):
            high, low = split(jnp.concatenate(pieces, axis=0))
            out = jnp.dot(half_ref[4 * kind + 2 * conj + k], jnp.concatenate([high, low], axis=0),
                          preferred_element_type=jnp.float32)
            out = out[:extent] + out[extent:]
            halves.append([out[:middle], out[middle:]])
        upper, lower = halves
        if kind == 1 or conj:
            upper, lower = add(upper, lower), [u - v for u, v in zip(upper, lower)]
        out = [jnp.concatenate([upper[c], lower[c]], axis=0) for c in range(2)]
        return [[[out[c][:, (i * MODES + m) * extent:(i * MODES + m + 1) * extent] for c in range(2)]
                 for m in modes] for i in range(len(fields))]

    lane = lax.broadcasted_iota(jnp.int32, (extent, extent), 1)

    def window(slot):
        r, c = scalars_ref[slot], scalars_ref[most + slot]
        shift = lax.rem(extent - c, extent)
        layers = []
        for layer in range(SLICES):
            parts = []
            for part in range(2):
                plane = (layer * 2 + part) * HALVES
                joined = jnp.where(lane >= c, obj[plane, pl.ds(r, extent), :], obj[plane + 1, pl.ds(r, extent), :])
                parts.append(pltpu.roll(joined, shift, 1))
            layers.append(parts)
        return layers

    def deposit(slot, layer, grad):
        r, c = scalars_ref[slot], scalars_ref[most + slot]
        for part in range(2):
            plane = (layer * 2 + part) * HALVES
            rolled = pltpu.roll(grad[part], lax.rem(c, extent), 1)
            acc[plane, pl.ds(r, extent), :] += jnp.where(lane >= c, rolled, 0.0)
            acc[plane + 1, pl.ds(r, extent), :] += jnp.where(lane >= c, 0.0, rolled)

    def measured(slot):
        return jnp.concatenate([patterns_ref[slot, pl.ds(k, extent // 2, stride=2), :] for k in range(2)], axis=0)

    def steps(slots):
        n = range(len(slots))
        field = [[probe[2 * m], probe[2 * m + 1]] for m in modes]
        objects = [window(slot) for slot in slots]
        state = right([[times(field[m], objects[i][0]) for m in modes] for i in n], 1, 0)
        yield
        entering = left(state, 1, 0)
        yield
        state = right([[times(entering[i][m], objects[i][1]) for m in modes] for i in n], 0, 0)
        yield
        state = left(state, 0, 0)
        yield
        weight = [2.0 * (sum(state[i][m][c] * state[i][m][c] for m in modes for c in range(2)) - measured(slots[i]))
                  for i in n]
        state = right([[[weight[i] * state[i][m][c] for c in range(2)] for m in modes] for i in n], 0, 1)
        yield
        state = left(state, 0, 1)
        yield
        for i in n:
            grad = conj_times(entering[i][0], state[i][0])
            for m in modes[1:]:
                grad = add(grad, conj_times(entering[i][m], state[i][m]))
            deposit(slots[i], 1, grad)
        state = right([[conj_times(objects[i][1], state[i][m]) for m in modes] for i in n], 1, 1)
        yield
        state = left(state, 1, 1)
        yield
        for i in n:
            grad = conj_times(field[0], state[i][0])
            for m in modes[1:]:
                grad = add(grad, conj_times(field[m], state[i][m]))
            deposit(slots[i], 0, grad)
        for m in modes:
            term = conj_times(objects[0][0], state[0][m])
            for i in n[1:]:
                term = add(term, conj_times(objects[i][0], state[i][m]))
            probe_acc[2 * m] += term[0]
            probe_acc[2 * m + 1] += term[1]

    def run(*sets):
        running = [steps(slots) for slots in sets]
        while running:
            running = [r for r in running if next(r, "done") is None]

    count = scalars_ref[2 * most]
    fours = lax.shift_right_logical(count, 2)

    def four(j, carry):
        run([4 * j, 4 * j + 1], [4 * j + 2, 4 * j + 3])
        return carry

    lax.fori_loop(0, fours, four, 0)

    @pl.when(lax.bitwise_and(count, 2) == 2)
    def _():
        run([4 * fours], [4 * fours + 1])

    @pl.when(lax.bitwise_and(count, 1) == 1)
    def _():
        run([count - 1])

    for layer in range(SLICES):
        for half in range(HALVES):
            for part in range(2):
                target = (layer * HALVES + half) * 2 + part
                plane = (layer * 2 + part) * HALVES + half
                own_out[pl.ds(target, tile_rows, stride=8), :] = acc[plane, :tile_rows]
                next_out[pl.ds(target, extent, stride=8), :] = acc[plane, tile_rows:]


def prepared(own, patterns):
    extent = patterns.shape[1]
    vmem = pl.BlockSpec(memory_space=pltpu.VMEM)
    parts = jnp.asarray(factors(extent))
    return pl.pallas_call(
        prepare,
        out_shape=(
            jax.ShapeDtypeStruct((8, own.shape[0] // 8, own.shape[1]), jnp.float32),
            jax.ShapeDtypeStruct(patterns.shape, jnp.float32),
            jax.ShapeDtypeStruct((8, 2 * extent, 2 * extent), jnp.bfloat16),
            jax.ShapeDtypeStruct((8, 2 * extent, 2 * extent), jnp.bfloat16),
        ),
        in_specs=[pl.BlockSpec(memory_space=pltpu.HBM)] * 3,
        out_specs=(vmem,) * 4,
        scratch_shapes=[
            pltpu.VMEM(own.shape, jnp.float32),
            pltpu.VMEM(parts.shape, jnp.float32),
            pltpu.SemaphoreType.DMA((3,)),
        ],
        compiler_params=pltpu.CompilerParams(vmem_limit_bytes=16 * 1024 * 1024),
        cost_estimate=pl.CostEstimate(flops=0, bytes_accessed=6 * 1024 * 1024, transcendentals=0),
    )(own, patterns, parts)


def terms(scalars, planes, low, high, near, far, patterns, mats):
    extent = patterns.shape[1]
    rows = planes.shape[1] + extent
    smem = pl.BlockSpec(memory_space=pltpu.SMEM)
    vmem = pl.BlockSpec(memory_space=pltpu.VMEM)
    return pl.pallas_call(
        kernel,
        out_shape=(
            jax.ShapeDtypeStruct((planes.shape[1] * 8, extent), jnp.float32),
            jax.ShapeDtypeStruct((extent * 8, extent), jnp.float32),
            jax.ShapeDtypeStruct((2 * MODES, extent, extent), jnp.float32),
        ),
        in_specs=[smem] + [vmem] * 8,
        out_specs=(vmem,) * 3,
        scratch_shapes=[
            pltpu.VMEM((8, rows, extent), jnp.float32),
            pltpu.VMEM((8, rows, extent), jnp.float32),
            pltpu.VMEM((2 * MODES, extent, extent), jnp.float32),
        ],
        compiler_params=pltpu.CompilerParams(vmem_limit_bytes=40 * 1024 * 1024),
    )(scalars, planes, low, high, near, far, patterns, *mats)


def placed(probe_grad, shape):
    vmem = pl.BlockSpec(memory_space=pltpu.VMEM)
    return pl.pallas_call(
        place,
        out_shape=(jax.ShapeDtypeStruct(shape, jnp.float32),) * 2,
        in_specs=[vmem],
        out_specs=(vmem,) * 2,
        compiler_params=pltpu.CompilerParams(vmem_limit_bytes=4 * 1024 * 1024),
    )(probe_grad)


def flat(block):
    rows, k, parts, columns = block.shape
    split_up = block.reshape(rows, k, parts, columns // 128, 128)
    return split_up.transpose(0, 1, 3, 2, 4).reshape(-1, 128)


def unflat(value, shape):
    rows, k, parts, columns = shape
    return value.reshape(rows, k, columns // 128, parts, 128).transpose(0, 1, 3, 2, 4).reshape(shape)


def partner(value, bits):
    return lax.ppermute(value, "tile", [(i, i ^ bits) for i in range(lax.axis_size("tile"))])


def halved(value):
    return value[:value.shape[0] // 2], value[value.shape[0] // 2:]


def places_on(value, distance):
    members = range(lax.axis_size("tile"))
    return lax.ppermute(value, "tile", [
        (i, i // GROUP_DEV * GROUP_DEV + (i + distance) % GROUP_DEV) for i in members])


def probe_share(probe_grad, shape):
    keep, send = placed(probe_grad, shape)
    blocks = jnp.split(keep + partner(send, 1), 4, axis=0)
    total = blocks[0] + sum(places_on(block, 4 * k) for k, block in enumerate(blocks) if k > 0)
    keep, send = halved(total)
    return keep + partner(send, 2)


def shards(object_slices, probe_field, patterns, row_offsets, col_offsets, counts):
    size = lax.axis_size("tile")
    down = [((i + 1) % size, i) for i in range(size)]
    own = flat(object_slices)
    low, high = halved(own)
    scalars = jnp.concatenate([row_offsets, col_offsets, counts])

    low = lax.ppermute(low, "tile", down)
    mine = flat(probe_field)
    quarter = jnp.concatenate([mine, partner(mine, 8), partner(mine, 4), partner(mine, 12)], axis=0)
    high, quarter, patterns, own = lax.optimization_barrier((high, quarter, patterns, own))
    near = jnp.concatenate([quarter, partner(quarter, 2)], axis=0)
    high = lax.ppermute(high, "tile", down)
    planes, patterns, *mats = prepared(own, patterns)
    near, planes, patterns, scalars, *mats = lax.optimization_barrier((near, planes, patterns, scalars, *mats))
    far = partner(near, 1)

    own_grad, back, probe_grad = terms(scalars, planes, low, high, near, far, patterns, mats)

    back = lax.ppermute(back, "tile", [(i, (i + 1) % size) for i in range(size)])
    probe_sum = lax.cond(
        counts[0] > 0,
        lambda grad: probe_share(grad, near.shape),
        lambda grad: jnp.zeros((near.shape[0] // 8, near.shape[1]), jnp.float32),
        probe_grad)
    object_grad = own_grad + back
    return unflat(object_grad, object_slices.shape), unflat(probe_sum, probe_field.shape)


def solution(mesh):
    in_specs = (
        P(("groups", "tile"), None, None, None),
        P(("groups", "tile"), None, None, None),
        P(("groups", "tile"), None, None),
        P(("groups", "tile")),
        P(("groups", "tile")),
        P(("groups", "tile")),
    )
    out_specs = (P(("groups", "tile"), None, None, None), P(("groups", "tile"), None, None, None))
    return jax.shard_map(shards, mesh=mesh, in_specs=in_specs, out_specs=out_specs, check_vma=False)
```

```python
import math

import jax
import jax.numpy as jnp
import numpy as np
from jax import lax
from jax.experimental import pallas as pl
from jax.experimental.pallas import tpu as pltpu
from jax.sharding import PartitionSpec as P

GROUP_DEV = 16
KAPPA = 4.0
MODES = 2
SLICES = 2
HALVES = 2
AHEAD = (0, 8, 4, 12, 2, 10, 6, 14)


def factors(extent):
    counter = np.arange(extent)
    half = extent // 2
    dft = np.exp(-2j * np.pi * (counter[:, None] * counter[None, :] % extent) / extent) / math.sqrt(extent)
    freq = ((counter + extent // 2) % extent - extent // 2) / extent
    prop = np.conj(dft) @ (np.exp(-1j * np.pi * KAPPA * freq**2)[:, None] * dft)
    whole = [part for matrix in (dft, prop) for part in (matrix.real, matrix.imag)]
    same, cross = prop[:half, :half], prop[:half, half:]
    even, odd = dft[0::2, :half], dft[1::2, :half]
    halves = [even, odd, np.conj(even.T), np.conj(odd.T),
              (same + cross) / 2, (same - cross) / 2, np.conj(same + cross) / 2, np.conj(same - cross) / 2]
    halves = [np.block([[m.real, -m.imag], [m.imag, m.real]]) for m in halves]
    return np.stack(whole + halves).astype(np.float32)


def split(value):
    high = value.astype(jnp.bfloat16)
    low = (value - high.astype(jnp.float32)).astype(jnp.bfloat16)
    return high, low


def prepare(own_ref, patterns_ref, factors_ref, planes_out, patterns_out, mats_out, half_out, own, parts, sems):
    copies = [pltpu.make_async_copy(source, target, sems.at[i]) for i, (source, target) in enumerate(
        ((factors_ref, parts), (own_ref, own), (patterns_ref, patterns_out)))]
    for copy in copies:
        copy.start()
    copies[0].wait()
    extent = parts.shape[1]
    for kind in range(2):
        real, imag = split(parts[2 * kind]), split(parts[2 * kind + 1])
        for conj in range(2):
            for k in range(2):
                mat = 4 * kind + 2 * conj + k
                upper, lower = (-imag[k], imag[k]) if conj else (imag[k], -imag[k])
                mats_out[mat, :extent, :extent] = real[k]
                mats_out[mat, :extent, extent:] = upper
                mats_out[mat, extent:, :extent] = lower
                mats_out[mat, extent:, extent:] = real[k]
    for k in range(half_out.shape[0]):
        high, low = split(parts[4 + k])
        half_out[k, :extent, :extent] = high
        half_out[k, :extent, extent:] = high
        half_out[k, extent:, :extent] = low
        half_out[k, extent:, extent:] = low
    copies[1].wait()
    rows = planes_out.shape[1]
    for layer in range(SLICES):
        for half in range(HALVES):
            for part in range(2):
                source = (layer * HALVES + half) * 2 + part
                plane = (layer * 2 + part) * HALVES + half
                planes_out[plane] = own[pl.ds(source, rows, stride=8), :]
    copies[2].wait()


def times(a, b):
    return [a[0] * b[0] - a[1] * b[1], a[0] * b[1] + a[1] * b[0]]


def conj_times(a, b):
    return [a[0] * b[0] + a[1] * b[1], a[0] * b[1] - a[1] * b[0]]


def add(a, b):
    return [a[0] + b[0], a[1] + b[1]]


def member_rows(member, order, share):
    return pl.ds(pl.multiple_of(lax.bitwise_xor(member, order) * share, share), share)


def place(probe_ref, keep_out, send_out):
    lanes, extent = probe_ref.shape[:2]
    share = extent // GROUP_DEV
    member = lax.rem(lax.axis_index("tile"), GROUP_DEV)
    for odd, ref in enumerate((keep_out, send_out)):
        for block in range(GROUP_DEV // 2):
            there = lax.bitwise_xor(lax.rem(member + block // 2 * 4, GROUP_DEV), 2 * (block % 2) + odd)
            for k in range(lanes):
                rows = pl.ds(block * share * lanes + k, share, stride=lanes)
                ref[rows, :] = probe_ref[k, pl.ds(pl.multiple_of(there * share, share), share), :]


def kernel(scalars_ref, own_ref, low_ref, high_ref, near_ref, far_ref, patterns_ref, mats_ref,
           half_ref, own_out, next_out, probe_acc, obj, acc, probe):
    most, extent = patterns_ref.shape[:2]
    share = extent // GROUP_DEV
    member = lax.rem(lax.axis_index("tile"), GROUP_DEV)
    tile_rows = own_ref.shape[1]
    middle = extent // 2
    lanes = 2 * MODES
    modes = range(MODES)

    for layer in range(SLICES):
        for half in range(HALVES):
            for part in range(2):
                source = (layer * HALVES + half) * 2 + part
                plane = (layer * 2 + part) * HALVES + half
                obj[plane, :tile_rows] = own_ref[plane]
                obj[plane, tile_rows:tile_rows + middle] = low_ref[pl.ds(source, middle, stride=8), :]
                obj[plane, tile_rows + middle:] = high_ref[pl.ds(source, extent - middle, stride=8), :]
    for odd, ref in enumerate((near_ref, far_ref)):
        for block, order in enumerate(AHEAD):
            for k in range(lanes):
                rows = pl.ds(block * share * lanes + k, share, stride=lanes)
                probe[k, member_rows(member, order + odd, share), :] = ref[rows, :]
    acc[...] = jnp.zeros(acc.shape, jnp.float32)
    probe_acc[...] = jnp.zeros(probe_acc.shape, jnp.float32)

    def right(fields, kind, conj):
        high_m, low_m = mats_ref[4 * kind + 2 * conj], mats_ref[4 * kind + 2 * conj + 1]
        rows = jnp.concatenate([jnp.concatenate(f[m], axis=1) for f in fields for m in modes], axis=0)
        high, low = split(rows)
        out = jnp.dot(jnp.concatenate([high, low, high], axis=1), jnp.concatenate([high_m, high_m, low_m], axis=0),
                      preferred_element_type=jnp.float32)
        return [[[out[(i * MODES + m) * extent:(i * MODES + m + 1) * extent, c * extent:(c + 1) * extent]
                  for c in range(2)] for m in modes] for i in range(len(fields))]

    def left(fields, kind, conj):
        middle = extent // 2
        cols = [jnp.concatenate([f[m][c] for f in fields for m in modes], axis=1) for c in range(2)]
        upper, lower = [c[:middle] for c in cols], [c[middle:] for c in cols]
        if kind == 1 or not conj:
            upper, lower = add(upper, lower), [u - v for u, v in zip(upper, lower)]
        halves = []
        for k, pieces in enumerate((upper, lower)):
            high, low = split(jnp.concatenate(pieces, axis=0))
            out = jnp.dot(half_ref[4 * kind + 2 * conj + k], jnp.concatenate([high, low], axis=0),
                          preferred_element_type=jnp.float32)
            out = out[:extent] + out[extent:]
            halves.append([out[:middle], out[middle:]])
        upper, lower = halves
        if kind == 1 or conj:
            upper, lower = add(upper, lower), [u - v for u, v in zip(upper, lower)]
        out = [jnp.concatenate([upper[c], lower[c]], axis=0) for c in range(2)]
        return [[[out[c][:, (i * MODES + m) * extent:(i * MODES + m + 1) * extent] for c in range(2)]
                 for m in modes] for i in range(len(fields))]

    lane = lax.broadcasted_iota(jnp.int32, (extent, extent), 1)

    def window(slot):
        r, c = scalars_ref[slot], scalars_ref[most + slot]
        shift = lax.rem(extent - c, extent)
        layers = []
        for layer in range(SLICES):
            parts = []
            for part in range(2):
                plane = (layer * 2 + part) * HALVES
                joined = jnp.where(lane >= c, obj[plane, pl.ds(r, extent), :], obj[plane + 1, pl.ds(r, extent), :])
                parts.append(pltpu.roll(joined, shift, 1))
            layers.append(parts)
        return layers

    def deposit(slot, layer, grad):
        r, c = scalars_ref[slot], scalars_ref[most + slot]
        for part in range(2):
            plane = (layer * 2 + part) * HALVES
            rolled = pltpu.roll(grad[part], lax.rem(c, extent), 1)
            acc[plane, pl.ds(r, extent), :] += jnp.where(lane >= c, rolled, 0.0)
            acc[plane + 1, pl.ds(r, extent), :] += jnp.where(lane >= c, 0.0, rolled)

    def measured(slot):
        return jnp.concatenate([patterns_ref[slot, pl.ds(k, extent // 2, stride=2), :] for k in range(2)], axis=0)

    def steps(slots):
        n = range(len(slots))
        field = [[probe[2 * m], probe[2 * m + 1]] for m in modes]
        objects = [window(slot) for slot in slots]
        state = right([[times(field[m], objects[i][0]) for m in modes] for i in n], 1, 0)
        yield
        entering = left(state, 1, 0)
        yield
        state = right([[times(entering[i][m], objects[i][1]) for m in modes] for i in n], 0, 0)
        yield
        state = left(state, 0, 0)
        yield
        weight = [2.0 * (sum(state[i][m][c] * state[i][m][c] for m in modes for c in range(2)) - measured(slots[i]))
                  for i in n]
        state = right([[[weight[i] * state[i][m][c] for c in range(2)] for m in modes] for i in n], 0, 1)
        yield
        state = left(state, 0, 1)
        yield
        for i in n:
            grad = conj_times(entering[i][0], state[i][0])
            for m in modes[1:]:
                grad = add(grad, conj_times(entering[i][m], state[i][m]))
            deposit(slots[i], 1, grad)
        state = right([[conj_times(objects[i][1], state[i][m]) for m in modes] for i in n], 1, 1)
        yield
        state = left(state, 1, 1)
        yield
        for i in n:
            grad = conj_times(field[0], state[i][0])
            for m in modes[1:]:
                grad = add(grad, conj_times(field[m], state[i][m]))
            deposit(slots[i], 0, grad)
        for m in modes:
            term = conj_times(objects[0][0], state[0][m])
            for i in n[1:]:
                term = add(term, conj_times(objects[i][0], state[i][m]))
            probe_acc[2 * m] += term[0]
            probe_acc[2 * m + 1] += term[1]

    def run(*sets):
        running = [steps(slots) for slots in sets]
        while running:
            running = [r for r in running if next(r, "done") is None]

    count = scalars_ref[2 * most]
    fours = lax.shift_right_logical(count, 2)

    def four(j, carry):
        run([4 * j, 4 * j + 1], [4 * j + 2, 4 * j + 3])
        return carry

    lax.fori_loop(0, fours, four, 0)

    @pl.when(lax.bitwise_and(count, 2) == 2)
    def _():
        run([4 * fours], [4 * fours + 1])

    @pl.when(lax.bitwise_and(count, 1) == 1)
    def _():
        run([count - 1])

    for layer in range(SLICES):
        for half in range(HALVES):
            for part in range(2):
                target = (layer * HALVES + half) * 2 + part
                plane = (layer * 2 + part) * HALVES + half
                own_out[pl.ds(target, tile_rows, stride=8), :] = acc[plane, :tile_rows]
                next_out[pl.ds(target, extent, stride=8), :] = acc[plane, tile_rows:]


def prepared(own, patterns):
    extent = patterns.shape[1]
    vmem = pl.BlockSpec(memory_space=pltpu.VMEM)
    parts = jnp.asarray(factors(extent))
    return pl.pallas_call(
        prepare,
        out_shape=(
            jax.ShapeDtypeStruct((8, own.shape[0] // 8, own.shape[1]), jnp.float32),
            jax.ShapeDtypeStruct(patterns.shape, jnp.float32),
            jax.ShapeDtypeStruct((8, 2 * extent, 2 * extent), jnp.bfloat16),
            jax.ShapeDtypeStruct((8, 2 * extent, 2 * extent), jnp.bfloat16),
        ),
        in_specs=[pl.BlockSpec(memory_space=pltpu.HBM)] * 3,
        out_specs=(vmem,) * 4,
        scratch_shapes=[
            pltpu.VMEM(own.shape, jnp.float32),
            pltpu.VMEM(parts.shape, jnp.float32),
            pltpu.SemaphoreType.DMA((3,)),
        ],
        compiler_params=pltpu.CompilerParams(vmem_limit_bytes=16 * 1024 * 1024),
        cost_estimate=pl.CostEstimate(flops=0, bytes_accessed=6 * 1024 * 1024, transcendentals=0),
    )(own, patterns, parts)


def terms(scalars, planes, low, high, near, far, patterns, mats):
    extent = patterns.shape[1]
    rows = planes.shape[1] + extent
    smem = pl.BlockSpec(memory_space=pltpu.SMEM)
    vmem = pl.BlockSpec(memory_space=pltpu.VMEM)
    return pl.pallas_call(
        kernel,
        out_shape=(
            jax.ShapeDtypeStruct((planes.shape[1] * 8, extent), jnp.float32),
            jax.ShapeDtypeStruct((extent * 8, extent), jnp.float32),
            jax.ShapeDtypeStruct((2 * MODES, extent, extent), jnp.float32),
        ),
        in_specs=[smem] + [vmem] * 8,
        out_specs=(vmem,) * 3,
        scratch_shapes=[
            pltpu.VMEM((8, rows, extent), jnp.float32),
            pltpu.VMEM((8, rows, extent), jnp.float32),
            pltpu.VMEM((2 * MODES, extent, extent), jnp.float32),
        ],
        compiler_params=pltpu.CompilerParams(vmem_limit_bytes=40 * 1024 * 1024),
    )(scalars, planes, low, high, near, far, patterns, *mats)


def placed(probe_grad, shape):
    vmem = pl.BlockSpec(memory_space=pltpu.VMEM)
    return pl.pallas_call(
        place,
        out_shape=(jax.ShapeDtypeStruct(shape, jnp.float32),) * 2,
        in_specs=[vmem],
        out_specs=(vmem,) * 2,
        compiler_params=pltpu.CompilerParams(vmem_limit_bytes=4 * 1024 * 1024),
    )(probe_grad)


def flat(block):
    rows, k, parts, columns = block.shape
    split_up = block.reshape(rows, k, parts, columns // 128, 128)
    return split_up.transpose(0, 1, 3, 2, 4).reshape(-1, 128)


def unflat(value, shape):
    rows, k, parts, columns = shape
    return value.reshape(rows, k, columns // 128, parts, 128).transpose(0, 1, 3, 2, 4).reshape(shape)


def partner(value, bits):
    return lax.ppermute(value, "tile", [(i, i ^ bits) for i in range(lax.axis_size("tile"))])


def halved(value):
    return value[:value.shape[0] // 2], value[value.shape[0] // 2:]


def places_on(value, distance):
    members = range(lax.axis_size("tile"))
    return lax.ppermute(value, "tile", [
        (i, i // GROUP_DEV * GROUP_DEV + (i + distance) % GROUP_DEV) for i in members])


def probe_share(probe_grad, shape):
    keep, send = placed(probe_grad, shape)
    blocks = jnp.split(keep + partner(send, 1), 4, axis=0)
    total = blocks[0] + sum(places_on(block, 4 * k) for k, block in enumerate(blocks) if k > 0)
    keep, send = halved(total)
    return keep + partner(send, 2)


def shards(object_slices, probe_field, patterns, row_offsets, col_offsets, counts):
    size = lax.axis_size("tile")
    down = [((i + 1) % size, i) for i in range(size)]
    own = flat(object_slices)
    low, high = halved(own)
    scalars = jnp.concatenate([row_offsets, col_offsets, counts])

    low = lax.ppermute(low, "tile", down)
    mine = flat(probe_field)
    quarter = mine
    for bits in (8, 4):
        quarter = jnp.concatenate([quarter, partner(quarter, bits)], axis=0)
    high, quarter, patterns, own = lax.optimization_barrier((high, quarter, patterns, own))
    near = jnp.concatenate([quarter, partner(quarter, 2)], axis=0)
    high = lax.ppermute(high, "tile", down)
    planes, patterns, *mats = prepared(own, patterns)
    near, planes, patterns, scalars, *mats = lax.optimization_barrier((near, planes, patterns, scalars, *mats))
    far = partner(near, 1)

    own_grad, back, probe_grad = terms(scalars, planes, low, high, near, far, patterns, mats)

    back = lax.ppermute(back, "tile", [(i, (i + 1) % size) for i in range(size)])
    probe_sum = lax.cond(
        counts[0] > 0,
        lambda grad: probe_share(grad, near.shape),
        lambda grad: jnp.zeros((near.shape[0] // 8, near.shape[1]), jnp.float32),
        probe_grad)
    object_grad = own_grad + back
    return unflat(object_grad, object_slices.shape), unflat(probe_sum, probe_field.shape)


def solution(mesh):
    in_specs = (
        P(("groups", "tile"), None, None, None),
        P(("groups", "tile"), None, None, None),
        P(("groups", "tile"), None, None),
        P(("groups", "tile")),
        P(("groups", "tile")),
        P(("groups", "tile")),
    )
    out_specs = (P(("groups", "tile"), None, None, None), P(("groups", "tile"), None, None, None))
    return jax.shard_map(shards, mesh=mesh, in_specs=in_specs, out_specs=out_specs, check_vma=False)
```

```python
import math

import jax
import jax.numpy as jnp
import numpy as np
from jax import lax
from jax.experimental import pallas as pl
from jax.experimental.pallas import tpu as pltpu
from jax.sharding import PartitionSpec as P

GROUP_DEV = 16
KAPPA = 4.0
MODES = 2
SLICES = 2
HALVES = 2
AHEAD = (0, 8, 4, 12, 2, 10, 6, 14)


def factors(extent):
    counter = np.arange(extent)
    half = extent // 2
    dft = np.exp(-2j * np.pi * (counter[:, None] * counter[None, :] % extent) / extent) / math.sqrt(extent)
    freq = ((counter + extent // 2) % extent - extent // 2) / extent
    prop = np.conj(dft) @ (np.exp(-1j * np.pi * KAPPA * freq**2)[:, None] * dft)
    whole = [part for matrix in (dft, prop) for part in (matrix.real, matrix.imag)]
    same, cross = prop[:half, :half], prop[:half, half:]
    even, odd = dft[0::2, :half], dft[1::2, :half]
    halves = [even, odd, np.conj(even.T), np.conj(odd.T),
              (same + cross) / 2, (same - cross) / 2, np.conj(same + cross) / 2, np.conj(same - cross) / 2]
    halves = [np.block([[m.real, -m.imag], [m.imag, m.real]]) for m in halves]
    return np.stack(whole + halves).astype(np.float32)


def split(value):
    high = value.astype(jnp.bfloat16)
    low = (value - high.astype(jnp.float32)).astype(jnp.bfloat16)
    return high, low


def prepare(own_ref, patterns_ref, factors_ref, planes_out, patterns_out, mats_out, half_out, own, parts, sems):
    copies = [pltpu.make_async_copy(source, target, sems.at[i]) for i, (source, target) in enumerate(
        ((factors_ref, parts), (own_ref, own), (patterns_ref, patterns_out)))]
    for copy in copies:
        copy.start()
    copies[0].wait()
    extent = parts.shape[1]
    for kind in range(2):
        real, imag = split(parts[2 * kind]), split(parts[2 * kind + 1])
        for conj in range(2):
            for k in range(2):
                mat = 4 * kind + 2 * conj + k
                upper, lower = (-imag[k], imag[k]) if conj else (imag[k], -imag[k])
                mats_out[mat, :extent, :extent] = real[k]
                mats_out[mat, :extent, extent:] = upper
                mats_out[mat, extent:, :extent] = lower
                mats_out[mat, extent:, extent:] = real[k]
    for k in range(half_out.shape[0]):
        high, low = split(parts[4 + k])
        half_out[k, :extent, :extent] = high
        half_out[k, :extent, extent:] = high
        half_out[k, extent:, :extent] = low
        half_out[k, extent:, extent:] = low
    copies[1].wait()
    rows = planes_out.shape[1]
    for layer in range(SLICES):
        for half in range(HALVES):
            for part in range(2):
                source = (layer * HALVES + half) * 2 + part
                plane = (layer * 2 + part) * HALVES + half
                planes_out[plane] = own[pl.ds(source, rows, stride=8), :]
    copies[2].wait()


def times(a, b):
    return [a[0] * b[0] - a[1] * b[1], a[0] * b[1] + a[1] * b[0]]


def conj_times(a, b):
    return [a[0] * b[0] + a[1] * b[1], a[0] * b[1] - a[1] * b[0]]


def add(a, b):
    return [a[0] + b[0], a[1] + b[1]]


def member_rows(member, order, share):
    return pl.ds(pl.multiple_of(lax.bitwise_xor(member, order) * share, share), share)


def place(probe_ref, keep_out, send_out):
    lanes, extent = probe_ref.shape[:2]
    share = extent // GROUP_DEV
    member = lax.rem(lax.axis_index("tile"), GROUP_DEV)
    for odd, ref in enumerate((keep_out, send_out)):
        for block in range(GROUP_DEV // 2):
            there = lax.bitwise_xor(lax.rem(member + block // 2 * 4, GROUP_DEV), 2 * (block % 2) + odd)
            for k in range(lanes):
                rows = pl.ds(block * share * lanes + k, share, stride=lanes)
                ref[rows, :] = probe_ref[k, pl.ds(pl.multiple_of(there * share, share), share), :]


def kernel(scalars_ref, own_ref, low_ref, high_ref, near_ref, far_ref, patterns_ref, mats_ref,
           half_ref, own_out, next_out, probe_acc, obj, acc, probe):
    most, extent = patterns_ref.shape[:2]
    share = extent // GROUP_DEV
    member = lax.rem(lax.axis_index("tile"), GROUP_DEV)
    tile_rows = own_ref.shape[1]
    middle = extent // 2
    lanes = 2 * MODES
    modes = range(MODES)

    for layer in range(SLICES):
        for half in range(HALVES):
            for part in range(2):
                source = (layer * HALVES + half) * 2 + part
                plane = (layer * 2 + part) * HALVES + half
                obj[plane, :tile_rows] = own_ref[plane]
                obj[plane, tile_rows:tile_rows + middle] = low_ref[pl.ds(source, middle, stride=8), :]
                obj[plane, tile_rows + middle:] = high_ref[pl.ds(source, extent - middle, stride=8), :]
    for odd, ref in enumerate((near_ref, far_ref)):
        for block, order in enumerate(AHEAD):
            for k in range(lanes):
                rows = pl.ds(block * share * lanes + k, share, stride=lanes)
                probe[k, member_rows(member, order + odd, share), :] = ref[rows, :]
    acc[...] = jnp.zeros(acc.shape, jnp.float32)
    probe_acc[...] = jnp.zeros(probe_acc.shape, jnp.float32)

    def right(fields, kind, conj):
        high_m, low_m = mats_ref[4 * kind + 2 * conj], mats_ref[4 * kind + 2 * conj + 1]
        rows = jnp.concatenate([jnp.concatenate(f[m], axis=1) for f in fields for m in modes], axis=0)
        high, low = split(rows)
        out = jnp.dot(jnp.concatenate([high, low, high], axis=1), jnp.concatenate([high_m, high_m, low_m], axis=0),
                      preferred_element_type=jnp.float32)
        return [[[out[(i * MODES + m) * extent:(i * MODES + m + 1) * extent, c * extent:(c + 1) * extent]
                  for c in range(2)] for m in modes] for i in range(len(fields))]

    def left(fields, kind, conj):
        middle = extent // 2
        cols = [jnp.concatenate([f[m][c] for f in fields for m in modes], axis=1) for c in range(2)]
        upper, lower = [c[:middle] for c in cols], [c[middle:] for c in cols]
        if kind == 1 or not conj:
            upper, lower = add(upper, lower), [u - v for u, v in zip(upper, lower)]
        halves = []
        for k, pieces in enumerate((upper, lower)):
            high, low = split(jnp.concatenate(pieces, axis=0))
            out = jnp.dot(half_ref[4 * kind + 2 * conj + k], jnp.concatenate([high, low], axis=0),
                          preferred_element_type=jnp.float32)
            out = out[:extent] + out[extent:]
            halves.append([out[:middle], out[middle:]])
        upper, lower = halves
        if kind == 1 or conj:
            upper, lower = add(upper, lower), [u - v for u, v in zip(upper, lower)]
        out = [jnp.concatenate([upper[c], lower[c]], axis=0) for c in range(2)]
        return [[[out[c][:, (i * MODES + m) * extent:(i * MODES + m + 1) * extent] for c in range(2)]
                 for m in modes] for i in range(len(fields))]

    lane = lax.broadcasted_iota(jnp.int32, (extent, extent), 1)

    def window(slot):
        r, c = scalars_ref[slot], scalars_ref[most + slot]
        shift = lax.rem(extent - c, extent)
        layers = []
        for layer in range(SLICES):
            parts = []
            for part in range(2):
                plane = (layer * 2 + part) * HALVES
                joined = jnp.where(lane >= c, obj[plane, pl.ds(r, extent), :], obj[plane + 1, pl.ds(r, extent), :])
                parts.append(pltpu.roll(joined, shift, 1))
            layers.append(parts)
        return layers

    def deposit(slot, layer, grad):
        r, c = scalars_ref[slot], scalars_ref[most + slot]
        for part in range(2):
            plane = (layer * 2 + part) * HALVES
            rolled = pltpu.roll(grad[part], lax.rem(c, extent), 1)
            acc[plane, pl.ds(r, extent), :] += jnp.where(lane >= c, rolled, 0.0)
            acc[plane + 1, pl.ds(r, extent), :] += jnp.where(lane >= c, 0.0, rolled)

    def measured(slot):
        return jnp.concatenate([patterns_ref[slot, pl.ds(k, extent // 2, stride=2), :] for k in range(2)], axis=0)

    def steps(slots):
        n = range(len(slots))
        field = [[probe[2 * m], probe[2 * m + 1]] for m in modes]
        objects = [window(slot) for slot in slots]
        state = right([[times(field[m], objects[i][0]) for m in modes] for i in n], 1, 0)
        yield
        entering = left(state, 1, 0)
        yield
        state = right([[times(entering[i][m], objects[i][1]) for m in modes] for i in n], 0, 0)
        yield
        state = left(state, 0, 0)
        yield
        weight = [2.0 * (sum(state[i][m][c] * state[i][m][c] for m in modes for c in range(2)) - measured(slots[i]))
                  for i in n]
        state = right([[[weight[i] * state[i][m][c] for c in range(2)] for m in modes] for i in n], 0, 1)
        yield
        state = left(state, 0, 1)
        yield
        for i in n:
            grad = conj_times(entering[i][0], state[i][0])
            for m in modes[1:]:
                grad = add(grad, conj_times(entering[i][m], state[i][m]))
            deposit(slots[i], 1, grad)
        state = right([[conj_times(objects[i][1], state[i][m]) for m in modes] for i in n], 1, 1)
        yield
        state = left(state, 1, 1)
        yield
        for i in n:
            grad = conj_times(field[0], state[i][0])
            for m in modes[1:]:
                grad = add(grad, conj_times(field[m], state[i][m]))
            deposit(slots[i], 0, grad)
        for m in modes:
            term = conj_times(objects[0][0], state[0][m])
            for i in n[1:]:
                term = add(term, conj_times(objects[i][0], state[i][m]))
            probe_acc[2 * m] += term[0]
            probe_acc[2 * m + 1] += term[1]

    def run(*sets):
        running = [steps(slots) for slots in sets]
        while running:
            running = [r for r in running if next(r, "done") is None]

    count = scalars_ref[2 * most]
    fours = lax.shift_right_logical(count, 2)

    def four(j, carry):
        run([4 * j, 4 * j + 1], [4 * j + 2, 4 * j + 3])
        return carry

    lax.fori_loop(0, fours, four, 0)

    @pl.when(lax.bitwise_and(count, 2) == 2)
    def _():
        run([4 * fours], [4 * fours + 1])

    @pl.when(lax.bitwise_and(count, 1) == 1)
    def _():
        run([count - 1])

    for layer in range(SLICES):
        for half in range(HALVES):
            for part in range(2):
                target = (layer * HALVES + half) * 2 + part
                plane = (layer * 2 + part) * HALVES + half
                own_out[pl.ds(target, tile_rows, stride=8), :] = acc[plane, :tile_rows]
                next_out[pl.ds(target, extent, stride=8), :] = acc[plane, tile_rows:]


def prepared(own, patterns):
    extent = patterns.shape[1]
    vmem = pl.BlockSpec(memory_space=pltpu.VMEM)
    parts = jnp.asarray(factors(extent))
    return pl.pallas_call(
        prepare,
        out_shape=(
            jax.ShapeDtypeStruct((8, own.shape[0] // 8, own.shape[1]), jnp.float32),
            jax.ShapeDtypeStruct(patterns.shape, jnp.float32),
            jax.ShapeDtypeStruct((8, 2 * extent, 2 * extent), jnp.bfloat16),
            jax.ShapeDtypeStruct((8, 2 * extent, 2 * extent), jnp.bfloat16),
        ),
        in_specs=[pl.BlockSpec(memory_space=pltpu.HBM)] * 3,
        out_specs=(vmem,) * 4,
        scratch_shapes=[
            pltpu.VMEM(own.shape, jnp.float32),
            pltpu.VMEM(parts.shape, jnp.float32),
            pltpu.SemaphoreType.DMA((3,)),
        ],
        compiler_params=pltpu.CompilerParams(vmem_limit_bytes=16 * 1024 * 1024),
        cost_estimate=pl.CostEstimate(flops=0, bytes_accessed=6 * 1024 * 1024, transcendentals=0),
    )(own, patterns, parts)


def terms(scalars, planes, low, high, near, far, patterns, mats):
    extent = patterns.shape[1]
    rows = planes.shape[1] + extent
    smem = pl.BlockSpec(memory_space=pltpu.SMEM)
    vmem = pl.BlockSpec(memory_space=pltpu.VMEM)
    return pl.pallas_call(
        kernel,
        out_shape=(
            jax.ShapeDtypeStruct((planes.shape[1] * 8, extent), jnp.float32),
            jax.ShapeDtypeStruct((extent * 8, extent), jnp.float32),
            jax.ShapeDtypeStruct((2 * MODES, extent, extent), jnp.float32),
        ),
        in_specs=[smem] + [vmem] * 8,
        out_specs=(vmem,) * 3,
        scratch_shapes=[
            pltpu.VMEM((8, rows, extent), jnp.float32),
            pltpu.VMEM((8, rows, extent), jnp.float32),
            pltpu.VMEM((2 * MODES, extent, extent), jnp.float32),
        ],
        compiler_params=pltpu.CompilerParams(vmem_limit_bytes=40 * 1024 * 1024),
    )(scalars, planes, low, high, near, far, patterns, *mats)


def placed(probe_grad, shape):
    vmem = pl.BlockSpec(memory_space=pltpu.VMEM)
    return pl.pallas_call(
        place,
        out_shape=(jax.ShapeDtypeStruct(shape, jnp.float32),) * 2,
        in_specs=[vmem],
        out_specs=(vmem,) * 2,
        compiler_params=pltpu.CompilerParams(vmem_limit_bytes=4 * 1024 * 1024),
    )(probe_grad)


def flat(block):
    rows, k, parts, columns = block.shape
    split_up = block.reshape(rows, k, parts, columns // 128, 128)
    return split_up.transpose(0, 1, 3, 2, 4).reshape(-1, 128)


def unflat(value, shape):
    rows, k, parts, columns = shape
    return value.reshape(rows, k, columns // 128, parts, 128).transpose(0, 1, 3, 2, 4).reshape(shape)


def partner(value, bits):
    return lax.ppermute(value, "tile", [(i, i ^ bits) for i in range(lax.axis_size("tile"))])


def halved(value):
    return value[:value.shape[0] // 2], value[value.shape[0] // 2:]


def places_on(value, distance):
    members = range(lax.axis_size("tile"))
    return lax.ppermute(value, "tile", [
        (i, i // GROUP_DEV * GROUP_DEV + (i + distance) % GROUP_DEV) for i in members])


def probe_share(probe_grad, shape):
    keep, send = placed(probe_grad, shape)
    blocks = jnp.split(keep + partner(send, 1), 4, axis=0)
    total = blocks[0] + sum(places_on(block, 4 * k) for k, block in enumerate(blocks) if k > 0)
    keep, send = halved(total)
    return keep + partner(send, 2)


def shards(object_slices, probe_field, patterns, row_offsets, col_offsets, counts):
    size = lax.axis_size("tile")
    down = [((i + 1) % size, i) for i in range(size)]
    own = flat(object_slices)
    low, high = halved(own)
    scalars = jnp.concatenate([row_offsets, col_offsets, counts])

    low, high, mine = lax.optimization_barrier((low, high, flat(probe_field)))
    low = lax.ppermute(low, "tile", down)
    quarter = jnp.concatenate([mine, partner(mine, 8), partner(mine, 4), partner(mine, 12)], axis=0)
    low, high, quarter, patterns, own = lax.optimization_barrier((low, high, quarter, patterns, own))
    near = jnp.concatenate([quarter, partner(quarter, 2)], axis=0)
    high = lax.ppermute(high, "tile", down)
    planes, patterns, *mats = prepared(own, patterns)
    near, planes, patterns, scalars, *mats = lax.optimization_barrier((near, planes, patterns, scalars, *mats))
    far = partner(near, 1)

    own_grad, back, probe_grad = terms(scalars, planes, low, high, near, far, patterns, mats)

    back = lax.ppermute(back, "tile", [(i, (i + 1) % size) for i in range(size)])
    probe_sum = lax.cond(
        counts[0] > 0,
        lambda grad: probe_share(grad, near.shape),
        lambda grad: jnp.zeros((near.shape[0] // 8, near.shape[1]), jnp.float32),
        probe_grad)
    object_grad = own_grad + back
    return unflat(object_grad, object_slices.shape), unflat(probe_sum, probe_field.shape)


def solution(mesh):
    in_specs = (
        P(("groups", "tile"), None, None, None),
        P(("groups", "tile"), None, None, None),
        P(("groups", "tile"), None, None),
        P(("groups", "tile")),
        P(("groups", "tile")),
        P(("groups", "tile")),
    )
    out_specs = (P(("groups", "tile"), None, None, None), P(("groups", "tile"), None, None, None))
    return jax.shard_map(shards, mesh=mesh, in_specs=in_specs, out_specs=out_specs, check_vma=False)
```

```python
import math

import jax
import jax.numpy as jnp
import numpy as np
from jax import lax
from jax.experimental import pallas as pl
from jax.experimental.pallas import tpu as pltpu
from jax.sharding import PartitionSpec as P

GROUP_DEV = 16
KAPPA = 4.0
MODES = 2
SLICES = 2
HALVES = 2
AHEAD = (0, 8, 4, 12, 2, 10, 6, 14)


def factors(extent):
    counter = np.arange(extent)
    half = extent // 2
    dft = np.exp(-2j * np.pi * (counter[:, None] * counter[None, :] % extent) / extent) / math.sqrt(extent)
    freq = ((counter + extent // 2) % extent - extent // 2) / extent
    prop = np.conj(dft) @ (np.exp(-1j * np.pi * KAPPA * freq**2)[:, None] * dft)
    whole = [part for matrix in (dft, prop) for part in (matrix.real, matrix.imag)]
    same, cross = prop[:half, :half], prop[:half, half:]
    even, odd = dft[0::2, :half], dft[1::2, :half]
    halves = [even, odd, np.conj(even.T), np.conj(odd.T),
              (same + cross) / 2, (same - cross) / 2, np.conj(same + cross) / 2, np.conj(same - cross) / 2]
    halves = [np.block([[m.real, -m.imag], [m.imag, m.real]]) for m in halves]
    return np.stack(whole + halves).astype(np.float32)


def split(value):
    high = value.astype(jnp.bfloat16)
    low = (value - high.astype(jnp.float32)).astype(jnp.bfloat16)
    return high, low


def prepare(own_ref, patterns_ref, factors_ref, planes_out, patterns_out, mats_out, half_out, own, parts, sems):
    copies = [pltpu.make_async_copy(source, target, sems.at[i]) for i, (source, target) in enumerate(
        ((factors_ref, parts), (own_ref, own), (patterns_ref, patterns_out)))]
    for copy in copies:
        copy.start()
    copies[0].wait()
    extent = parts.shape[1]
    for kind in range(2):
        real, imag = split(parts[2 * kind]), split(parts[2 * kind + 1])
        for conj in range(2):
            for k in range(2):
                mat = 4 * kind + 2 * conj + k
                upper, lower = (-imag[k], imag[k]) if conj else (imag[k], -imag[k])
                mats_out[mat, :extent, :extent] = real[k]
                mats_out[mat, :extent, extent:] = upper
                mats_out[mat, extent:, :extent] = lower
                mats_out[mat, extent:, extent:] = real[k]
    for k in range(half_out.shape[0]):
        high, low = split(parts[4 + k])
        half_out[k, :extent, :extent] = high
        half_out[k, :extent, extent:] = high
        half_out[k, extent:, :extent] = low
        half_out[k, extent:, extent:] = low
    copies[1].wait()
    rows = planes_out.shape[1]
    for layer in range(SLICES):
        for half in range(HALVES):
            for part in range(2):
                source = (layer * HALVES + half) * 2 + part
                plane = (layer * 2 + part) * HALVES + half
                planes_out[plane] = own[pl.ds(source, rows, stride=8), :]
    copies[2].wait()


def times(a, b):
    return [a[0] * b[0] - a[1] * b[1], a[0] * b[1] + a[1] * b[0]]


def conj_times(a, b):
    return [a[0] * b[0] + a[1] * b[1], a[0] * b[1] - a[1] * b[0]]


def add(a, b):
    return [a[0] + b[0], a[1] + b[1]]


def member_rows(member, order, share):
    return pl.ds(pl.multiple_of(lax.bitwise_xor(member, order) * share, share), share)


def place(probe_ref, keep_out, send_out):
    lanes, extent = probe_ref.shape[:2]
    share = extent // GROUP_DEV
    member = lax.rem(lax.axis_index("tile"), GROUP_DEV)
    for odd, ref in enumerate((keep_out, send_out)):
        for block in range(GROUP_DEV // 2):
            there = lax.bitwise_xor(lax.rem(member + block // 2 * 4, GROUP_DEV), 2 * (block % 2) + odd)
            for k in range(lanes):
                rows = pl.ds(block * share * lanes + k, share, stride=lanes)
                ref[rows, :] = probe_ref[k, pl.ds(pl.multiple_of(there * share, share), share), :]


def kernel(scalars_ref, own_ref, low_ref, high_ref, near_ref, far_ref, patterns_ref, mats_ref,
           half_ref, own_out, next_out, probe_acc, obj, acc, probe):
    most, extent = patterns_ref.shape[:2]
    share = extent // GROUP_DEV
    member = lax.rem(lax.axis_index("tile"), GROUP_DEV)
    tile_rows = own_ref.shape[1]
    middle = extent // 2
    lanes = 2 * MODES
    modes = range(MODES)

    for layer in range(SLICES):
        for half in range(HALVES):
            for part in range(2):
                source = (layer * HALVES + half) * 2 + part
                plane = (layer * 2 + part) * HALVES + half
                obj[plane, :tile_rows] = own_ref[plane]
                obj[plane, tile_rows:tile_rows + middle] = low_ref[pl.ds(source, middle, stride=8), :]
                obj[plane, tile_rows + middle:] = high_ref[pl.ds(source, extent - middle, stride=8), :]
    for odd, ref in enumerate((near_ref, far_ref)):
        for block, order in enumerate(AHEAD):
            for k in range(lanes):
                rows = pl.ds(block * share * lanes + k, share, stride=lanes)
                probe[k, member_rows(member, order + odd, share), :] = ref[rows, :]
    acc[...] = jnp.zeros(acc.shape, jnp.float32)
    probe_acc[...] = jnp.zeros(probe_acc.shape, jnp.float32)

    def right(fields, kind, conj):
        high_m, low_m = mats_ref[4 * kind + 2 * conj], mats_ref[4 * kind + 2 * conj + 1]
        rows = jnp.concatenate([jnp.concatenate(f[m], axis=1) for f in fields for m in modes], axis=0)
        high, low = split(rows)
        out = jnp.dot(jnp.concatenate([high, low, high], axis=1), jnp.concatenate([high_m, high_m, low_m], axis=0),
                      preferred_element_type=jnp.float32)
        return [[[out[(i * MODES + m) * extent:(i * MODES + m + 1) * extent, c * extent:(c + 1) * extent]
                  for c in range(2)] for m in modes] for i in range(len(fields))]

    def left(fields, kind, conj):
        middle = extent // 2
        cols = [jnp.concatenate([f[m][c] for f in fields for m in modes], axis=1) for c in range(2)]
        upper, lower = [c[:middle] for c in cols], [c[middle:] for c in cols]
        if kind == 1 or not conj:
            upper, lower = add(upper, lower), [u - v for u, v in zip(upper, lower)]
        halves = []
        for k, pieces in enumerate((upper, lower)):
            high, low = split(jnp.concatenate(pieces, axis=0))
            out = jnp.dot(half_ref[4 * kind + 2 * conj + k], jnp.concatenate([high, low], axis=0),
                          preferred_element_type=jnp.float32)
            out = out[:extent] + out[extent:]
            halves.append([out[:middle], out[middle:]])
        upper, lower = halves
        if kind == 1 or conj:
            upper, lower = add(upper, lower), [u - v for u, v in zip(upper, lower)]
        out = [jnp.concatenate([upper[c], lower[c]], axis=0) for c in range(2)]
        return [[[out[c][:, (i * MODES + m) * extent:(i * MODES + m + 1) * extent] for c in range(2)]
                 for m in modes] for i in range(len(fields))]

    lane = lax.broadcasted_iota(jnp.int32, (extent, extent), 1)

    def window(slot):
        r, c = scalars_ref[slot], scalars_ref[most + slot]
        shift = lax.rem(extent - c, extent)
        layers = []
        for layer in range(SLICES):
            parts = []
            for part in range(2):
                plane = (layer * 2 + part) * HALVES
                joined = jnp.where(lane >= c, obj[plane, pl.ds(r, extent), :], obj[plane + 1, pl.ds(r, extent), :])
                parts.append(pltpu.roll(joined, shift, 1))
            layers.append(parts)
        return layers

    def deposit(slot, layer, grad):
        r, c = scalars_ref[slot], scalars_ref[most + slot]
        for part in range(2):
            plane = (layer * 2 + part) * HALVES
            rolled = pltpu.roll(grad[part], lax.rem(c, extent), 1)
            acc[plane, pl.ds(r, extent), :] += jnp.where(lane >= c, rolled, 0.0)
            acc[plane + 1, pl.ds(r, extent), :] += jnp.where(lane >= c, 0.0, rolled)

    def measured(slot):
        return jnp.concatenate([patterns_ref[slot, pl.ds(k, extent // 2, stride=2), :] for k in range(2)], axis=0)

    def steps(slots):
        n = range(len(slots))
        field = [[probe[2 * m], probe[2 * m + 1]] for m in modes]
        objects = [window(slot) for slot in slots]
        state = right([[times(field[m], objects[i][0]) for m in modes] for i in n], 1, 0)
        yield
        entering = left(state, 1, 0)
        yield
        state = right([[times(entering[i][m], objects[i][1]) for m in modes] for i in n], 0, 0)
        yield
        state = left(state, 0, 0)
        yield
        weight = [2.0 * (sum(state[i][m][c] * state[i][m][c] for m in modes for c in range(2)) - measured(slots[i]))
                  for i in n]
        state = right([[[weight[i] * state[i][m][c] for c in range(2)] for m in modes] for i in n], 0, 1)
        yield
        state = left(state, 0, 1)
        yield
        for i in n:
            grad = conj_times(entering[i][0], state[i][0])
            for m in modes[1:]:
                grad = add(grad, conj_times(entering[i][m], state[i][m]))
            deposit(slots[i], 1, grad)
        state = right([[conj_times(objects[i][1], state[i][m]) for m in modes] for i in n], 1, 1)
        yield
        state = left(state, 1, 1)
        yield
        for i in n:
            grad = conj_times(field[0], state[i][0])
            for m in modes[1:]:
                grad = add(grad, conj_times(field[m], state[i][m]))
            deposit(slots[i], 0, grad)
        for m in modes:
            term = conj_times(objects[0][0], state[0][m])
            for i in n[1:]:
                term = add(term, conj_times(objects[i][0], state[i][m]))
            probe_acc[2 * m] += term[0]
            probe_acc[2 * m + 1] += term[1]

    def run(*sets):
        running = [steps(slots) for slots in sets]
        while running:
            running = [r for r in running if next(r, "done") is None]

    count = scalars_ref[2 * most]
    fours = lax.shift_right_logical(count, 2)

    def four(j, carry):
        run([4 * j, 4 * j + 1], [4 * j + 2, 4 * j + 3])
        return carry

    lax.fori_loop(0, fours, four, 0)

    @pl.when(lax.bitwise_and(count, 2) == 2)
    def _():
        run([4 * fours], [4 * fours + 1])

    @pl.when(lax.bitwise_and(count, 1) == 1)
    def _():
        run([count - 1])

    for layer in range(SLICES):
        for half in range(HALVES):
            for part in range(2):
                target = (layer * HALVES + half) * 2 + part
                plane = (layer * 2 + part) * HALVES + half
                own_out[pl.ds(target, tile_rows, stride=8), :] = acc[plane, :tile_rows]
                next_out[pl.ds(target, extent, stride=8), :] = acc[plane, tile_rows:]


def prepared(own, patterns):
    extent = patterns.shape[1]
    vmem = pl.BlockSpec(memory_space=pltpu.VMEM)
    parts = jnp.asarray(factors(extent))
    return pl.pallas_call(
        prepare,
        out_shape=(
            jax.ShapeDtypeStruct((8, own.shape[0] // 8, own.shape[1]), jnp.float32),
            jax.ShapeDtypeStruct(patterns.shape, jnp.float32),
            jax.ShapeDtypeStruct((8, 2 * extent, 2 * extent), jnp.bfloat16),
            jax.ShapeDtypeStruct((8, 2 * extent, 2 * extent), jnp.bfloat16),
        ),
        in_specs=[pl.BlockSpec(memory_space=pltpu.HBM)] * 3,
        out_specs=(vmem,) * 4,
        scratch_shapes=[
            pltpu.VMEM(own.shape, jnp.float32),
            pltpu.VMEM(parts.shape, jnp.float32),
            pltpu.SemaphoreType.DMA((3,)),
        ],
        compiler_params=pltpu.CompilerParams(vmem_limit_bytes=16 * 1024 * 1024),
        cost_estimate=pl.CostEstimate(flops=0, bytes_accessed=6 * 1024 * 1024, transcendentals=0),
    )(own, patterns, parts)


def terms(scalars, planes, low, high, near, far, patterns, mats):
    extent = patterns.shape[1]
    rows = planes.shape[1] + extent
    smem = pl.BlockSpec(memory_space=pltpu.SMEM)
    vmem = pl.BlockSpec(memory_space=pltpu.VMEM)
    return pl.pallas_call(
        kernel,
        out_shape=(
            jax.ShapeDtypeStruct((planes.shape[1] * 8, extent), jnp.float32),
            jax.ShapeDtypeStruct((extent * 8, extent), jnp.float32),
            jax.ShapeDtypeStruct((2 * MODES, extent, extent), jnp.float32),
        ),
        in_specs=[smem] + [vmem] * 8,
        out_specs=(vmem,) * 3,
        scratch_shapes=[
            pltpu.VMEM((8, rows, extent), jnp.float32),
            pltpu.VMEM((8, rows, extent), jnp.float32),
            pltpu.VMEM((2 * MODES, extent, extent), jnp.float32),
        ],
        compiler_params=pltpu.CompilerParams(vmem_limit_bytes=40 * 1024 * 1024),
    )(scalars, planes, low, high, near, far, patterns, *mats)


def placed(probe_grad, shape):
    vmem = pl.BlockSpec(memory_space=pltpu.VMEM)
    return pl.pallas_call(
        place,
        out_shape=(jax.ShapeDtypeStruct(shape, jnp.float32),) * 2,
        in_specs=[vmem],
        out_specs=(vmem,) * 2,
        compiler_params=pltpu.CompilerParams(vmem_limit_bytes=4 * 1024 * 1024),
    )(probe_grad)


def flat(block):
    rows, k, parts, columns = block.shape
    split_up = block.reshape(rows, k, parts, columns // 128, 128)
    return split_up.transpose(0, 1, 3, 2, 4).reshape(-1, 128)


def unflat(value, shape):
    rows, k, parts, columns = shape
    return value.reshape(rows, k, columns // 128, parts, 128).transpose(0, 1, 3, 2, 4).reshape(shape)


def partner(value, bits):
    return lax.ppermute(value, "tile", [(i, i ^ bits) for i in range(lax.axis_size("tile"))])


def halved(value):
    return value[:value.shape[0] // 2], value[value.shape[0] // 2:]


def places_on(value, distance):
    members = range(lax.axis_size("tile"))
    return lax.ppermute(value, "tile", [
        (i, i // GROUP_DEV * GROUP_DEV + (i + distance) % GROUP_DEV) for i in members])


def probe_share(probe_grad, shape):
    keep, send = placed(probe_grad, shape)
    blocks = jnp.split(keep + partner(send, 1), 4, axis=0)
    total = blocks[0] + sum(places_on(block, 4 * k) for k, block in enumerate(blocks) if k > 0)
    keep, send = halved(total)
    return keep + partner(send, 2)


def shards(object_slices, probe_field, patterns, row_offsets, col_offsets, counts):
    size = lax.axis_size("tile")
    down = [((i + 1) % size, i) for i in range(size)]
    own = flat(object_slices)
    low, high = halved(own)
    scalars = jnp.concatenate([row_offsets, col_offsets, counts])

    low, high, mine = lax.optimization_barrier((low, high, flat(probe_field)))
    low = lax.ppermute(low, "tile", down)
    quarter = mine
    for bits in (8, 4):
        quarter = jnp.concatenate([quarter, partner(quarter, bits)], axis=0)
    planes, patterns, *mats = prepared(own, patterns)
    low, high, quarter, planes, patterns, scalars, *mats = lax.optimization_barrier(
        (low, high, quarter, planes, patterns, scalars, *mats))
    near = jnp.concatenate([quarter, partner(quarter, 2)], axis=0)
    high = lax.ppermute(high, "tile", down)
    far = partner(near, 1)

    own_grad, back, probe_grad = terms(scalars, planes, low, high, near, far, patterns, mats)

    back = lax.ppermute(back, "tile", [(i, (i + 1) % size) for i in range(size)])
    probe_sum = lax.cond(
        counts[0] > 0,
        lambda grad: probe_share(grad, near.shape),
        lambda grad: jnp.zeros((near.shape[0] // 8, near.shape[1]), jnp.float32),
        probe_grad)
    object_grad = own_grad + back
    return unflat(object_grad, object_slices.shape), unflat(probe_sum, probe_field.shape)


def solution(mesh):
    in_specs = (
        P(("groups", "tile"), None, None, None),
        P(("groups", "tile"), None, None, None),
        P(("groups", "tile"), None, None),
        P(("groups", "tile")),
        P(("groups", "tile")),
        P(("groups", "tile")),
    )
    out_specs = (P(("groups", "tile"), None, None, None), P(("groups", "tile"), None, None, None))
    return jax.shard_map(shards, mesh=mesh, in_specs=in_specs, out_specs=out_specs, check_vma=False)
```

```python
import math

import jax
import jax.numpy as jnp
import numpy as np
from jax import lax
from jax.experimental import pallas as pl
from jax.experimental.pallas import tpu as pltpu
from jax.sharding import PartitionSpec as P

GROUP_DEV = 16
KAPPA = 4.0
MODES = 2
SLICES = 2
HALVES = 2
AHEAD = (0, 8, 4, 12, 2, 10, 6, 14)


def factors(extent):
    counter = np.arange(extent)
    half = extent // 2
    dft = np.exp(-2j * np.pi * (counter[:, None] * counter[None, :] % extent) / extent) / math.sqrt(extent)
    freq = ((counter + extent // 2) % extent - extent // 2) / extent
    prop = np.conj(dft) @ (np.exp(-1j * np.pi * KAPPA * freq**2)[:, None] * dft)
    whole = [part for matrix in (dft, prop) for part in (matrix.real, matrix.imag)]
    same, cross = prop[:half, :half], prop[:half, half:]
    even, odd = dft[0::2, :half], dft[1::2, :half]
    halves = [even, odd, np.conj(even.T), np.conj(odd.T),
              (same + cross) / 2, (same - cross) / 2, np.conj(same + cross) / 2, np.conj(same - cross) / 2]
    halves = [np.block([[m.real, -m.imag], [m.imag, m.real]]) for m in halves]
    return np.stack(whole + halves).astype(np.float32)


def split(value):
    high = value.astype(jnp.bfloat16)
    low = (value - high.astype(jnp.float32)).astype(jnp.bfloat16)
    return high, low


def prepare(own_ref, patterns_ref, factors_ref, planes_out, patterns_out, mats_out, half_out, own, parts, sems):
    copies = [pltpu.make_async_copy(source, target, sems.at[i]) for i, (source, target) in enumerate(
        ((factors_ref, parts), (own_ref, own), (patterns_ref, patterns_out)))]
    for copy in copies:
        copy.start()
    copies[0].wait()
    extent = parts.shape[1]
    for kind in range(2):
        real, imag = split(parts[2 * kind]), split(parts[2 * kind + 1])
        for conj in range(2):
            for k in range(2):
                mat = 4 * kind + 2 * conj + k
                upper, lower = (-imag[k], imag[k]) if conj else (imag[k], -imag[k])
                mats_out[mat, :extent, :extent] = real[k]
                mats_out[mat, :extent, extent:] = upper
                mats_out[mat, extent:, :extent] = lower
                mats_out[mat, extent:, extent:] = real[k]
    for k in range(half_out.shape[0]):
        high, low = split(parts[4 + k])
        half_out[k, :extent, :extent] = high
        half_out[k, :extent, extent:] = high
        half_out[k, extent:, :extent] = low
        half_out[k, extent:, extent:] = low
    copies[1].wait()
    rows = planes_out.shape[1]
    for layer in range(SLICES):
        for half in range(HALVES):
            for part in range(2):
                source = (layer * HALVES + half) * 2 + part
                plane = (layer * 2 + part) * HALVES + half
                planes_out[plane] = own[pl.ds(source, rows, stride=8), :]
    copies[2].wait()


def times(a, b):
    return [a[0] * b[0] - a[1] * b[1], a[0] * b[1] + a[1] * b[0]]


def conj_times(a, b):
    return [a[0] * b[0] + a[1] * b[1], a[0] * b[1] - a[1] * b[0]]


def add(a, b):
    return [a[0] + b[0], a[1] + b[1]]


def member_rows(member, order, share):
    return pl.ds(pl.multiple_of(lax.bitwise_xor(member, order) * share, share), share)


def place(probe_ref, keep_out, send_out):
    lanes, extent = probe_ref.shape[:2]
    share = extent // GROUP_DEV
    member = lax.rem(lax.axis_index("tile"), GROUP_DEV)
    for odd, ref in enumerate((keep_out, send_out)):
        for block in range(GROUP_DEV // 2):
            there = lax.bitwise_xor(lax.rem(member + block // 2 * 4, GROUP_DEV), 2 * (block % 2) + odd)
            for k in range(lanes):
                rows = pl.ds(block * share * lanes + k, share, stride=lanes)
                ref[rows, :] = probe_ref[k, pl.ds(pl.multiple_of(there * share, share), share), :]


def kernel(scalars_ref, own_ref, low_ref, high_ref, near_ref, far_ref, patterns_ref, mats_ref,
           half_ref, own_out, next_out, probe_acc, obj, acc, probe):
    most, extent = patterns_ref.shape[:2]
    share = extent // GROUP_DEV
    member = lax.rem(lax.axis_index("tile"), GROUP_DEV)
    tile_rows = own_ref.shape[1]
    middle = extent // 2
    lanes = 2 * MODES
    modes = range(MODES)

    for layer in range(SLICES):
        for half in range(HALVES):
            for part in range(2):
                source = (layer * HALVES + half) * 2 + part
                plane = (layer * 2 + part) * HALVES + half
                obj[plane, :tile_rows] = own_ref[plane]
                obj[plane, tile_rows:tile_rows + middle] = low_ref[pl.ds(source, middle, stride=8), :]
                obj[plane, tile_rows + middle:] = high_ref[pl.ds(source, extent - middle, stride=8), :]
    for odd, ref in enumerate((near_ref, far_ref)):
        for block, order in enumerate(AHEAD):
            for k in range(lanes):
                rows = pl.ds(block * share * lanes + k, share, stride=lanes)
                probe[k, member_rows(member, order + odd, share), :] = ref[rows, :]
    acc[...] = jnp.zeros(acc.shape, jnp.float32)
    probe_acc[...] = jnp.zeros(probe_acc.shape, jnp.float32)

    def right(fields, kind, conj):
        high_m, low_m = mats_ref[4 * kind + 2 * conj], mats_ref[4 * kind + 2 * conj + 1]
        rows = jnp.concatenate([jnp.concatenate(f[m], axis=1) for f in fields for m in modes], axis=0)
        high, low = split(rows)
        out = jnp.dot(jnp.concatenate([high, low, high], axis=1), jnp.concatenate([high_m, high_m, low_m], axis=0),
                      preferred_element_type=jnp.float32)
        return [[[out[(i * MODES + m) * extent:(i * MODES + m + 1) * extent, c * extent:(c + 1) * extent]
                  for c in range(2)] for m in modes] for i in range(len(fields))]

    def left(fields, kind, conj):
        middle = extent // 2
        cols = [jnp.concatenate([f[m][c] for f in fields for m in modes], axis=1) for c in range(2)]
        upper, lower = [c[:middle] for c in cols], [c[middle:] for c in cols]
        if kind == 1 or not conj:
            upper, lower = add(upper, lower), [u - v for u, v in zip(upper, lower)]
        halves = []
        for k, pieces in enumerate((upper, lower)):
            high, low = split(jnp.concatenate(pieces, axis=0))
            out = jnp.dot(half_ref[4 * kind + 2 * conj + k], jnp.concatenate([high, low], axis=0),
                          preferred_element_type=jnp.float32)
            out = out[:extent] + out[extent:]
            halves.append([out[:middle], out[middle:]])
        upper, lower = halves
        if kind == 1 or conj:
            upper, lower = add(upper, lower), [u - v for u, v in zip(upper, lower)]
        out = [jnp.concatenate([upper[c], lower[c]], axis=0) for c in range(2)]
        return [[[out[c][:, (i * MODES + m) * extent:(i * MODES + m + 1) * extent] for c in range(2)]
                 for m in modes] for i in range(len(fields))]

    lane = lax.broadcasted_iota(jnp.int32, (extent, extent), 1)

    def window(slot):
        r, c = scalars_ref[slot], scalars_ref[most + slot]
        shift = lax.rem(extent - c, extent)
        layers = []
        for layer in range(SLICES):
            parts = []
            for part in range(2):
                plane = (layer * 2 + part) * HALVES
                joined = jnp.where(lane >= c, obj[plane, pl.ds(r, extent), :], obj[plane + 1, pl.ds(r, extent), :])
                parts.append(pltpu.roll(joined, shift, 1))
            layers.append(parts)
        return layers

    def deposit(slot, layer, grad):
        r, c = scalars_ref[slot], scalars_ref[most + slot]
        for part in range(2):
            plane = (layer * 2 + part) * HALVES
            rolled = pltpu.roll(grad[part], lax.rem(c, extent), 1)
            acc[plane, pl.ds(r, extent), :] += jnp.where(lane >= c, rolled, 0.0)
            acc[plane + 1, pl.ds(r, extent), :] += jnp.where(lane >= c, 0.0, rolled)

    def measured(slot):
        return jnp.concatenate([patterns_ref[slot, pl.ds(k, extent // 2, stride=2), :] for k in range(2)], axis=0)

    def steps(slots):
        n = range(len(slots))
        field = [[probe[2 * m], probe[2 * m + 1]] for m in modes]
        objects = [window(slot) for slot in slots]
        state = right([[times(field[m], objects[i][0]) for m in modes] for i in n], 1, 0)
        yield
        entering = left(state, 1, 0)
        yield
        state = right([[times(entering[i][m], objects[i][1]) for m in modes] for i in n], 0, 0)
        yield
        state = left(state, 0, 0)
        yield
        weight = [2.0 * (sum(state[i][m][c] * state[i][m][c] for m in modes for c in range(2)) - measured(slots[i]))
                  for i in n]
        state = right([[[weight[i] * state[i][m][c] for c in range(2)] for m in modes] for i in n], 0, 1)
        yield
        state = left(state, 0, 1)
        yield
        for i in n:
            grad = conj_times(entering[i][0], state[i][0])
            for m in modes[1:]:
                grad = add(grad, conj_times(entering[i][m], state[i][m]))
            deposit(slots[i], 1, grad)
        state = right([[conj_times(objects[i][1], state[i][m]) for m in modes] for i in n], 1, 1)
        yield
        state = left(state, 1, 1)
        yield
        for i in n:
            grad = conj_times(field[0], state[i][0])
            for m in modes[1:]:
                grad = add(grad, conj_times(field[m], state[i][m]))
            deposit(slots[i], 0, grad)
        for m in modes:
            term = conj_times(objects[0][0], state[0][m])
            for i in n[1:]:
                term = add(term, conj_times(objects[i][0], state[i][m]))
            probe_acc[2 * m] += term[0]
            probe_acc[2 * m + 1] += term[1]

    def run(*sets):
        running = [steps(slots) for slots in sets]
        while running:
            running = [r for r in running if next(r, "done") is None]

    count = scalars_ref[2 * most]
    eights = lax.shift_right_logical(count, 3)
    fours = lax.shift_right_logical(count, 2)

    def eight(j, carry):
        run(*([8 * j + k, 8 * j + k + 1] for k in range(0, 8, 2)))
        return carry

    def four(j, carry):
        run([4 * j, 4 * j + 1], [4 * j + 2, 4 * j + 3])
        return carry

    lax.fori_loop(0, eights, eight, 0)
    lax.fori_loop(2 * eights, fours, four, 0)

    @pl.when(lax.bitwise_and(count, 2) == 2)
    def _():
        run([4 * fours], [4 * fours + 1])

    @pl.when(lax.bitwise_and(count, 1) == 1)
    def _():
        run([count - 1])

    for layer in range(SLICES):
        for half in range(HALVES):
            for part in range(2):
                target = (layer * HALVES + half) * 2 + part
                plane = (layer * 2 + part) * HALVES + half
                own_out[pl.ds(target, tile_rows, stride=8), :] = acc[plane, :tile_rows]
                next_out[pl.ds(target, extent, stride=8), :] = acc[plane, tile_rows:]


def prepared(own, patterns):
    extent = patterns.shape[1]
    vmem = pl.BlockSpec(memory_space=pltpu.VMEM)
    parts = jnp.asarray(factors(extent))
    return pl.pallas_call(
        prepare,
        out_shape=(
            jax.ShapeDtypeStruct((8, own.shape[0] // 8, own.shape[1]), jnp.float32),
            jax.ShapeDtypeStruct(patterns.shape, jnp.float32),
            jax.ShapeDtypeStruct((8, 2 * extent, 2 * extent), jnp.bfloat16),
            jax.ShapeDtypeStruct((8, 2 * extent, 2 * extent), jnp.bfloat16),
        ),
        in_specs=[pl.BlockSpec(memory_space=pltpu.HBM)] * 3,
        out_specs=(vmem,) * 4,
        scratch_shapes=[
            pltpu.VMEM(own.shape, jnp.float32),
            pltpu.VMEM(parts.shape, jnp.float32),
            pltpu.SemaphoreType.DMA((3,)),
        ],
        compiler_params=pltpu.CompilerParams(vmem_limit_bytes=16 * 1024 * 1024),
        cost_estimate=pl.CostEstimate(flops=0, bytes_accessed=6 * 1024 * 1024, transcendentals=0),
    )(own, patterns, parts)


def terms(scalars, planes, low, high, near, far, patterns, mats):
    extent = patterns.shape[1]
    rows = planes.shape[1] + extent
    smem = pl.BlockSpec(memory_space=pltpu.SMEM)
    vmem = pl.BlockSpec(memory_space=pltpu.VMEM)
    return pl.pallas_call(
        kernel,
        out_shape=(
            jax.ShapeDtypeStruct((planes.shape[1] * 8, extent), jnp.float32),
            jax.ShapeDtypeStruct((extent * 8, extent), jnp.float32),
            jax.ShapeDtypeStruct((2 * MODES, extent, extent), jnp.float32),
        ),
        in_specs=[smem] + [vmem] * 8,
        out_specs=(vmem,) * 3,
        scratch_shapes=[
            pltpu.VMEM((8, rows, extent), jnp.float32),
            pltpu.VMEM((8, rows, extent), jnp.float32),
            pltpu.VMEM((2 * MODES, extent, extent), jnp.float32),
        ],
        compiler_params=pltpu.CompilerParams(vmem_limit_bytes=40 * 1024 * 1024),
    )(scalars, planes, low, high, near, far, patterns, *mats)


def placed(probe_grad, shape):
    vmem = pl.BlockSpec(memory_space=pltpu.VMEM)
    return pl.pallas_call(
        place,
        out_shape=(jax.ShapeDtypeStruct(shape, jnp.float32),) * 2,
        in_specs=[vmem],
        out_specs=(vmem,) * 2,
        compiler_params=pltpu.CompilerParams(vmem_limit_bytes=4 * 1024 * 1024),
    )(probe_grad)


def flat(block):
    rows, k, parts, columns = block.shape
    split_up = block.reshape(rows, k, parts, columns // 128, 128)
    return split_up.transpose(0, 1, 3, 2, 4).reshape(-1, 128)


def unflat(value, shape):
    rows, k, parts, columns = shape
    return value.reshape(rows, k, columns // 128, parts, 128).transpose(0, 1, 3, 2, 4).reshape(shape)


def partner(value, bits):
    return lax.ppermute(value, "tile", [(i, i ^ bits) for i in range(lax.axis_size("tile"))])


def halved(value):
    return value[:value.shape[0] // 2], value[value.shape[0] // 2:]


def places_on(value, distance):
    members = range(lax.axis_size("tile"))
    return lax.ppermute(value, "tile", [
        (i, i // GROUP_DEV * GROUP_DEV + (i + distance) % GROUP_DEV) for i in members])


def probe_share(probe_grad, shape):
    keep, send = placed(probe_grad, shape)
    blocks = jnp.split(keep + partner(send, 1), 4, axis=0)
    total = blocks[0] + sum(places_on(block, 4 * k) for k, block in enumerate(blocks) if k > 0)
    keep, send = halved(total)
    return keep + partner(send, 2)


def shards(object_slices, probe_field, patterns, row_offsets, col_offsets, counts):
    size = lax.axis_size("tile")
    down = [((i + 1) % size, i) for i in range(size)]
    own = flat(object_slices)
    low, high = halved(own)
    scalars = jnp.concatenate([row_offsets, col_offsets, counts])

    low, high, mine = lax.optimization_barrier((low, high, flat(probe_field)))
    low = lax.ppermute(low, "tile", down)
    quarter = jnp.concatenate([mine, partner(mine, 8), partner(mine, 4), partner(mine, 12)], axis=0)
    low, high, quarter, patterns, own = lax.optimization_barrier((low, high, quarter, patterns, own))
    near = jnp.concatenate([quarter, partner(quarter, 2)], axis=0)
    high = lax.ppermute(high, "tile", down)
    planes, patterns, *mats = prepared(own, patterns)
    near, planes, patterns, scalars, *mats = lax.optimization_barrier((near, planes, patterns, scalars, *mats))
    far = partner(near, 1)

    own_grad, back, probe_grad = terms(scalars, planes, low, high, near, far, patterns, mats)

    back = lax.ppermute(back, "tile", [(i, (i + 1) % size) for i in range(size)])
    probe_sum = lax.cond(
        counts[0] > 0,
        lambda grad: probe_share(grad, near.shape),
        lambda grad: jnp.zeros((near.shape[0] // 8, near.shape[1]), jnp.float32),
        probe_grad)
    object_grad = own_grad + back
    return unflat(object_grad, object_slices.shape), unflat(probe_sum, probe_field.shape)


def solution(mesh):
    in_specs = (
        P(("groups", "tile"), None, None, None),
        P(("groups", "tile"), None, None, None),
        P(("groups", "tile"), None, None),
        P(("groups", "tile")),
        P(("groups", "tile")),
        P(("groups", "tile")),
    )
    out_specs = (P(("groups", "tile"), None, None, None), P(("groups", "tile"), None, None, None))
    return jax.shard_map(shards, mesh=mesh, in_specs=in_specs, out_specs=out_specs, check_vma=False)
```

```python
import math

import jax
import jax.numpy as jnp
import numpy as np
from jax import lax
from jax.experimental import pallas as pl
from jax.experimental.pallas import tpu as pltpu
from jax.sharding import PartitionSpec as P

GROUP_DEV = 16
KAPPA = 4.0
MODES = 2
SLICES = 2
HALVES = 2
AHEAD = (0, 8, 4, 12, 2, 10, 6, 14)


def factors(extent):
    counter = np.arange(extent)
    half = extent // 2
    dft = np.exp(-2j * np.pi * (counter[:, None] * counter[None, :] % extent) / extent) / math.sqrt(extent)
    freq = ((counter + extent // 2) % extent - extent // 2) / extent
    prop = np.conj(dft) @ (np.exp(-1j * np.pi * KAPPA * freq**2)[:, None] * dft)
    whole = [part for matrix in (dft, prop) for part in (matrix.real, matrix.imag)]
    same, cross = prop[:half, :half], prop[:half, half:]
    even, odd = dft[0::2, :half], dft[1::2, :half]
    halves = [even, odd, np.conj(even.T), np.conj(odd.T),
              (same + cross) / 2, (same - cross) / 2, np.conj(same + cross) / 2, np.conj(same - cross) / 2]
    halves = [np.block([[m.real, -m.imag], [m.imag, m.real]]) for m in halves]
    return np.stack(whole + halves).astype(np.float32)


def split(value):
    high = value.astype(jnp.bfloat16)
    low = (value - high.astype(jnp.float32)).astype(jnp.bfloat16)
    return high, low


def prepare(own_ref, patterns_ref, factors_ref, planes_out, patterns_out, mats_out, half_out, own, parts, sems):
    copies = [pltpu.make_async_copy(source, target, sems.at[i]) for i, (source, target) in enumerate(
        ((factors_ref, parts), (own_ref, own), (patterns_ref, patterns_out)))]
    for copy in copies:
        copy.start()
    copies[0].wait()
    extent = parts.shape[1]
    for kind in range(2):
        real, imag = split(parts[2 * kind]), split(parts[2 * kind + 1])
        for conj in range(2):
            for k in range(2):
                mat = 4 * kind + 2 * conj + k
                upper, lower = (-imag[k], imag[k]) if conj else (imag[k], -imag[k])
                mats_out[mat, :extent, :extent] = real[k]
                mats_out[mat, :extent, extent:] = upper
                mats_out[mat, extent:, :extent] = lower
                mats_out[mat, extent:, extent:] = real[k]
    for k in range(half_out.shape[0]):
        high, low = split(parts[4 + k])
        half_out[k, :extent, :extent] = high
        half_out[k, :extent, extent:] = high
        half_out[k, extent:, :extent] = low
        half_out[k, extent:, extent:] = low
    copies[1].wait()
    rows = planes_out.shape[1]
    for layer in range(SLICES):
        for half in range(HALVES):
            for part in range(2):
                source = (layer * HALVES + half) * 2 + part
                plane = (layer * 2 + part) * HALVES + half
                planes_out[plane] = own[pl.ds(source, rows, stride=8), :]
    copies[2].wait()


def times(a, b):
    return [a[0] * b[0] - a[1] * b[1], a[0] * b[1] + a[1] * b[0]]


def conj_times(a, b):
    return [a[0] * b[0] + a[1] * b[1], a[0] * b[1] - a[1] * b[0]]


def add(a, b):
    return [a[0] + b[0], a[1] + b[1]]


def member_rows(member, order, share):
    return pl.ds(pl.multiple_of(lax.bitwise_xor(member, order) * share, share), share)


def place(probe_ref, keep_out, send_out):
    lanes, extent = probe_ref.shape[:2]
    share = extent // GROUP_DEV
    member = lax.rem(lax.axis_index("tile"), GROUP_DEV)
    for odd, ref in enumerate((keep_out, send_out)):
        for block in range(GROUP_DEV // 2):
            there = lax.bitwise_xor(lax.rem(member + block // 2 * 4, GROUP_DEV), 2 * (block % 2) + odd)
            for k in range(lanes):
                rows = pl.ds(block * share * lanes + k, share, stride=lanes)
                ref[rows, :] = probe_ref[k, pl.ds(pl.multiple_of(there * share, share), share), :]


def kernel(scalars_ref, own_ref, low_ref, high_ref, near_ref, far_ref, patterns_ref, mats_ref,
           half_ref, own_out, next_out, probe_acc, obj, acc, probe):
    most, extent = patterns_ref.shape[:2]
    share = extent // GROUP_DEV
    member = lax.rem(lax.axis_index("tile"), GROUP_DEV)
    tile_rows = own_ref.shape[1]
    middle = extent // 2
    lanes = 2 * MODES
    modes = range(MODES)

    for layer in range(SLICES):
        for half in range(HALVES):
            for part in range(2):
                source = (layer * HALVES + half) * 2 + part
                plane = (layer * 2 + part) * HALVES + half
                obj[plane, :tile_rows] = own_ref[plane]
                obj[plane, tile_rows:tile_rows + middle] = low_ref[pl.ds(source, middle, stride=8), :]
                obj[plane, tile_rows + middle:] = high_ref[pl.ds(source, extent - middle, stride=8), :]
    for odd, ref in enumerate((near_ref, far_ref)):
        for block, order in enumerate(AHEAD):
            for k in range(lanes):
                rows = pl.ds(block * share * lanes + k, share, stride=lanes)
                probe[k, member_rows(member, order + odd, share), :] = ref[rows, :]
    acc[...] = jnp.zeros(acc.shape, jnp.float32)
    probe_acc[...] = jnp.zeros(probe_acc.shape, jnp.float32)

    def right(fields, kind, conj):
        high_m, low_m = mats_ref[4 * kind + 2 * conj], mats_ref[4 * kind + 2 * conj + 1]
        rows = jnp.concatenate([jnp.concatenate(f[m], axis=1) for f in fields for m in modes], axis=0)
        high, low = split(rows)
        out = jnp.dot(jnp.concatenate([high, low, high], axis=1), jnp.concatenate([high_m, high_m, low_m], axis=0),
                      preferred_element_type=jnp.float32)
        return [[[out[(i * MODES + m) * extent:(i * MODES + m + 1) * extent, c * extent:(c + 1) * extent]
                  for c in range(2)] for m in modes] for i in range(len(fields))]

    def left(fields, kind, conj):
        middle = extent // 2
        cols = [jnp.concatenate([f[m][c] for f in fields for m in modes], axis=1) for c in range(2)]
        upper, lower = [c[:middle] for c in cols], [c[middle:] for c in cols]
        if kind == 1 or not conj:
            upper, lower = add(upper, lower), [u - v for u, v in zip(upper, lower)]
        halves = []
        for k, pieces in enumerate((upper, lower)):
            high, low = split(jnp.concatenate(pieces, axis=0))
            out = jnp.dot(half_ref[4 * kind + 2 * conj + k], jnp.concatenate([high, low], axis=0),
                          preferred_element_type=jnp.float32)
            out = out[:extent] + out[extent:]
            halves.append([out[:middle], out[middle:]])
        upper, lower = halves
        if kind == 1 or conj:
            upper, lower = add(upper, lower), [u - v for u, v in zip(upper, lower)]
        out = [jnp.concatenate([upper[c], lower[c]], axis=0) for c in range(2)]
        return [[[out[c][:, (i * MODES + m) * extent:(i * MODES + m + 1) * extent] for c in range(2)]
                 for m in modes] for i in range(len(fields))]

    lane = lax.broadcasted_iota(jnp.int32, (extent, extent), 1)

    def window(slot):
        r, c = scalars_ref[slot], scalars_ref[most + slot]
        shift = lax.rem(extent - c, extent)
        layers = []
        for layer in range(SLICES):
            parts = []
            for part in range(2):
                plane = (layer * 2 + part) * HALVES
                joined = jnp.where(lane >= c, obj[plane, pl.ds(r, extent), :], obj[plane + 1, pl.ds(r, extent), :])
                parts.append(pltpu.roll(joined, shift, 1))
            layers.append(parts)
        return layers

    def deposit(slot, layer, grad):
        r, c = scalars_ref[slot], scalars_ref[most + slot]
        for part in range(2):
            plane = (layer * 2 + part) * HALVES
            rolled = pltpu.roll(grad[part], lax.rem(c, extent), 1)
            acc[plane, pl.ds(r, extent), :] += jnp.where(lane >= c, rolled, 0.0)
            acc[plane + 1, pl.ds(r, extent), :] += jnp.where(lane >= c, 0.0, rolled)

    def measured(slot):
        return jnp.concatenate([patterns_ref[slot, pl.ds(k, extent // 2, stride=2), :] for k in range(2)], axis=0)

    def steps(slots):
        n = range(len(slots))
        field = [[probe[2 * m], probe[2 * m + 1]] for m in modes]
        objects = [window(slot) for slot in slots]
        state = right([[times(field[m], objects[i][0]) for m in modes] for i in n], 1, 0)
        yield
        entering = left(state, 1, 0)
        yield
        state = right([[times(entering[i][m], objects[i][1]) for m in modes] for i in n], 0, 0)
        yield
        state = left(state, 0, 0)
        yield
        weight = [2.0 * (sum(state[i][m][c] * state[i][m][c] for m in modes for c in range(2)) - measured(slots[i]))
                  for i in n]
        state = right([[[weight[i] * state[i][m][c] for c in range(2)] for m in modes] for i in n], 0, 1)
        yield
        state = left(state, 0, 1)
        yield
        for i in n:
            grad = conj_times(entering[i][0], state[i][0])
            for m in modes[1:]:
                grad = add(grad, conj_times(entering[i][m], state[i][m]))
            deposit(slots[i], 1, grad)
        state = right([[conj_times(objects[i][1], state[i][m]) for m in modes] for i in n], 1, 1)
        yield
        state = left(state, 1, 1)
        yield
        for i in n:
            grad = conj_times(field[0], state[i][0])
            for m in modes[1:]:
                grad = add(grad, conj_times(field[m], state[i][m]))
            deposit(slots[i], 0, grad)
        for m in modes:
            term = conj_times(objects[0][0], state[0][m])
            for i in n[1:]:
                term = add(term, conj_times(objects[i][0], state[i][m]))
            probe_acc[2 * m] += term[0]
            probe_acc[2 * m + 1] += term[1]

    def run(*sets):
        running = [steps(slots) for slots in sets]
        while running:
            running = [r for r in running if next(r, "done") is None]

    count = scalars_ref[2 * most]
    eights = lax.shift_right_logical(count, 3)
    fours = lax.shift_right_logical(count, 2)

    def eight(j, carry):
        run(*([8 * j + k + i for i in range(4)] for k in (0, 4)))
        return carry

    def four(j, carry):
        run([4 * j, 4 * j + 1], [4 * j + 2, 4 * j + 3])
        return carry

    lax.fori_loop(0, eights, eight, 0)
    lax.fori_loop(2 * eights, fours, four, 0)

    @pl.when(lax.bitwise_and(count, 2) == 2)
    def _():
        run([4 * fours], [4 * fours + 1])

    @pl.when(lax.bitwise_and(count, 1) == 1)
    def _():
        run([count - 1])

    for layer in range(SLICES):
        for half in range(HALVES):
            for part in range(2):
                target = (layer * HALVES + half) * 2 + part
                plane = (layer * 2 + part) * HALVES + half
                own_out[pl.ds(target, tile_rows, stride=8), :] = acc[plane, :tile_rows]
                next_out[pl.ds(target, extent, stride=8), :] = acc[plane, tile_rows:]


def prepared(own, patterns):
    extent = patterns.shape[1]
    vmem = pl.BlockSpec(memory_space=pltpu.VMEM)
    parts = jnp.asarray(factors(extent))
    return pl.pallas_call(
        prepare,
        out_shape=(
            jax.ShapeDtypeStruct((8, own.shape[0] // 8, own.shape[1]), jnp.float32),
            jax.ShapeDtypeStruct(patterns.shape, jnp.float32),
            jax.ShapeDtypeStruct((8, 2 * extent, 2 * extent), jnp.bfloat16),
            jax.ShapeDtypeStruct((8, 2 * extent, 2 * extent), jnp.bfloat16),
        ),
        in_specs=[pl.BlockSpec(memory_space=pltpu.HBM)] * 3,
        out_specs=(vmem,) * 4,
        scratch_shapes=[
            pltpu.VMEM(own.shape, jnp.float32),
            pltpu.VMEM(parts.shape, jnp.float32),
            pltpu.SemaphoreType.DMA((3,)),
        ],
        compiler_params=pltpu.CompilerParams(vmem_limit_bytes=16 * 1024 * 1024),
        cost_estimate=pl.CostEstimate(flops=0, bytes_accessed=6 * 1024 * 1024, transcendentals=0),
    )(own, patterns, parts)


def terms(scalars, planes, low, high, near, far, patterns, mats):
    extent = patterns.shape[1]
    rows = planes.shape[1] + extent
    smem = pl.BlockSpec(memory_space=pltpu.SMEM)
    vmem = pl.BlockSpec(memory_space=pltpu.VMEM)
    return pl.pallas_call(
        kernel,
        out_shape=(
            jax.ShapeDtypeStruct((planes.shape[1] * 8, extent), jnp.float32),
            jax.ShapeDtypeStruct((extent * 8, extent), jnp.float32),
            jax.ShapeDtypeStruct((2 * MODES, extent, extent), jnp.float32),
        ),
        in_specs=[smem] + [vmem] * 8,
        out_specs=(vmem,) * 3,
        scratch_shapes=[
            pltpu.VMEM((8, rows, extent), jnp.float32),
            pltpu.VMEM((8, rows, extent), jnp.float32),
            pltpu.VMEM((2 * MODES, extent, extent), jnp.float32),
        ],
        compiler_params=pltpu.CompilerParams(vmem_limit_bytes=40 * 1024 * 1024),
    )(scalars, planes, low, high, near, far, patterns, *mats)


def placed(probe_grad, shape):
    vmem = pl.BlockSpec(memory_space=pltpu.VMEM)
    return pl.pallas_call(
        place,
        out_shape=(jax.ShapeDtypeStruct(shape, jnp.float32),) * 2,
        in_specs=[vmem],
        out_specs=(vmem,) * 2,
        compiler_params=pltpu.CompilerParams(vmem_limit_bytes=4 * 1024 * 1024),
    )(probe_grad)


def flat(block):
    rows, k, parts, columns = block.shape
    split_up = block.reshape(rows, k, parts, columns // 128, 128)
    return split_up.transpose(0, 1, 3, 2, 4).reshape(-1, 128)


def unflat(value, shape):
    rows, k, parts, columns = shape
    return value.reshape(rows, k, columns // 128, parts, 128).transpose(0, 1, 3, 2, 4).reshape(shape)


def partner(value, bits):
    return lax.ppermute(value, "tile", [(i, i ^ bits) for i in range(lax.axis_size("tile"))])


def halved(value):
    return value[:value.shape[0] // 2], value[value.shape[0] // 2:]


def places_on(value, distance):
    members = range(lax.axis_size("tile"))
    return lax.ppermute(value, "tile", [
        (i, i // GROUP_DEV * GROUP_DEV + (i + distance) % GROUP_DEV) for i in members])


def probe_share(probe_grad, shape):
    keep, send = placed(probe_grad, shape)
    blocks = jnp.split(keep + partner(send, 1), 4, axis=0)
    total = blocks[0] + sum(places_on(block, 4 * k) for k, block in enumerate(blocks) if k > 0)
    keep, send = halved(total)
    return keep + partner(send, 2)


def shards(object_slices, probe_field, patterns, row_offsets, col_offsets, counts):
    size = lax.axis_size("tile")
    down = [((i + 1) % size, i) for i in range(size)]
    own = flat(object_slices)
    low, high = halved(own)
    scalars = jnp.concatenate([row_offsets, col_offsets, counts])

    low, high, mine = lax.optimization_barrier((low, high, flat(probe_field)))
    low = lax.ppermute(low, "tile", down)
    quarter = jnp.concatenate([mine, partner(mine, 8), partner(mine, 4), partner(mine, 12)], axis=0)
    low, high, quarter, patterns, own = lax.optimization_barrier((low, high, quarter, patterns, own))
    near = jnp.concatenate([quarter, partner(quarter, 2)], axis=0)
    high = lax.ppermute(high, "tile", down)
    planes, patterns, *mats = prepared(own, patterns)
    near, planes, patterns, scalars, *mats = lax.optimization_barrier((near, planes, patterns, scalars, *mats))
    far = partner(near, 1)

    own_grad, back, probe_grad = terms(scalars, planes, low, high, near, far, patterns, mats)

    back = lax.ppermute(back, "tile", [(i, (i + 1) % size) for i in range(size)])
    probe_sum = lax.cond(
        counts[0] > 0,
        lambda grad: probe_share(grad, near.shape),
        lambda grad: jnp.zeros((near.shape[0] // 8, near.shape[1]), jnp.float32),
        probe_grad)
    object_grad = own_grad + back
    return unflat(object_grad, object_slices.shape), unflat(probe_sum, probe_field.shape)


def solution(mesh):
    in_specs = (
        P(("groups", "tile"), None, None, None),
        P(("groups", "tile"), None, None, None),
        P(("groups", "tile"), None, None),
        P(("groups", "tile")),
        P(("groups", "tile")),
        P(("groups", "tile")),
    )
    out_specs = (P(("groups", "tile"), None, None, None), P(("groups", "tile"), None, None, None))
    return jax.shard_map(shards, mesh=mesh, in_specs=in_specs, out_specs=out_specs, check_vma=False)
```

```python
import math

import jax
import jax.numpy as jnp
import numpy as np
from jax import lax
from jax.experimental import pallas as pl
from jax.experimental.pallas import tpu as pltpu
from jax.sharding import PartitionSpec as P

GROUP_DEV = 16
KAPPA = 4.0
MODES = 2
SLICES = 2
HALVES = 2
AHEAD = (0, 8, 4, 12, 2, 10, 6, 14)


def factors(extent):
    counter = np.arange(extent)
    half = extent // 2
    dft = np.exp(-2j * np.pi * (counter[:, None] * counter[None, :] % extent) / extent) / math.sqrt(extent)
    freq = ((counter + extent // 2) % extent - extent // 2) / extent
    prop = np.conj(dft) @ (np.exp(-1j * np.pi * KAPPA * freq**2)[:, None] * dft)
    whole = [part for matrix in (dft, prop) for part in (matrix.real, matrix.imag)]
    same, cross = prop[:half, :half], prop[:half, half:]
    even, odd = dft[0::2, :half], dft[1::2, :half]
    halves = [even, odd, np.conj(even.T), np.conj(odd.T),
              (same + cross) / 2, (same - cross) / 2, np.conj(same + cross) / 2, np.conj(same - cross) / 2]
    halves = [np.block([[m.real, -m.imag], [m.imag, m.real]]) for m in halves]
    return np.stack(whole + halves).astype(np.float32)


def split(value):
    high = value.astype(jnp.bfloat16)
    low = (value - high.astype(jnp.float32)).astype(jnp.bfloat16)
    return high, low


def prepare(own_ref, patterns_ref, factors_ref, planes_out, patterns_out, mats_out, half_out, own, parts, sems):
    copies = [pltpu.make_async_copy(source, target, sems.at[i]) for i, (source, target) in enumerate(
        ((factors_ref, parts), (own_ref, own), (patterns_ref, patterns_out)))]
    for copy in copies:
        copy.start()
    copies[0].wait()
    extent = parts.shape[1]
    for kind in range(2):
        real, imag = split(parts[2 * kind]), split(parts[2 * kind + 1])
        for conj in range(2):
            for k in range(2):
                mat = 4 * kind + 2 * conj + k
                upper, lower = (-imag[k], imag[k]) if conj else (imag[k], -imag[k])
                mats_out[mat, :extent, :extent] = real[k]
                mats_out[mat, :extent, extent:] = upper
                mats_out[mat, extent:, :extent] = lower
                mats_out[mat, extent:, extent:] = real[k]
    for k in range(half_out.shape[0]):
        high, low = split(parts[4 + k])
        half_out[k, :extent, :extent] = high
        half_out[k, :extent, extent:] = high
        half_out[k, extent:, :extent] = low
        half_out[k, extent:, extent:] = low
    copies[1].wait()
    rows = planes_out.shape[1]
    for layer in range(SLICES):
        for half in range(HALVES):
            for part in range(2):
                source = (layer * HALVES + half) * 2 + part
                plane = (layer * 2 + part) * HALVES + half
                planes_out[plane] = own[pl.ds(source, rows, stride=8), :]
    copies[2].wait()


def times(a, b):
    return [a[0] * b[0] - a[1] * b[1], a[0] * b[1] + a[1] * b[0]]


def conj_times(a, b):
    return [a[0] * b[0] + a[1] * b[1], a[0] * b[1] - a[1] * b[0]]


def add(a, b):
    return [a[0] + b[0], a[1] + b[1]]


def member_rows(member, order, share):
    return pl.ds(pl.multiple_of(lax.bitwise_xor(member, order) * share, share), share)


def place(probe_ref, keep_out, send_out):
    lanes, extent = probe_ref.shape[:2]
    share = extent // GROUP_DEV
    member = lax.rem(lax.axis_index("tile"), GROUP_DEV)
    for odd, ref in enumerate((keep_out, send_out)):
        for block in range(GROUP_DEV // 2):
            there = lax.bitwise_xor(lax.rem(member + block // 2 * 4, GROUP_DEV), 2 * (block % 2) + odd)
            for k in range(lanes):
                rows = pl.ds(block * share * lanes + k, share, stride=lanes)
                ref[rows, :] = probe_ref[k, pl.ds(pl.multiple_of(there * share, share), share), :]


def kernel(scalars_ref, own_ref, low_ref, high_ref, near_ref, far_ref, patterns_ref, mats_ref,
           half_ref, own_out, next_out, probe_acc, obj, acc, probe):
    most, extent = patterns_ref.shape[:2]
    share = extent // GROUP_DEV
    member = lax.rem(lax.axis_index("tile"), GROUP_DEV)
    tile_rows = own_ref.shape[1]
    middle = extent // 2
    lanes = 2 * MODES
    modes = range(MODES)

    for layer in range(SLICES):
        for half in range(HALVES):
            for part in range(2):
                source = (layer * HALVES + half) * 2 + part
                plane = (layer * 2 + part) * HALVES + half
                obj[plane, :tile_rows] = own_ref[plane]
                obj[plane, tile_rows:tile_rows + middle] = low_ref[pl.ds(source, middle, stride=8), :]
                obj[plane, tile_rows + middle:] = high_ref[pl.ds(source, extent - middle, stride=8), :]
    for odd, ref in enumerate((near_ref, far_ref)):
        for block, order in enumerate(AHEAD):
            for k in range(lanes):
                rows = pl.ds(block * share * lanes + k, share, stride=lanes)
                probe[k, member_rows(member, order + odd, share), :] = ref[rows, :]
    acc[...] = jnp.zeros(acc.shape, jnp.float32)
    probe_acc[...] = jnp.zeros(probe_acc.shape, jnp.float32)

    def right(fields, kind, conj):
        high_m, low_m = mats_ref[4 * kind + 2 * conj], mats_ref[4 * kind + 2 * conj + 1]
        rows = jnp.concatenate([jnp.concatenate(f[m], axis=1) for f in fields for m in modes], axis=0)
        high, low = split(rows)
        out = jnp.dot(jnp.concatenate([high, low, high], axis=1), jnp.concatenate([high_m, high_m, low_m], axis=0),
                      preferred_element_type=jnp.float32)
        return [[[out[(i * MODES + m) * extent:(i * MODES + m + 1) * extent, c * extent:(c + 1) * extent]
                  for c in range(2)] for m in modes] for i in range(len(fields))]

    def left(fields, kind, conj):
        middle = extent // 2
        cols = [jnp.concatenate([f[m][c] for f in fields for m in modes], axis=1) for c in range(2)]
        upper, lower = [c[:middle] for c in cols], [c[middle:] for c in cols]
        if kind == 1 or not conj:
            upper, lower = add(upper, lower), [u - v for u, v in zip(upper, lower)]
        halves = []
        for k, pieces in enumerate((upper, lower)):
            high, low = split(jnp.concatenate(pieces, axis=0))
            out = jnp.dot(half_ref[4 * kind + 2 * conj + k], jnp.concatenate([high, low], axis=0),
                          preferred_element_type=jnp.float32)
            out = out[:extent] + out[extent:]
            halves.append([out[:middle], out[middle:]])
        upper, lower = halves
        if kind == 1 or conj:
            upper, lower = add(upper, lower), [u - v for u, v in zip(upper, lower)]
        out = [jnp.concatenate([upper[c], lower[c]], axis=0) for c in range(2)]
        return [[[out[c][:, (i * MODES + m) * extent:(i * MODES + m + 1) * extent] for c in range(2)]
                 for m in modes] for i in range(len(fields))]

    lane = lax.broadcasted_iota(jnp.int32, (extent, extent), 1)

    def window(slot):
        r, c = scalars_ref[slot], scalars_ref[most + slot]
        shift = lax.rem(extent - c, extent)
        layers = []
        for layer in range(SLICES):
            parts = []
            for part in range(2):
                plane = (layer * 2 + part) * HALVES
                joined = jnp.where(lane >= c, obj[plane, pl.ds(r, extent), :], obj[plane + 1, pl.ds(r, extent), :])
                parts.append(pltpu.roll(joined, shift, 1))
            layers.append(parts)
        return layers

    def deposit(slot, layer, grad):
        r, c = scalars_ref[slot], scalars_ref[most + slot]
        for part in range(2):
            plane = (layer * 2 + part) * HALVES
            rolled = pltpu.roll(grad[part], lax.rem(c, extent), 1)
            acc[plane, pl.ds(r, extent), :] += jnp.where(lane >= c, rolled, 0.0)
            acc[plane + 1, pl.ds(r, extent), :] += jnp.where(lane >= c, 0.0, rolled)

    def measured(slot):
        return jnp.concatenate([patterns_ref[slot, pl.ds(k, extent // 2, stride=2), :] for k in range(2)], axis=0)

    def steps(slots):
        n = range(len(slots))
        field = [[probe[2 * m], probe[2 * m + 1]] for m in modes]
        objects = [window(slot) for slot in slots]
        state = right([[times(field[m], objects[i][0]) for m in modes] for i in n], 1, 0)
        yield
        entering = left(state, 1, 0)
        yield
        state = right([[times(entering[i][m], objects[i][1]) for m in modes] for i in n], 0, 0)
        yield
        state = left(state, 0, 0)
        yield
        weight = [2.0 * (sum(state[i][m][c] * state[i][m][c] for m in modes for c in range(2)) - measured(slots[i]))
                  for i in n]
        state = right([[[weight[i] * state[i][m][c] for c in range(2)] for m in modes] for i in n], 0, 1)
        yield
        state = left(state, 0, 1)
        yield
        for i in n:
            grad = conj_times(entering[i][0], state[i][0])
            for m in modes[1:]:
                grad = add(grad, conj_times(entering[i][m], state[i][m]))
            deposit(slots[i], 1, grad)
        state = right([[conj_times(objects[i][1], state[i][m]) for m in modes] for i in n], 1, 1)
        yield
        state = left(state, 1, 1)
        yield
        for i in n:
            grad = conj_times(field[0], state[i][0])
            for m in modes[1:]:
                grad = add(grad, conj_times(field[m], state[i][m]))
            deposit(slots[i], 0, grad)
        for m in modes:
            term = conj_times(objects[0][0], state[0][m])
            for i in n[1:]:
                term = add(term, conj_times(objects[i][0], state[i][m]))
            probe_acc[2 * m] += term[0]
            probe_acc[2 * m + 1] += term[1]

    def run(*sets):
        running = [steps(slots) for slots in sets]
        while running:
            running = [r for r in running if next(r, "done") is None]

    count = scalars_ref[2 * most]
    eights = lax.shift_right_logical(count, 3)
    fours = lax.shift_right_logical(count, 2)

    def eight(j, carry):
        run(*([8 * j + k + i for i in range(4)] for k in (0, 4)))
        return carry

    def four(j, carry):
        run([4 * j, 4 * j + 1], [4 * j + 2, 4 * j + 3])
        return carry

    lax.fori_loop(0, eights, eight, 0)
    lax.fori_loop(2 * eights, fours, four, 0)

    @pl.when(lax.bitwise_and(count, 2) == 2)
    def _():
        run([4 * fours], [4 * fours + 1])

    @pl.when(lax.bitwise_and(count, 1) == 1)
    def _():
        run([count - 1])

    for layer in range(SLICES):
        for half in range(HALVES):
            for part in range(2):
                target = (layer * HALVES + half) * 2 + part
                plane = (layer * 2 + part) * HALVES + half
                own_out[pl.ds(target, tile_rows, stride=8), :] = acc[plane, :tile_rows]
                next_out[pl.ds(target, extent, stride=8), :] = acc[plane, tile_rows:]


def prepared(own, patterns):
    extent = patterns.shape[1]
    vmem = pl.BlockSpec(memory_space=pltpu.VMEM)
    parts = jnp.asarray(factors(extent))
    return pl.pallas_call(
        prepare,
        out_shape=(
            jax.ShapeDtypeStruct((8, own.shape[0] // 8, own.shape[1]), jnp.float32),
            jax.ShapeDtypeStruct(patterns.shape, jnp.float32),
            jax.ShapeDtypeStruct((8, 2 * extent, 2 * extent), jnp.bfloat16),
            jax.ShapeDtypeStruct((8, 2 * extent, 2 * extent), jnp.bfloat16),
        ),
        in_specs=[pl.BlockSpec(memory_space=pltpu.HBM)] * 3,
        out_specs=(vmem,) * 4,
        scratch_shapes=[
            pltpu.VMEM(own.shape, jnp.float32),
            pltpu.VMEM(parts.shape, jnp.float32),
            pltpu.SemaphoreType.DMA((3,)),
        ],
        compiler_params=pltpu.CompilerParams(vmem_limit_bytes=16 * 1024 * 1024),
        cost_estimate=pl.CostEstimate(flops=0, bytes_accessed=6 * 1024 * 1024, transcendentals=0),
    )(own, patterns, parts)


def terms(scalars, planes, low, high, near, far, patterns, mats):
    extent = patterns.shape[1]
    rows = planes.shape[1] + extent
    smem = pl.BlockSpec(memory_space=pltpu.SMEM)
    vmem = pl.BlockSpec(memory_space=pltpu.VMEM)
    return pl.pallas_call(
        kernel,
        out_shape=(
            jax.ShapeDtypeStruct((planes.shape[1] * 8, extent), jnp.float32),
            jax.ShapeDtypeStruct((extent * 8, extent), jnp.float32),
            jax.ShapeDtypeStruct((2 * MODES, extent, extent), jnp.float32),
        ),
        in_specs=[smem] + [vmem] * 8,
        out_specs=(vmem,) * 3,
        scratch_shapes=[
            pltpu.VMEM((8, rows, extent), jnp.float32),
            pltpu.VMEM((8, rows, extent), jnp.float32),
            pltpu.VMEM((2 * MODES, extent, extent), jnp.float32),
        ],
        compiler_params=pltpu.CompilerParams(vmem_limit_bytes=40 * 1024 * 1024),
    )(scalars, planes, low, high, near, far, patterns, *mats)


def placed(probe_grad, shape):
    vmem = pl.BlockSpec(memory_space=pltpu.VMEM)
    return pl.pallas_call(
        place,
        out_shape=(jax.ShapeDtypeStruct(shape, jnp.float32),) * 2,
        in_specs=[vmem],
        out_specs=(vmem,) * 2,
        compiler_params=pltpu.CompilerParams(vmem_limit_bytes=4 * 1024 * 1024),
    )(probe_grad)


def flat(block):
    rows, k, parts, columns = block.shape
    split_up = block.reshape(rows, k, parts, columns // 128, 128)
    return split_up.transpose(0, 1, 3, 2, 4).reshape(-1, 128)


def unflat(value, shape):
    rows, k, parts, columns = shape
    return value.reshape(rows, k, columns // 128, parts, 128).transpose(0, 1, 3, 2, 4).reshape(shape)


def partner(value, bits):
    return lax.ppermute(value, "tile", [(i, i ^ bits) for i in range(lax.axis_size("tile"))])


def halved(value):
    return value[:value.shape[0] // 2], value[value.shape[0] // 2:]


def places_on(value, distance):
    members = range(lax.axis_size("tile"))
    return lax.ppermute(value, "tile", [
        (i, i // GROUP_DEV * GROUP_DEV + (i + distance) % GROUP_DEV) for i in members])


def probe_share(probe_grad, shape):
    keep, send = placed(probe_grad, shape)
    blocks = jnp.split(keep + partner(send, 1), 4, axis=0)
    total = blocks[0] + sum(places_on(block, 4 * k) for k, block in enumerate(blocks) if k > 0)
    keep, send = halved(total)
    return keep + partner(send, 2)


def shards(object_slices, probe_field, patterns, row_offsets, col_offsets, counts):
    size = lax.axis_size("tile")
    down = [((i + 1) % size, i) for i in range(size)]
    own = flat(object_slices)
    low, high = halved(own)
    scalars = jnp.concatenate([row_offsets, col_offsets, counts])

    low, high, mine = lax.optimization_barrier((low, high, flat(probe_field)))
    low = lax.ppermute(low, "tile", down)
    quarter = jnp.concatenate([mine, partner(mine, 8), partner(mine, 4), partner(mine, 12)], axis=0)
    planes, patterns, *mats = prepared(own, patterns)
    low, high, quarter, planes, patterns, scalars, *mats = lax.optimization_barrier(
        (low, high, quarter, planes, patterns, scalars, *mats))
    near = jnp.concatenate([quarter, partner(quarter, 2)], axis=0)
    high = lax.ppermute(high, "tile", down)
    far = partner(near, 1)

    own_grad, back, probe_grad = terms(scalars, planes, low, high, near, far, patterns, mats)

    back = lax.ppermute(back, "tile", [(i, (i + 1) % size) for i in range(size)])
    probe_sum = lax.cond(
        counts[0] > 0,
        lambda grad: probe_share(grad, near.shape),
        lambda grad: jnp.zeros((near.shape[0] // 8, near.shape[1]), jnp.float32),
        probe_grad)
    object_grad = own_grad + back
    return unflat(object_grad, object_slices.shape), unflat(probe_sum, probe_field.shape)


def solution(mesh):
    in_specs = (
        P(("groups", "tile"), None, None, None),
        P(("groups", "tile"), None, None, None),
        P(("groups", "tile"), None, None),
        P(("groups", "tile")),
        P(("groups", "tile")),
        P(("groups", "tile")),
    )
    out_specs = (P(("groups", "tile"), None, None, None), P(("groups", "tile"), None, None, None))
    return jax.shard_map(shards, mesh=mesh, in_specs=in_specs, out_specs=out_specs, check_vma=False)
```

```python
import math

import jax
import jax.numpy as jnp
import numpy as np
from jax import lax
from jax.experimental import pallas as pl
from jax.experimental.pallas import tpu as pltpu
from jax.sharding import PartitionSpec as P

GROUP_DEV = 16
KAPPA = 4.0
MODES = 2
SLICES = 2
HALVES = 2
AHEAD = (0, 8, 4, 12, 2, 10, 6, 14)


def factors(extent):
    counter = np.arange(extent)
    half = extent // 2
    dft = np.exp(-2j * np.pi * (counter[:, None] * counter[None, :] % extent) / extent) / math.sqrt(extent)
    freq = ((counter + extent // 2) % extent - extent // 2) / extent
    prop = np.conj(dft) @ (np.exp(-1j * np.pi * KAPPA * freq**2)[:, None] * dft)
    whole = [part for matrix in (dft, prop) for part in (matrix.real, matrix.imag)]
    same, cross = prop[:half, :half], prop[:half, half:]
    even, odd = dft[0::2, :half], dft[1::2, :half]
    halves = [even, odd, np.conj(even.T), np.conj(odd.T),
              (same + cross) / 2, (same - cross) / 2, np.conj(same + cross) / 2, np.conj(same - cross) / 2]
    halves = [np.block([[m.real, -m.imag], [m.imag, m.real]]) for m in halves]
    return np.stack(whole + halves).astype(np.float32)


def split(value):
    high = value.astype(jnp.bfloat16)
    low = (value - high.astype(jnp.float32)).astype(jnp.bfloat16)
    return high, low


def matrices(factors_ref, mats_out, half_out):
    extent = factors_ref.shape[1]
    for kind in range(2):
        real, imag = split(factors_ref[2 * kind]), split(factors_ref[2 * kind + 1])
        for conj in range(2):
            for k in range(2):
                mat = 4 * kind + 2 * conj + k
                upper, lower = (-imag[k], imag[k]) if conj else (imag[k], -imag[k])
                mats_out[mat, :extent, :extent] = real[k]
                mats_out[mat, :extent, extent:] = upper
                mats_out[mat, extent:, :extent] = lower
                mats_out[mat, extent:, extent:] = real[k]
    for k in range(half_out.shape[0]):
        high, low = split(factors_ref[4 + k])
        half_out[k, :extent, :extent] = high
        half_out[k, :extent, extent:] = high
        half_out[k, extent:, :extent] = low
        half_out[k, extent:, extent:] = low


def prepare(own_ref, patterns_ref, planes_out, patterns_out, own, sems):
    copies = [pltpu.make_async_copy(source, target, sems.at[i]) for i, (source, target) in enumerate(
        ((own_ref, own), (patterns_ref, patterns_out)))]
    for copy in copies:
        copy.start()
    copies[0].wait()
    rows = planes_out.shape[1]
    for layer in range(SLICES):
        for half in range(HALVES):
            for part in range(2):
                source = (layer * HALVES + half) * 2 + part
                plane = (layer * 2 + part) * HALVES + half
                planes_out[plane] = own[pl.ds(source, rows, stride=8), :]
    copies[1].wait()


def times(a, b):
    return [a[0] * b[0] - a[1] * b[1], a[0] * b[1] + a[1] * b[0]]


def conj_times(a, b):
    return [a[0] * b[0] + a[1] * b[1], a[0] * b[1] - a[1] * b[0]]


def add(a, b):
    return [a[0] + b[0], a[1] + b[1]]


def member_rows(member, order, share):
    return pl.ds(pl.multiple_of(lax.bitwise_xor(member, order) * share, share), share)


def place(probe_ref, keep_out, send_out):
    lanes, extent = probe_ref.shape[:2]
    share = extent // GROUP_DEV
    member = lax.rem(lax.axis_index("tile"), GROUP_DEV)
    for odd, ref in enumerate((keep_out, send_out)):
        for block in range(GROUP_DEV // 2):
            there = lax.bitwise_xor(lax.rem(member + block // 2 * 4, GROUP_DEV), 2 * (block % 2) + odd)
            for k in range(lanes):
                rows = pl.ds(block * share * lanes + k, share, stride=lanes)
                ref[rows, :] = probe_ref[k, pl.ds(pl.multiple_of(there * share, share), share), :]


def kernel(scalars_ref, own_ref, low_ref, high_ref, near_ref, far_ref, patterns_ref, mats_ref,
           half_ref, own_out, next_out, probe_acc, obj, acc, probe):
    most, extent = patterns_ref.shape[:2]
    share = extent // GROUP_DEV
    member = lax.rem(lax.axis_index("tile"), GROUP_DEV)
    tile_rows = own_ref.shape[1]
    middle = extent // 2
    lanes = 2 * MODES
    modes = range(MODES)

    for layer in range(SLICES):
        for half in range(HALVES):
            for part in range(2):
                source = (layer * HALVES + half) * 2 + part
                plane = (layer * 2 + part) * HALVES + half
                obj[plane, :tile_rows] = own_ref[plane]
                obj[plane, tile_rows:tile_rows + middle] = low_ref[pl.ds(source, middle, stride=8), :]
                obj[plane, tile_rows + middle:] = high_ref[pl.ds(source, extent - middle, stride=8), :]
    for odd, ref in enumerate((near_ref, far_ref)):
        for block, order in enumerate(AHEAD):
            for k in range(lanes):
                rows = pl.ds(block * share * lanes + k, share, stride=lanes)
                probe[k, member_rows(member, order + odd, share), :] = ref[rows, :]
    acc[...] = jnp.zeros(acc.shape, jnp.float32)
    probe_acc[...] = jnp.zeros(probe_acc.shape, jnp.float32)

    def right(fields, kind, conj):
        high_m, low_m = mats_ref[4 * kind + 2 * conj], mats_ref[4 * kind + 2 * conj + 1]
        rows = jnp.concatenate([jnp.concatenate(f[m], axis=1) for f in fields for m in modes], axis=0)
        high, low = split(rows)
        out = jnp.dot(jnp.concatenate([high, low, high], axis=1), jnp.concatenate([high_m, high_m, low_m], axis=0),
                      preferred_element_type=jnp.float32)
        return [[[out[(i * MODES + m) * extent:(i * MODES + m + 1) * extent, c * extent:(c + 1) * extent]
                  for c in range(2)] for m in modes] for i in range(len(fields))]

    def left(fields, kind, conj):
        middle = extent // 2
        cols = [jnp.concatenate([f[m][c] for f in fields for m in modes], axis=1) for c in range(2)]
        upper, lower = [c[:middle] for c in cols], [c[middle:] for c in cols]
        if kind == 1 or not conj:
            upper, lower = add(upper, lower), [u - v for u, v in zip(upper, lower)]
        halves = []
        for k, pieces in enumerate((upper, lower)):
            high, low = split(jnp.concatenate(pieces, axis=0))
            out = jnp.dot(half_ref[4 * kind + 2 * conj + k], jnp.concatenate([high, low], axis=0),
                          preferred_element_type=jnp.float32)
            out = out[:extent] + out[extent:]
            halves.append([out[:middle], out[middle:]])
        upper, lower = halves
        if kind == 1 or conj:
            upper, lower = add(upper, lower), [u - v for u, v in zip(upper, lower)]
        out = [jnp.concatenate([upper[c], lower[c]], axis=0) for c in range(2)]
        return [[[out[c][:, (i * MODES + m) * extent:(i * MODES + m + 1) * extent] for c in range(2)]
                 for m in modes] for i in range(len(fields))]

    lane = lax.broadcasted_iota(jnp.int32, (extent, extent), 1)

    def window(slot):
        r, c = scalars_ref[slot], scalars_ref[most + slot]
        shift = lax.rem(extent - c, extent)
        layers = []
        for layer in range(SLICES):
            parts = []
            for part in range(2):
                plane = (layer * 2 + part) * HALVES
                joined = jnp.where(lane >= c, obj[plane, pl.ds(r, extent), :], obj[plane + 1, pl.ds(r, extent), :])
                parts.append(pltpu.roll(joined, shift, 1))
            layers.append(parts)
        return layers

    def deposit(slot, layer, grad):
        r, c = scalars_ref[slot], scalars_ref[most + slot]
        for part in range(2):
            plane = (layer * 2 + part) * HALVES
            rolled = pltpu.roll(grad[part], lax.rem(c, extent), 1)
            acc[plane, pl.ds(r, extent), :] += jnp.where(lane >= c, rolled, 0.0)
            acc[plane + 1, pl.ds(r, extent), :] += jnp.where(lane >= c, 0.0, rolled)

    def measured(slot):
        return jnp.concatenate([patterns_ref[slot, pl.ds(k, extent // 2, stride=2), :] for k in range(2)], axis=0)

    def steps(slots):
        n = range(len(slots))
        field = [[probe[2 * m], probe[2 * m + 1]] for m in modes]
        objects = [window(slot) for slot in slots]
        state = right([[times(field[m], objects[i][0]) for m in modes] for i in n], 1, 0)
        yield
        entering = left(state, 1, 0)
        yield
        state = right([[times(entering[i][m], objects[i][1]) for m in modes] for i in n], 0, 0)
        yield
        state = left(state, 0, 0)
        yield
        weight = [2.0 * (sum(state[i][m][c] * state[i][m][c] for m in modes for c in range(2)) - measured(slots[i]))
                  for i in n]
        state = right([[[weight[i] * state[i][m][c] for c in range(2)] for m in modes] for i in n], 0, 1)
        yield
        state = left(state, 0, 1)
        yield
        for i in n:
            grad = conj_times(entering[i][0], state[i][0])
            for m in modes[1:]:
                grad = add(grad, conj_times(entering[i][m], state[i][m]))
            deposit(slots[i], 1, grad)
        state = right([[conj_times(objects[i][1], state[i][m]) for m in modes] for i in n], 1, 1)
        yield
        state = left(state, 1, 1)
        yield
        for i in n:
            grad = conj_times(field[0], state[i][0])
            for m in modes[1:]:
                grad = add(grad, conj_times(field[m], state[i][m]))
            deposit(slots[i], 0, grad)
        for m in modes:
            term = conj_times(objects[0][0], state[0][m])
            for i in n[1:]:
                term = add(term, conj_times(objects[i][0], state[i][m]))
            probe_acc[2 * m] += term[0]
            probe_acc[2 * m + 1] += term[1]

    def run(*sets):
        running = [steps(slots) for slots in sets]
        while running:
            running = [r for r in running if next(r, "done") is None]

    count = scalars_ref[2 * most]
    eights = lax.shift_right_logical(count, 3)
    fours = lax.shift_right_logical(count, 2)

    def eight(j, carry):
        run(*([8 * j + k + i for i in range(4)] for k in (0, 4)))
        return carry

    def four(j, carry):
        run([4 * j, 4 * j + 1], [4 * j + 2, 4 * j + 3])
        return carry

    lax.fori_loop(0, eights, eight, 0)
    lax.fori_loop(2 * eights, fours, four, 0)

    @pl.when(lax.bitwise_and(count, 2) == 2)
    def _():
        run([4 * fours], [4 * fours + 1])

    @pl.when(lax.bitwise_and(count, 1) == 1)
    def _():
        run([count - 1])

    for layer in range(SLICES):
        for half in range(HALVES):
            for part in range(2):
                target = (layer * HALVES + half) * 2 + part
                plane = (layer * 2 + part) * HALVES + half
                own_out[pl.ds(target, tile_rows, stride=8), :] = acc[plane, :tile_rows]
                next_out[pl.ds(target, extent, stride=8), :] = acc[plane, tile_rows:]


def prepared(own, patterns):
    vmem = pl.BlockSpec(memory_space=pltpu.VMEM)
    return pl.pallas_call(
        prepare,
        out_shape=(
            jax.ShapeDtypeStruct((8, own.shape[0] // 8, own.shape[1]), jnp.float32),
            jax.ShapeDtypeStruct(patterns.shape, jnp.float32),
        ),
        in_specs=[pl.BlockSpec(memory_space=pltpu.HBM)] * 2,
        out_specs=(vmem,) * 2,
        scratch_shapes=[pltpu.VMEM(own.shape, jnp.float32), pltpu.SemaphoreType.DMA((2,))],
        compiler_params=pltpu.CompilerParams(vmem_limit_bytes=16 * 1024 * 1024),
        cost_estimate=pl.CostEstimate(flops=0, bytes_accessed=4 * 1024 * 1024, transcendentals=0),
    )(own, patterns)


def built_matrices(extent):
    vmem = pl.BlockSpec(memory_space=pltpu.VMEM)
    return pl.pallas_call(
        matrices,
        out_shape=(jax.ShapeDtypeStruct((8, 2 * extent, 2 * extent), jnp.bfloat16),) * 2,
        in_specs=[vmem],
        out_specs=(vmem,) * 2,
        compiler_params=pltpu.CompilerParams(vmem_limit_bytes=16 * 1024 * 1024),
        cost_estimate=pl.CostEstimate(flops=0, bytes_accessed=3 * 1024 * 1024, transcendentals=0),
    )(jnp.asarray(factors(extent)))


def terms(scalars, planes, low, high, near, far, patterns, mats):
    extent = patterns.shape[1]
    rows = planes.shape[1] + extent
    smem = pl.BlockSpec(memory_space=pltpu.SMEM)
    vmem = pl.BlockSpec(memory_space=pltpu.VMEM)
    return pl.pallas_call(
        kernel,
        out_shape=(
            jax.ShapeDtypeStruct((planes.shape[1] * 8, extent), jnp.float32),
            jax.ShapeDtypeStruct((extent * 8, extent), jnp.float32),
            jax.ShapeDtypeStruct((2 * MODES, extent, extent), jnp.float32),
        ),
        in_specs=[smem] + [vmem] * 8,
        out_specs=(vmem,) * 3,
        scratch_shapes=[
            pltpu.VMEM((8, rows, extent), jnp.float32),
            pltpu.VMEM((8, rows, extent), jnp.float32),
            pltpu.VMEM((2 * MODES, extent, extent), jnp.float32),
        ],
        compiler_params=pltpu.CompilerParams(vmem_limit_bytes=40 * 1024 * 1024),
    )(scalars, planes, low, high, near, far, patterns, *mats)


def placed(probe_grad, shape):
    vmem = pl.BlockSpec(memory_space=pltpu.VMEM)
    return pl.pallas_call(
        place,
        out_shape=(jax.ShapeDtypeStruct(shape, jnp.float32),) * 2,
        in_specs=[vmem],
        out_specs=(vmem,) * 2,
        compiler_params=pltpu.CompilerParams(vmem_limit_bytes=4 * 1024 * 1024),
    )(probe_grad)


def flat(block):
    rows, k, parts, columns = block.shape
    split_up = block.reshape(rows, k, parts, columns // 128, 128)
    return split_up.transpose(0, 1, 3, 2, 4).reshape(-1, 128)


def unflat(value, shape):
    rows, k, parts, columns = shape
    return value.reshape(rows, k, columns // 128, parts, 128).transpose(0, 1, 3, 2, 4).reshape(shape)


def partner(value, bits):
    return lax.ppermute(value, "tile", [(i, i ^ bits) for i in range(lax.axis_size("tile"))])


def halved(value):
    return value[:value.shape[0] // 2], value[value.shape[0] // 2:]


def places_on(value, distance):
    members = range(lax.axis_size("tile"))
    return lax.ppermute(value, "tile", [
        (i, i // GROUP_DEV * GROUP_DEV + (i + distance) % GROUP_DEV) for i in members])


def probe_share(probe_grad, shape):
    keep, send = placed(probe_grad, shape)
    blocks = jnp.split(keep + partner(send, 1), 4, axis=0)
    total = blocks[0] + sum(places_on(block, 4 * k) for k, block in enumerate(blocks) if k > 0)
    keep, send = halved(total)
    return keep + partner(send, 2)


def shards(object_slices, probe_field, patterns, row_offsets, col_offsets, counts):
    size = lax.axis_size("tile")
    down = [((i + 1) % size, i) for i in range(size)]
    own = flat(object_slices)
    low, high = halved(own)
    scalars = jnp.concatenate([row_offsets, col_offsets, counts])

    low, high, mine = lax.optimization_barrier((low, high, flat(probe_field)))
    low = lax.ppermute(low, "tile", down)
    quarter = jnp.concatenate([mine, partner(mine, 8), partner(mine, 4), partner(mine, 12)], axis=0)
    mats = built_matrices(patterns.shape[1])
    low, high, quarter, patterns, own, *mats = lax.optimization_barrier((low, high, quarter, patterns, own, *mats))
    near = jnp.concatenate([quarter, partner(quarter, 2)], axis=0)
    high = lax.ppermute(high, "tile", down)
    planes, patterns = prepared(own, patterns)
    near, planes, patterns, scalars = lax.optimization_barrier((near, planes, patterns, scalars))
    far = partner(near, 1)

    own_grad, back, probe_grad = terms(scalars, planes, low, high, near, far, patterns, mats)

    back = lax.ppermute(back, "tile", [(i, (i + 1) % size) for i in range(size)])
    probe_sum = lax.cond(
        counts[0] > 0,
        lambda grad: probe_share(grad, near.shape),
        lambda grad: jnp.zeros((near.shape[0] // 8, near.shape[1]), jnp.float32),
        probe_grad)
    object_grad = own_grad + back
    return unflat(object_grad, object_slices.shape), unflat(probe_sum, probe_field.shape)


def solution(mesh):
    in_specs = (
        P(("groups", "tile"), None, None, None),
        P(("groups", "tile"), None, None, None),
        P(("groups", "tile"), None, None),
        P(("groups", "tile")),
        P(("groups", "tile")),
        P(("groups", "tile")),
    )
    out_specs = (P(("groups", "tile"), None, None, None), P(("groups", "tile"), None, None, None))
    return jax.shard_map(shards, mesh=mesh, in_specs=in_specs, out_specs=out_specs, check_vma=False)
```
